32 devices in a mesh: ctx: 32 (over z, y, x, core), exp: 1.
Axes of the slice: x: 2, y: 2, z: 4, core: 2. Of those that a mesh axis runs over, the one named last changes fastest.
Arguments:
- tokens: bfloat16 [4096, 2880], P('ctx', 'exp'), may hold values from -6 to 6
- route_ids: int32 [4096, 4], P('ctx'), may hold values from 0 to 31, all different within a row; in each aligned block of 128 rows (0 to 127, 128 to 255, ...) at most 20 rows name the same one
- combine: float32 [4096, 4], P('ctx'), may hold values from 0.05 to 0.6
- gain_attn: float32 [2880], replicated, may hold values from 0.25 to 1.75
- gain_moe: float32 [2880], replicated, may hold values from 0.25 to 1.75
- query_weight: bfloat16 [2880, 4096], P(None, ('exp', 'ctx'))
- key_weight: bfloat16 [2880, 512], P(None, ('exp', 'ctx')), may hold values from -0.109375 to 0.109375
- value_weight: bfloat16 [2880, 512], P(None, ('exp', 'ctx')), may hold values from -0.109375 to 0.109375
- attn_sinks: float32 [64], P('exp'), may hold values from 1 to 6
- out_weight: bfloat16 [4096, 2880], P('exp', 'ctx'), may hold values from -0.09375 to 0.09375
- gate_up_weight: bfloat16 [32, 2, 2880, 2880], P('ctx', None, None, 'exp'), may hold values from -0.109375 to 0.109375
- down_weight: bfloat16 [32, 2880, 2880], P('ctx', 'exp'), may hold values from -0.109375 to 0.109375
Outputs:
- layer_out: bfloat16 [4096, 2880], P('ctx', 'exp')
The draws below stay inside these ranges and needn't reach their ends.
Inputs may be any that keep to these rules, and one draw needn't show every extreme that they name: `route_ids`: in each aligned block of 128 rows (the tokens of one index of ctx) no expert is named by more than 20 rows, a bound that some block reaches.
All inputs are finite; a program needn't handle non-finite values.
Results may differ from the reference program's by a relative error of at most 0.02.
Values may be sent and summed in bfloat16 or wider, within the bound.
No kernel may reach another device: no remote copies, remote signals or barrier semaphores. Data moves between devices by JAX's collectives and lax.ppermute only.
A program may use at most 256 MiB of HBM per device.

```python
import math
import jax
import jax.numpy as jnp
import numpy as np
from jax import lax

D = 2880
HQ = 64
HK = 8
HD = 64
FF = 2880
TOP = 4
WINDOW = 128
TOK_DEV = 128
TOKENS = 4096
EXPERTS = 32
CAP = 20
N_CTX = 32
N_EXP = 1


def draw_query_weight(key, part):
    base = jax.random.truncated_normal(key, -6.0, 6.0, (D, HQ * HD), jnp.float32) * D ** (-0.5)
    return base.astype(jnp.bfloat16)


def levels(rng, shape, split, smallest, largest):
    def one(dim, blocks):
        steps = jax.random.uniform(jax.random.fold_in(jax.random.fold_in(rng, 6), dim), (blocks,), jnp.float32, smallest / len(split), largest / len(split))
        return jnp.repeat(jnp.exp(steps), shape[dim] // blocks).reshape((-1,) + (1,) * (len(shape) - dim - 1))

    level = one(*split[0])
    for cut in split[1:]:
        level = level * one(*cut)
    return level


def assign_block(rng, own, number, rows, amount, top, reach, slope):
    ranking = jax.random.permutation(rng, amount)
    crowded, common = load_shares(amount, rows * top, reach, slope, True), load_shares(amount, rows * top, reach, slope, False)
    places = jnp.arange(amount)

    def named(lengths, turn):
        used = int((lengths > 0).sum())
        fixed = max(1, used // 4)
        shifted = fixed + (places - fixed + turn * (used - fixed)) % max(1, amount - fixed)
        return jnp.zeros((amount,), jnp.int32).at[ranking[jnp.where(places < fixed, places, shifted)]].set(jnp.asarray(lengths, jnp.int32))

    lengths = jnp.where(number % 4 == 0, named(crowded, number // 4), named(common, number - number // 4 - 1))
    mixed = jax.random.permutation(jax.random.fold_in(own, 3), amount)
    donor, receiver = mixed[0:amount // 2 * 2:2], mixed[1:amount // 2 * 2:2]
    room = jnp.minimum(lengths[donor] - 1, reach - lengths[receiver]) // 2
    room = jnp.where((donor == ranking[0]) | (receiver == ranking[0]) | (lengths[receiver] == 0), 0, jnp.maximum(room, 0))
    shifted = jax.random.randint(jax.random.fold_in(own, 4), (amount // 2,), 0, 1 << 20) % (room + 1)
    lengths = lengths.at[donor].add(-shifted).at[receiver].add(shifted)
    items = jnp.searchsorted(jnp.cumsum(lengths), jnp.arange(rows * top), side="right").astype(jnp.int32)
    grid = items.reshape(top, rows).T
    grid = grid[jax.random.permutation(jax.random.fold_in(own, 1), rows)]
    turn = jax.random.randint(jax.random.fold_in(own, 2), (rows, 1), 0, top)
    return jnp.take_along_axis(grid, (jnp.arange(top)[None, :] + turn) % top, axis=1)


def load_shares(amount, total, bound, lean, full):
    loads = [(1 << 20) // math.isqrt(grade ** lean) + 1 for grade in range(1, amount + 1)]
    largest = bound if full else min(bound, max(-(-total // amount), total * loads[0] // sum(loads)))
    least = 1 if total - largest >= amount - 1 else 0
    holding, rest = [largest] + [least] * (amount - 1), total - largest - least * (amount - 1)
    while rest > 0:
        movable = [i for i in range(1, amount) if holding[i] < largest] or [i for i in range(1, amount) if holding[i] < bound]
        pool, budget = sum([loads[i] for i in movable]), rest
        for i in movable:
            addition = min(bound - holding[i], max(1, budget * loads[i] // pool), rest)
            holding[i] = holding[i] + addition
            rest = rest - addition
    return np.array(holding)


def noise(stream_key, dims, spread, most, split=(), kind=jnp.bfloat16):
    level = levels(stream_key, dims, split, -0.22, 0.18) if split else 1.0
    values = jax.random.normal(stream_key, dims, jnp.float32) * spread * level
    return jnp.minimum(jnp.maximum(values, -most), most).astype(kind)


def setup_inputs(seed: int = 0) -> dict:
    key_list = jax.random.split(jax.random.key(seed), 13)
    tokens = noise(key_list[0], (TOKENS, D), 1.0, 6.0, ((0, 32),))
    route_ids_keys = jax.random.split(jax.random.fold_in(key_list[1], 1), TOKENS // TOK_DEV)
    route_ids_turns = jax.random.permutation(jax.random.fold_in(key_list[1], 3), TOKENS // TOK_DEV)
    route_ids = jax.vmap(lambda own, number: assign_block(jax.random.fold_in(key_list[1], 2), own, number, TOK_DEV, EXPERTS, TOP, CAP, 2))(route_ids_keys, route_ids_turns).reshape((TOKENS, TOP))
    combine = jnp.clip(0.05 + 0.55 * jax.random.uniform(key_list[2], (TOKENS, TOP), jnp.float32) ** levels(key_list[2], (TOKENS, TOP), ((0, 32),), -0.2, 0.2), 0.05, 0.6)
    gain_attn = jnp.clip(1.0 + 0.15 * jax.random.normal(key_list[3], (D,), jnp.float32), 0.25, 1.75)
    gain_moe = jnp.clip(1.0 + 0.15 * jax.random.normal(key_list[4], (D,), jnp.float32), 0.25, 1.75)
    query_weight = draw_query_weight(jax.random.fold_in(key_list[12], 71), 0)
    key_weight = noise(key_list[6], (D, HK * HD), D ** -0.5, 0.109375, ((1, 32),))
    value_weight = noise(key_list[7], (D, HK * HD), D ** -0.5, 0.109375, ((1, 32),))
    attn_sinks = jnp.clip(jax.random.uniform(key_list[8], (HQ,), jnp.float32, 1.0, 6.0), 1.0, 6.0)
    out_weight = noise(key_list[9], (HQ * HD, D), (HQ * HD) ** -0.5, 0.09375, ((1, 32),))
    gate_up_weight = noise(key_list[10], (EXPERTS, 2, D, FF), D ** -0.5, 0.109375, ((0, 32),))
    down_weight = noise(key_list[11], (EXPERTS, FF, D), FF ** -0.5, 0.109375, ((0, 32),))
    return dict(tokens=tokens, route_ids=route_ids, combine=combine, gain_attn=gain_attn, gain_moe=gain_moe, query_weight=query_weight, key_weight=key_weight, value_weight=value_weight, attn_sinks=attn_sinks, out_weight=out_weight, gate_up_weight=gate_up_weight, down_weight=down_weight)


EPSILON = 1e-05
ROPE_BASE = 150000.0

def rms_norm(values, gain):
    wide = values.astype(jnp.float32)
    meansq = lax.optimization_barrier(jnp.mean(wide * wide, axis=-1, keepdims=True))
    return (wide * lax.rsqrt(meansq + EPSILON) * gain).astype(jnp.bfloat16)

def rotary(values, angles_pos):
    half_dim = values.shape[-1] // 2
    inverse_freq = jnp.exp(-(2.0 * jnp.arange(half_dim, dtype=jnp.float32) / values.shape[-1]) * math.log(ROPE_BASE))
    angles = angles_pos[:, None] * inverse_freq[None, :]
    cosine = jnp.cos(angles)[:, None, :]
    sine_part = jnp.sin(angles)[:, None, :]
    first_half = values[..., :half_dim]
    second_half = values[..., half_dim:]
    return jnp.concatenate([first_half * cosine - second_half * sine_part, second_half * cosine + first_half * sine_part], axis=-1)

def sink_softmax(scores, key_mask, sink_col):
    masked = jnp.where(key_mask, scores, -1e+30)
    row_top = jnp.maximum(lax.optimization_barrier(jnp.max(masked, axis=-1, keepdims=True)), sink_col)
    weights = jnp.where(key_mask, jnp.exp(masked - row_top), 0.0)
    denominator = lax.optimization_barrier(jnp.sum(weights, axis=-1, keepdims=True)) + jnp.exp(sink_col - row_top)
    return (weights / denominator).astype(jnp.bfloat16)

def reference(tokens, route_ids, combine, gain_attn, gain_moe, query_weight, key_weight, value_weight, attn_sinks, out_weight, gate_up_weight, down_weight):
    normed_attn = rms_norm(tokens, gain_attn)
    angles_pos = jnp.arange(TOKENS, dtype=jnp.int32).astype(jnp.float32)
    query_lin = jnp.dot(normed_attn, query_weight, preferred_element_type=jnp.float32)
    key_lin = jnp.dot(normed_attn, key_weight, preferred_element_type=jnp.float32)
    value_lin = jnp.dot(normed_attn, value_weight, preferred_element_type=jnp.float32)
    query = rotary(query_lin.reshape(TOKENS, HQ, HD), angles_pos).astype(jnp.bfloat16)
    keys = rotary(key_lin.reshape(TOKENS, HK, HD), angles_pos).astype(jnp.bfloat16)
    values_all = value_lin.astype(jnp.bfloat16).reshape(TOKENS, HK, HD)
    group_size = HQ // HK
    key_pad = jnp.concatenate([jnp.zeros((WINDOW, HK, HD), jnp.bfloat16), keys], axis=0)
    value_pad = jnp.concatenate([jnp.zeros((WINDOW, HK, HD), jnp.bfloat16), values_all], axis=0)
    sink_col = attn_sinks.reshape(HK, group_size, 1, 1)

    def one_block(block):
        offset = block * TOK_DEV
        query_rows = lax.dynamic_slice_in_dim(query, offset, TOK_DEV, 0).reshape(TOK_DEV, HK, group_size, HD).astype(jnp.float32)
        key_rows = lax.dynamic_slice_in_dim(key_pad, offset, TOK_DEV + WINDOW, 0).astype(jnp.float32)
        value_rows = lax.dynamic_slice_in_dim(value_pad, offset, TOK_DEV + WINDOW, 0).astype(jnp.float32)
        scores = jnp.einsum('qkgd,skd->kgqs', query_rows, key_rows) * HD ** (-0.5)
        query_pos = offset + jnp.arange(TOK_DEV, dtype=jnp.int32)
        key_pos = offset - WINDOW + jnp.arange(TOK_DEV + WINDOW, dtype=jnp.int32)
        distance = query_pos[:, None] - key_pos[None, :]
        key_mask = (distance >= 0) & (distance < WINDOW) & (key_pos >= 0)[None, :]
        weights = sink_softmax(scores, key_mask, sink_col)
        mixed_rows = jnp.einsum('kgqs,skd->qkgd', weights.astype(jnp.float32), value_rows)
        return mixed_rows.astype(jnp.bfloat16).reshape(TOK_DEV, HQ * HD)
    attended = lax.map(one_block, jnp.arange(N_CTX, dtype=jnp.int32)).reshape(TOKENS, HQ * HD)
    attn_proj = jnp.dot(attended, out_weight, preferred_element_type=jnp.float32)
    residual = (tokens.astype(jnp.float32) + attn_proj).astype(jnp.bfloat16)
    normed_moe = rms_norm(residual, gain_moe)
    block_ids = route_ids.reshape(N_CTX, TOK_DEV * TOP)
    onehot = (block_ids[..., None] == jnp.arange(EXPERTS, dtype=jnp.int32)[None, None, :]).astype(jnp.int32)
    earlier = jnp.cumsum(onehot, axis=1).astype(jnp.int32) - onehot
    slot_index = lax.optimization_barrier(jnp.sum(earlier * onehot, axis=-1)).astype(jnp.int32)
    dest_row = (jnp.arange(N_CTX, dtype=jnp.int32)[:, None] * CAP + slot_index).astype(jnp.int32)
    token_of = (jnp.arange(N_CTX, dtype=jnp.int32)[:, None] * TOK_DEV + jnp.arange(TOK_DEV * TOP, dtype=jnp.int32)[None, :] // TOP).astype(jnp.int32)
    source_table = jnp.full((EXPERTS, N_CTX * CAP), TOKENS, jnp.int32).at[block_ids, dest_row].set(token_of)
    padded = jnp.concatenate([normed_moe, jnp.zeros((1, D), jnp.bfloat16)], axis=0)
    group_width = FF // N_EXP

    def one_expert(expert):
        flat_rows = padded[source_table[expert]]
        gate_part = jnp.dot(flat_rows, gate_up_weight[expert, 0], preferred_element_type=jnp.float32)
        upper_part = jnp.dot(flat_rows, gate_up_weight[expert, 1], preferred_element_type=jnp.float32)
        activation = (gate_part * jax.nn.sigmoid(1.702 * gate_part) * (upper_part + 1.0)).astype(jnp.bfloat16)
        partial_sums = jnp.einsum('rgf,gfd->grd', activation.reshape(-1, N_EXP, group_width).astype(jnp.float32), down_weight[expert].reshape(N_EXP, group_width, D).astype(jnp.float32))
        rounded = lax.optimization_barrier(partial_sums.astype(jnp.bfloat16)).astype(jnp.float32)
        return lax.optimization_barrier(jnp.sum(rounded, axis=0)).astype(jnp.bfloat16)
    expert_out = lax.map(one_expert, jnp.arange(EXPERTS, dtype=jnp.int32))
    picked = expert_out[block_ids, dest_row].astype(jnp.float32) * combine.reshape(N_CTX, TOK_DEV * TOP)[..., None]
    moe_out = lax.optimization_barrier(jnp.sum(picked.reshape(TOKENS, TOP, D), axis=1))
    return (residual.astype(jnp.float32) + moe_out).astype(jnp.bfloat16)
```

```python
import math

import jax
import jax.numpy as jnp
from jax import lax
from jax.sharding import PartitionSpec as P

HD = 64
WINDOW = 128
EPSILON = 1e-05
ROPE_BASE = 150000.0
PLANE = 8
BF16 = jnp.bfloat16
F32 = jnp.float32


def rms_norm(values, gain):
    wide = values.astype(F32)
    meansq = jnp.mean(wide * wide, axis=-1, keepdims=True)
    return (wide * lax.rsqrt(meansq + EPSILON) * gain).astype(BF16)


def rotary(values, angles_pos):
    half_dim = values.shape[-1] // 2
    inverse_freq = jnp.exp(
        -(2.0 * jnp.arange(half_dim, dtype=F32) / values.shape[-1]) * math.log(ROPE_BASE)
    )
    angles = angles_pos[:, None] * inverse_freq[None, :]
    cosine = jnp.cos(angles)[:, None, :]
    sine_part = jnp.sin(angles)[:, None, :]
    first_half = values[..., :half_dim]
    second_half = values[..., half_dim:]
    return jnp.concatenate(
        [
            first_half * cosine - second_half * sine_part,
            second_half * cosine + first_half * sine_part,
        ],
        axis=-1,
    )


def sink_softmax(scores, key_mask, sink_col):
    masked = jnp.where(key_mask, scores, -1e30)
    row_top = jnp.maximum(jnp.max(masked, axis=-1, keepdims=True), sink_col)
    weights = jnp.where(key_mask, jnp.exp(masked - row_top), 0.0)
    denominator = jnp.sum(weights, axis=-1, keepdims=True) + jnp.exp(sink_col - row_top)
    return (weights / denominator).astype(BF16)


def attend_block(query_rows, key_rows, value_rows, query_pos, key_pos, sink_col):
    scores = jnp.einsum(
        "qkgd,skd->kgqs", query_rows, key_rows, preferred_element_type=F32
    ) * HD ** (-0.5)
    distance = query_pos[:, None] - key_pos[None, :]
    key_mask = (distance >= 0) & (distance < WINDOW) & (key_pos >= 0)[None, :]
    weights = sink_softmax(scores, key_mask, sink_col)
    mixed_rows = jnp.einsum("kgqs,skd->qkgd", weights, value_rows, preferred_element_type=F32)
    return mixed_rows.astype(BF16).reshape(query_rows.shape[0], -1)


def dot32(a, b):
    return jnp.dot(a, b, preferred_element_type=F32)


def project_whole(tokens, gain_attn, query_weight, key_weight, value_weight, attn_sinks, out_weight):
    tok_dev = tokens.shape[0]
    full_rows = lax.all_gather(tokens, "exp", axis=1, tiled=True)
    normed = rms_norm(full_rows, gain_attn)
    pieces = lax.all_gather((query_weight, key_weight, value_weight), "ctx", axis=1, tiled=True)
    query_lin, key_lin, value_lin = tuple(dot32(normed, piece) for piece in pieces)
    heads_local = query_lin.shape[1] // HD
    kv_local = key_lin.shape[1] // HD
    group_size = heads_local // kv_local
    position_ids = lax.axis_index("ctx") * tok_dev + jnp.arange(tok_dev, dtype=jnp.int32)
    angles_pos = position_ids.astype(F32)
    query = rotary(query_lin.reshape(tok_dev, heads_local, HD), angles_pos).astype(BF16)
    keys_own = rotary(key_lin.reshape(tok_dev, kv_local, HD), angles_pos).astype(BF16)
    key_value = jnp.stack([keys_own.reshape(tok_dev, kv_local * HD), value_lin.astype(BF16)])
    n_ctx = lax.axis_size("ctx")
    previous = lax.ppermute(key_value, "ctx", [(i, i + 1) for i in range(n_ctx - 1)])
    context = jnp.concatenate([previous, key_value], axis=1)
    key_pos = position_ids[0] - WINDOW + jnp.arange(tok_dev + WINDOW, dtype=jnp.int32)
    attended = attend_block(
        query.reshape(tok_dev, kv_local, group_size, HD),
        context[0].reshape(-1, kv_local, HD),
        context[1].reshape(-1, kv_local, HD),
        position_ids,
        key_pos,
        attn_sinks.reshape(kv_local, group_size, 1, 1),
    )
    head_terms = dot32(attended, lax.all_gather(out_weight, "ctx", axis=1, tiled=True))
    attn_proj = lax.psum(head_terms.astype(BF16), "exp").astype(F32)
    return (full_rows.astype(F32) + attn_proj).astype(BF16)


def project_planes(tokens, gain_attn, query_weight, key_weight, value_weight, attn_sinks, out_weight):
    tok_dev, width = tokens.shape
    n_ctx = lax.axis_size("ctx")
    n_z = n_ctx // PLANE
    index = lax.axis_index("ctx")
    z, j = index // PLANE, index % PLANE
    planes = [[PLANE * a + b for b in range(PLANE)] for a in range(n_z)]
    same_core = [[2 * a + b for a in range(n_ctx // 2)] for b in range(2)]

    def shift(block, steps):
        return lax.ppermute(block, "ctx", [(i, (i + steps * PLANE) % n_ctx) for i in range(n_ctx)])

    def behind(block):
        route = [(a * PLANE + b, a * PLANE + (b + 1) % PLANE) for a in range(n_z) for b in range(PLANE)]
        return lax.ppermute(block, "ctx", route)

    def sibling(block):
        return lax.ppermute(block, "ctx", [(i, i ^ 1) for i in range(n_ctx)])

    blocks = [rms_norm(tokens, gain_attn)]
    for _ in range(n_z - 1):
        blocks.append(shift(blocks[-1], 1))

    key_value_weight = jnp.concatenate([key_weight.T, value_weight.T], axis=0)
    kv_cols = key_weight.shape[1]
    kv_all = lax.all_gather(key_value_weight, "ctx", axis_index_groups=planes)
    key_matrix = kv_all[:, :kv_cols].reshape(PLANE * kv_cols, width)
    value_matrix = kv_all[:, kv_cols:].reshape(PLANE * kv_cols, width)
    query_matrix = lax.all_gather(query_weight, "ctx", axis=1, tiled=True, axis_index_groups=planes)

    heads = query_matrix.shape[1] // HD
    kv_heads = key_matrix.shape[0] // HD
    group_size = heads // kv_heads
    sink_col = lax.dynamic_slice_in_dim(attn_sinks, z * heads, heads).reshape(kv_heads, group_size, 1, 1)

    own_rows = jnp.arange(tok_dev, dtype=jnp.int32)
    queries, key_values, halos, positions = [], [], [], []
    for r in range(n_z):
        block = blocks[r]
        start = (((z - r) % n_z) * PLANE + j) * tok_dev
        position_ids = start + own_rows
        angles_pos = position_ids.astype(F32)
        query = rotary(dot32(block, query_matrix).reshape(tok_dev, heads, HD), angles_pos)
        key_lin = lax.dot_general(block, key_matrix, (((1,), (1,)), ((), ())), preferred_element_type=F32)
        value_lin = lax.dot_general(block, value_matrix, (((1,), (1,)), ((), ())), preferred_element_type=F32)
        keys = rotary(key_lin.reshape(tok_dev, kv_heads, HD), angles_pos).astype(BF16)
        key_value = jnp.stack([keys.reshape(tok_dev, kv_heads * HD), value_lin.astype(BF16)])
        queries.append(query.astype(BF16).reshape(tok_dev, kv_heads, group_size, HD))
        key_values.append(key_value)
        halos.append(behind(key_value))
        positions.append(position_ids)

    parts = []
    for r in range(n_z):
        previous = jnp.where(j == 0, halos[(r + 1) % n_z], halos[r])
        context = jnp.concatenate([previous, key_values[r]], axis=1)
        key_pos = positions[r][0] - WINDOW + jnp.arange(tok_dev + WINDOW, dtype=jnp.int32)
        attended = attend_block(
            queries[r],
            context[0].reshape(-1, kv_heads, HD),
            context[1].reshape(-1, kv_heads, HD),
            positions[r],
            key_pos,
            sink_col,
        )
        parts.append(shift(attended, -r) if r else attended)

    plane_cols = heads * HD
    twice = jnp.concatenate(parts + parts[:-1], axis=1)
    attended = lax.dynamic_slice_in_dim(
        twice, ((n_z - z) % n_z) * plane_cols, n_z * plane_cols, axis=1
    )

    cols = out_weight.shape[1]
    padded_cols = -(-cols // 16) * 16
    out_rows = jnp.pad(out_weight.T, ((0, padded_cols - cols), (0, 0)))
    out_half = lax.all_gather(out_rows, "ctx", axis_index_groups=same_core, tiled=True)
    both = jnp.concatenate([attended, sibling(attended)], axis=0)
    terms = lax.dot_general(both, out_half, (((1,), (1,)), ((), ())), preferred_element_type=F32)
    terms = terms.astype(BF16).reshape(2, tok_dev, n_ctx // 2, padded_cols)[..., :cols]
    own_cols, other_cols = terms[0], sibling(terms[1])
    odd = index % 2 == 1
    attn_proj = jnp.stack(
        [jnp.where(odd, other_cols, own_cols), jnp.where(odd, own_cols, other_cols)], axis=2
    ).reshape(tok_dev, width)
    return (tokens.astype(F32) + attn_proj.astype(F32)).astype(BF16)


def slot_chunks(capacity):
    sizes = []
    while capacity:
        size = min(8, capacity)
        sizes.append(size)
        capacity -= size
    return sizes


def per_device(
    tokens,
    route_ids,
    combine,
    gain_attn,
    gain_moe,
    query_weight,
    key_weight,
    value_weight,
    attn_sinks,
    out_weight,
    gate_up_weight,
    down_weight,
):
    tok_dev, width_local = tokens.shape
    n_ctx = lax.axis_size("ctx")
    n_exp = lax.axis_size("exp")
    project = project_planes if n_exp == 1 and n_ctx % PLANE == 0 else project_whole
    residual = project(
        tokens, gain_attn, query_weight, key_weight, value_weight, attn_sinks, out_weight
    )
    width = residual.shape[1]
    normed_moe = rms_norm(residual, gain_moe)
    exp_index = lax.axis_index("exp")
    residual_local = lax.dynamic_slice_in_dim(residual, exp_index * width_local, width_local, 1)

    top_count = route_ids.shape[1]
    capacity = tok_dev * top_count * 5 // (4 * n_ctx)
    named = route_ids[:, :, None] == jnp.arange(n_ctx, dtype=jnp.int32)[None, None, :]
    member = jnp.any(named, axis=1)
    weight_of = jnp.sum(jnp.where(named, combine[:, :, None], 0.0), axis=1)
    rows = jnp.arange(tok_dev, dtype=jnp.int32)
    earlier = (rows[:, None] > rows[None, :]).astype(BF16)
    slot_of = dot32(earlier, member.astype(BF16)).astype(jnp.int32)
    slot_of = jnp.where(member, slot_of, -1)

    gate_matrix = gate_up_weight[0, 0]
    upper_matrix = gate_up_weight[0, 1]
    down_matrix = down_weight[0]

    def expert(flat_rows):
        gate_part = dot32(flat_rows, gate_matrix)
        upper_part = dot32(flat_rows, upper_matrix)
        activation = (gate_part * jax.nn.sigmoid(1.702 * gate_part) * (upper_part + 1.0)).astype(BF16)
        return dot32(activation, down_matrix).astype(BF16)

    def exchange(rows_of):
        return lax.all_to_all(rows_of, "ctx", split_axis=0, concat_axis=0, tiled=True)

    chunks, received = [], []
    first = 0
    for size in slot_chunks(capacity):
        slots = first + jnp.arange(size, dtype=jnp.int32)
        chosen = (slot_of[:, :, None] == slots[None, None, :]).reshape(tok_dev, n_ctx * size)
        outgoing = lax.dot_general(
            chosen.astype(BF16), normed_moe, (((0,), (0,)), ((), ())), preferred_element_type=F32
        ).astype(BF16)
        received.append(exchange(outgoing.reshape(n_ctx, size, width)).reshape(n_ctx * size, width))
        scale = jnp.where(chosen, jnp.repeat(weight_of, size, axis=1), 0.0)
        high = scale.astype(BF16)
        low = (scale - high.astype(F32)).astype(BF16)
        chunks.append((size, jnp.concatenate([high, low], axis=0)))
        first += size

    results = [expert(received[0])]
    if len(received) > 1:
        rest = expert(jnp.concatenate(received[1:], axis=0))
        first = 0
        for size, _ in chunks[1:]:
            results.append(rest[first : first + n_ctx * size])
            first += n_ctx * size

    moe_out = jnp.zeros((tok_dev, width_local), F32)
    for (size, scale), result in zip(chunks, results):
        answer = exchange(result.reshape(n_ctx, size, width))
        if n_exp > 1:
            answer = lax.psum_scatter(answer, "exp", scatter_dimension=2, tiled=True)
        terms = dot32(scale, answer.reshape(n_ctx * size, width_local))
        moe_out = moe_out + terms[:tok_dev] + terms[tok_dev:]
    return (residual_local.astype(F32) + moe_out).astype(BF16)


def solution(mesh):
    return jax.shard_map(
        per_device,
        mesh=mesh,
        in_specs=(
            P("ctx", "exp"),
            P("ctx", None),
            P("ctx", None),
            P(),
            P(),
            P(None, ("exp", "ctx")),
            P(None, ("exp", "ctx")),
            P(None, ("exp", "ctx")),
            P("exp"),
            P("exp", "ctx"),
            P("ctx", None, None, "exp"),
            P("ctx", "exp", None),
        ),
        out_specs=P("ctx", "exp"),
        check_vma=False,
    )
```

```python
import functools
import math

import jax
import jax.numpy as jnp
from jax import lax
from jax.experimental import pallas as pl
from jax.experimental.pallas import tpu as pltpu
from jax.sharding import PartitionSpec as P

HD = 64
WINDOW = 128
EPSILON = 1e-05
ROPE_BASE = 150000.0
PLANE = 8
BF16 = jnp.bfloat16
F32 = jnp.float32


def rms_norm(values, gain):
    wide = values.astype(F32)
    meansq = jnp.mean(wide * wide, axis=-1, keepdims=True)
    return (wide * lax.rsqrt(meansq + EPSILON) * gain).astype(BF16)


def rotary(values, angles_pos):
    half_dim = values.shape[-1] // 2
    inverse_freq = jnp.exp(
        -(2.0 * jnp.arange(half_dim, dtype=F32) / values.shape[-1]) * math.log(ROPE_BASE)
    )
    angles = angles_pos[:, None] * inverse_freq[None, :]
    cosine = jnp.cos(angles)[:, None, :]
    sine_part = jnp.sin(angles)[:, None, :]
    first_half = values[..., :half_dim]
    second_half = values[..., half_dim:]
    return jnp.concatenate(
        [
            first_half * cosine - second_half * sine_part,
            second_half * cosine + first_half * sine_part,
        ],
        axis=-1,
    )


def sink_softmax(scores, key_mask, sink_col):
    masked = jnp.where(key_mask, scores, -1e30)
    row_top = jnp.maximum(jnp.max(masked, axis=-1, keepdims=True), sink_col)
    weights = jnp.where(key_mask, jnp.exp(masked - row_top), 0.0)
    denominator = jnp.sum(weights, axis=-1, keepdims=True) + jnp.exp(sink_col - row_top)
    return (weights / denominator).astype(BF16)


def attend_block(query_rows, key_rows, value_rows, query_pos, key_pos, sink_col):
    scores = jnp.einsum(
        "qkgd,skd->kgqs", query_rows, key_rows, preferred_element_type=F32
    ) * HD ** (-0.5)
    distance = query_pos[:, None] - key_pos[None, :]
    key_mask = (distance >= 0) & (distance < WINDOW) & (key_pos >= 0)[None, :]
    weights = sink_softmax(scores, key_mask, sink_col)
    mixed_rows = jnp.einsum("kgqs,skd->qkgd", weights, value_rows, preferred_element_type=F32)
    return mixed_rows.astype(BF16).reshape(query_rows.shape[0], -1)


def dot32(a, b):
    return jnp.dot(a, b, preferred_element_type=F32)


def project_whole(tokens, gain_attn, query_weight, key_weight, value_weight, attn_sinks, out_weight):
    tok_dev = tokens.shape[0]
    full_rows = lax.all_gather(tokens, "exp", axis=1, tiled=True)
    normed = rms_norm(full_rows, gain_attn)
    pieces = lax.all_gather((query_weight, key_weight, value_weight), "ctx", axis=1, tiled=True)
    query_lin, key_lin, value_lin = tuple(dot32(normed, piece) for piece in pieces)
    heads_local = query_lin.shape[1] // HD
    kv_local = key_lin.shape[1] // HD
    group_size = heads_local // kv_local
    position_ids = lax.axis_index("ctx") * tok_dev + jnp.arange(tok_dev, dtype=jnp.int32)
    angles_pos = position_ids.astype(F32)
    query = rotary(query_lin.reshape(tok_dev, heads_local, HD), angles_pos).astype(BF16)
    keys_own = rotary(key_lin.reshape(tok_dev, kv_local, HD), angles_pos).astype(BF16)
    key_value = jnp.stack([keys_own.reshape(tok_dev, kv_local * HD), value_lin.astype(BF16)])
    n_ctx = lax.axis_size("ctx")
    previous = lax.ppermute(key_value, "ctx", [(i, i + 1) for i in range(n_ctx - 1)])
    context = jnp.concatenate([previous, key_value], axis=1)
    key_pos = position_ids[0] - WINDOW + jnp.arange(tok_dev + WINDOW, dtype=jnp.int32)
    attended = attend_block(
        query.reshape(tok_dev, kv_local, group_size, HD),
        context[0].reshape(-1, kv_local, HD),
        context[1].reshape(-1, kv_local, HD),
        position_ids,
        key_pos,
        attn_sinks.reshape(kv_local, group_size, 1, 1),
    )
    head_terms = dot32(attended, lax.all_gather(out_weight, "ctx", axis=1, tiled=True))
    attn_proj = lax.psum(head_terms.astype(BF16), "exp").astype(F32)
    return (full_rows.astype(F32) + attn_proj).astype(BF16).T


def dot_nt(a, b):
    return lax.dot_general(a, b, (((1,), (1,)), ((), ())), preferred_element_type=F32)


def turn(values, cosine, signed_sine):
    width = values.shape[1]
    half = HD // 2
    lane = lax.broadcasted_iota(jnp.int32, values.shape, 1) % HD
    partner = jnp.where(
        lane < half,
        pltpu.roll(values, width - half, 1),
        pltpu.roll(values, half, 1),
    )
    return values * cosine + partner * signed_sine


def qkv_kernel(place_ref, block_ref, query_ref, kv_ref, cos_ref, sin_ref, q_ref, key_value_ref):
    step = pl.program_id(0)
    block = block_ref[...]
    cosine, signed_sine = cos_ref[...], sin_ref[...]
    q_ref[...] = turn(dot32(block, query_ref[0]), cosine, signed_sine).astype(BF16)

    @pl.when(step == 0)
    def _():
        cols = kv_ref.shape[1] // 2
        shares = [kv_ref[place_ref[p]] for p in range(PLANE)]
        key_rows = jnp.concatenate([share[:cols] for share in shares], axis=0)
        value_rows = jnp.concatenate([share[cols:] for share in shares], axis=0)
        width = PLANE * cols
        key_value_ref[:, :width] = turn(dot_nt(block, key_rows), cosine, signed_sine).astype(BF16)
        key_value_ref[:, width:] = dot_nt(block, value_rows).astype(BF16)


def project_block(place, block, query_all, kv_all, cosine, signed_sine):
    rows, width = block.shape
    cols = query_all.shape[2]
    kv_cols = kv_all.shape[1] * PLANE
    whole = lambda p, place: (0, 0)
    return pl.pallas_call(
        qkv_kernel,
        grid_spec=pltpu.PrefetchScalarGridSpec(
            num_scalar_prefetch=1,
            grid=(PLANE,),
            in_specs=[
                pl.BlockSpec((rows, width), whole),
                pl.BlockSpec((1, width, cols), lambda p, place: (place[p], 0, 0)),
                pl.BlockSpec(kv_all.shape, lambda p, place: (0, 0, 0)),
                pl.BlockSpec(cosine.shape, whole),
                pl.BlockSpec(signed_sine.shape, whole),
            ],
            out_specs=[
                pl.BlockSpec((rows, cols), lambda p, place: (0, p)),
                pl.BlockSpec((rows, kv_cols), whole),
            ],
        ),
        out_shape=[
            jax.ShapeDtypeStruct((rows, PLANE * cols), BF16),
            jax.ShapeDtypeStruct((rows, kv_cols), BF16),
        ],
        compiler_params=pltpu.CompilerParams(vmem_limit_bytes=32 * 2**20),
        cost_estimate=pl.CostEstimate(
            flops=2 * rows * width * (PLANE * cols + kv_cols),
            bytes_accessed=2 * width * (PLANE * cols + kv_cols + rows),
            transcendentals=0,
        ),
    )(place, block, query_all, kv_all, cosine, signed_sine)


def attend_kernel(n_add, first_ref, sinks_ref, q_ref, own_ref, previous_ref, weight_ref, *refs):
    addends, out_ref, att_ref, total_ref = refs[:n_add], refs[n_add], refs[n_add + 1], refs[n_add + 2]
    rows = q_ref.shape[0]
    pair = 2 * HD
    kv_heads = own_ref.shape[1] // pair
    kv_cols = kv_heads * HD
    pairs = q_ref.shape[1] // pair
    lane = lax.broadcasted_iota(jnp.int32, (rows, pair), 1)
    low = lane < HD

    def spread(values, head):
        moved = pltpu.roll(values.astype(F32), HD, 1)
        chunk = values.astype(F32)
        lower, upper = (chunk, moved) if head % 2 == 0 else (moved, chunk)
        zero = jnp.zeros_like(chunk)
        return jnp.concatenate(
            [jnp.where(low, lower, zero), jnp.where(low, zero, upper)], axis=0
        ).astype(BF16)

    def side(ref):
        tables = []
        for head in range(kv_heads):
            at = head // 2 * pair
            keys = spread(ref[:, at : at + pair], head)
            values = spread(ref[:, kv_cols + at : kv_cols + at + pair], head)
            tables.append((keys, values))
        return tables

    own, previous = side(own_ref), side(previous_ref)
    row = lax.broadcasted_iota(jnp.int32, (rows, rows), 0)
    col = lax.broadcasted_iota(jnp.int32, (rows, rows), 1)
    inside = col <= row
    shown = jnp.logical_or(inside, first_ref[0] == 0)
    scale = HD**-0.5
    for p in range(pairs):
        head = p * kv_heads // pairs
        chunk = q_ref[:, p * pair : (p + 1) * pair]
        scores_own = dot_nt(chunk, own[head][0])
        scores_previous = dot_nt(chunk, previous[head][0])
        probs_own, probs_previous = [], []
        for h in range(2):
            at = h * rows
            scores = jnp.where(
                inside, scores_own[:, at : at + rows], scores_previous[:, at : at + rows]
            ) * scale
            scores = jnp.where(shown, scores, -1e30)
            sink = sinks_ref[2 * p + h]
            top = jnp.maximum(jnp.max(scores, axis=1, keepdims=True), sink)
            weights = jnp.exp(scores - top)
            total = jnp.sum(weights, axis=1, keepdims=True) + jnp.exp(sink - top)
            probs = weights / total
            probs_own.append(jnp.where(inside, probs, 0.0).astype(BF16))
            probs_previous.append(jnp.where(inside, 0.0, probs).astype(BF16))
        mixed = dot32(jnp.concatenate(probs_own, axis=1), own[head][1])
        mixed = mixed + dot32(jnp.concatenate(probs_previous, axis=1), previous[head][1])
        att_ref[:, p * pair : (p + 1) * pair] = mixed.astype(BF16)

    shares, groups, padded, depth = weight_ref.shape
    cols = out_ref.shape[0] // (shares * groups)
    attended = att_ref[...]
    for p in range(shares):
        terms = dot_nt(weight_ref[p].reshape(groups * padded, depth), attended)
        for g in range(groups):
            at = (g * shares + p) * cols
            total_ref[at : at + cols, :] = terms[g * padded : g * padded + cols]
    total = total_ref[...]
    for ref in addends:
        total = total + ref[...].astype(F32)
    out_ref[...] = total.astype(BF16)


def attend_and_project(rows, shape, first, sinks, query, own, previous, weight, addends, width):
    shares, groups, padded, depth = shape
    vmem = pl.BlockSpec(memory_space=pltpu.VMEM)
    smem = pl.BlockSpec(memory_space=pltpu.SMEM)
    return pl.pallas_call(
        functools.partial(attend_kernel, len(addends)),
        in_specs=[smem, smem] + [vmem] * (4 + len(addends)),
        out_specs=vmem,
        out_shape=jax.ShapeDtypeStruct((width, rows), BF16),
        scratch_shapes=[pltpu.VMEM((rows, depth), BF16), pltpu.VMEM((width, rows), F32)],
        compiler_params=pltpu.CompilerParams(vmem_limit_bytes=40 * 2**20),
        cost_estimate=pl.CostEstimate(
            flops=2 * rows * depth * (width + 8 * rows),
            bytes_accessed=2 * (width * depth + 2 * width * rows),
            transcendentals=rows * rows * depth // HD,
        ),
    )(first, sinks, query, own, previous, weight, *addends)


def project_planes(tokens, gain_attn, query_weight, key_weight, value_weight, attn_sinks, out_weight):
    tok_dev, width = tokens.shape
    n_ctx = lax.axis_size("ctx")
    n_z = n_ctx // PLANE
    index = lax.axis_index("ctx")
    z, j = index // PLANE, index % PLANE
    planes = [[PLANE * a + b for b in range(PLANE)] for a in range(n_z)]

    def shift(block, steps):
        return lax.ppermute(block, "ctx", [(i, (i + steps * PLANE) % n_ctx) for i in range(n_ctx)])

    def behind(block):
        route = [(a * PLANE + b, a * PLANE + (b + 1) % PLANE) for a in range(n_z) for b in range(PLANE)]
        return lax.ppermute(block, "ctx", route)

    def swap(block, bits):
        return lax.ppermute(block, "ctx", [(i, i ^ bits) for i in range(n_ctx)])

    def plane_gather(block):
        half = jnp.stack([block] + [swap(block, bits) for bits in (2, 4, 6)])
        return jnp.concatenate([half, swap(half, 1)])

    blocks = [rms_norm(tokens, gain_attn)]
    for _ in range(n_z - 1):
        blocks.append(shift(blocks[-1], -1))

    kv_all = plane_gather(jnp.concatenate([key_weight.T, value_weight.T], axis=0))
    query_all = plane_gather(query_weight)
    relative = jnp.arange(PLANE, dtype=jnp.int32) ^ j
    place = (relative % 2) * (PLANE // 2) + relative // 2

    cols = out_weight.shape[1]
    padded = -(-cols // 16) * 16
    group_rows = out_weight.shape[0] // n_z
    out_rows = jnp.pad(out_weight.T, ((0, padded - cols), (0, 0)))
    out_groups = jnp.stack(jnp.split(out_rows, n_z, axis=1))
    pieces = [
        shift(lax.dynamic_index_in_dim(out_groups, (z + s) % n_z, 0, keepdims=False), s) if s
        else lax.dynamic_index_in_dim(out_groups, z, 0, keepdims=False)
        for s in range(n_z)
    ]
    ordered = jnp.stack(pieces[::-1] + pieces[:0:-1])
    out_mine = lax.dynamic_slice_in_dim(ordered, n_z - 1 - z, n_z, 0)
    out_all = lax.all_gather(out_mine, "ctx", axis_index_groups=planes)

    heads = PLANE * query_weight.shape[1] // HD
    sinks = lax.dynamic_slice_in_dim(attn_sinks, z * heads, heads)
    own_rows = jnp.arange(tok_dev, dtype=jnp.int32)
    lane = jnp.arange(2 * HD, dtype=jnp.int32) % HD
    half = HD // 2
    inverse_freq = jnp.exp(-(2.0 * (lane % half).astype(F32) / HD) * math.log(ROPE_BASE))
    queries, key_values, halos, numbers = [], [], [], []
    for r in range(n_z):
        number = ((z + r) % n_z) * PLANE + j
        angles = (number * tok_dev + own_rows).astype(F32)[:, None] * inverse_freq[None, :]
        signed_sine = jnp.where(lane[None, :] < half, -jnp.sin(angles), jnp.sin(angles))
        query, key_value = project_block(
            place, blocks[r], query_all, kv_all, jnp.cos(angles), signed_sine
        )
        queries.append(query)
        key_values.append(key_value)
        halos.append(behind(key_value))
        numbers.append(number)

    running = None
    for r in list(range(1, n_z)) + [0]:
        previous = jnp.where(j == 0, halos[(r - 1) % n_z], halos[r])
        first = (numbers[r] == 0).astype(jnp.int32).reshape(1)
        addends = [] if running is None else [running]
        if r == 0:
            addends.append(tokens.T)
        partial_sum = attend_and_project(
            tok_dev, out_all.shape, first, sinks, queries[r], key_values[r], previous, out_all, addends, width
        )
        running = shift(partial_sum, -1) if r else partial_sum
    return running


def expert_kernel(tile, hidden, rows_ref, gate_ref, upper_ref, down_ref, out_ref, total_ref):
    step = pl.program_id(0)
    steps = pl.num_programs(0)

    def add(count, initial):
        rows = rows_ref[...]
        gate = dot32(rows, gate_ref[0, :, :count])
        upper = dot32(rows, upper_ref[0, :, :count])
        activation = (gate * jax.nn.sigmoid(1.702 * gate) * (upper + 1.0)).astype(BF16)
        terms = dot32(activation, down_ref[:count, :])
        total_ref[...] = terms if initial else total_ref[...] + terms

    last = hidden - (-(-hidden // tile) - 1) * tile

    @pl.when(step == 0)
    def _():
        add(tile, True)

    @pl.when(jnp.logical_and(step > 0, step < steps - 1))
    def _():
        add(tile, False)

    @pl.when(step == steps - 1)
    def _():
        add(last, False)
        out_ref[...] = total_ref[...].astype(BF16)


def run_expert(rows, gate_up, down):
    count, width = rows.shape
    hidden = down.shape[0]
    tile = 512 if hidden > 1024 else 256
    return pl.pallas_call(
        functools.partial(expert_kernel, tile, hidden),
        grid=(-(-hidden // tile),),
        in_specs=[
            pl.BlockSpec((count, width), lambda f: (0, 0)),
            pl.BlockSpec((1, width, tile), lambda f: (0, 0, f)),
            pl.BlockSpec((1, width, tile), lambda f: (1, 0, f)),
            pl.BlockSpec((tile, width), lambda f: (f, 0)),
        ],
        out_specs=pl.BlockSpec((count, width), lambda f: (0, 0)),
        out_shape=jax.ShapeDtypeStruct((count, width), BF16),
        scratch_shapes=[pltpu.VMEM((count, width), F32)],
        compiler_params=pltpu.CompilerParams(vmem_limit_bytes=52 * 2**20),
        cost_estimate=pl.CostEstimate(
            flops=6 * count * width * hidden,
            bytes_accessed=6 * width * hidden + 4 * count * width,
            transcendentals=count * hidden,
        ),
    )(rows, gate_up, gate_up, down)


def slot_chunks(capacity):
    sizes = []
    while capacity:
        size = min(8, capacity)
        sizes.append(size)
        capacity -= size
    return sizes


def per_device(
    tokens,
    route_ids,
    combine,
    gain_attn,
    gain_moe,
    query_weight,
    key_weight,
    value_weight,
    attn_sinks,
    out_weight,
    gate_up_weight,
    down_weight,
):
    tok_dev, width_local = tokens.shape
    n_ctx = lax.axis_size("ctx")
    n_exp = lax.axis_size("exp")
    project = project_planes if n_exp == 1 and n_ctx % PLANE == 0 else project_whole
    residual = project(
        tokens, gain_attn, query_weight, key_weight, value_weight, attn_sinks, out_weight
    )
    width = residual.shape[0]
    wide = residual.astype(F32)
    meansq = jnp.mean(wide * wide, axis=0, keepdims=True)
    normed_moe = (wide * lax.rsqrt(meansq + EPSILON) * gain_moe[:, None]).astype(BF16)
    exp_index = lax.axis_index("exp")
    residual_local = lax.dynamic_slice_in_dim(residual, exp_index * width_local, width_local, 0)

    top_count = route_ids.shape[1]
    capacity = tok_dev * top_count * 5 // (4 * n_ctx)
    named = route_ids[:, :, None] == jnp.arange(n_ctx, dtype=jnp.int32)[None, None, :]
    member = jnp.any(named, axis=1)
    weight_of = jnp.sum(jnp.where(named, combine[:, :, None], 0.0), axis=1)
    rows = jnp.arange(tok_dev, dtype=jnp.int32)
    earlier = (rows[:, None] > rows[None, :]).astype(BF16)
    slot_of = dot32(earlier, member.astype(BF16)).astype(jnp.int32)
    slot_of = jnp.where(member, slot_of, -1)

    def exchange(rows_of):
        return lax.all_to_all(rows_of, "ctx", split_axis=0, concat_axis=0, tiled=True)

    sizes = slot_chunks(capacity)
    outgoing, scales = [], []
    first = 0
    for size in sizes:
        slots = first + jnp.arange(size, dtype=jnp.int32)
        chosen = (slot_of[:, :, None] == slots[None, None, :]).reshape(tok_dev, n_ctx * size)
        rows_out = lax.dot_general(
            chosen.astype(BF16), normed_moe, (((0,), (1,)), ((), ())), preferred_element_type=F32
        ).astype(BF16)
        outgoing.append(rows_out.reshape(n_ctx, size, width))
        scale = jnp.where(chosen, jnp.repeat(weight_of, size, axis=1), 0.0)
        high = scale.astype(BF16)
        low = (scale - high.astype(F32)).astype(BF16)
        scales.append(jnp.concatenate([high, low], axis=0))
        first += size

    received = []
    for size, rows_out in zip(sizes, outgoing):
        if received:
            rows_out, received[-1] = lax.optimization_barrier((rows_out, received[-1]))
        received.append(exchange(rows_out))
    received = [rows_in.reshape(-1, width) for rows_in in received]

    results = [run_expert(received[0], gate_up_weight[0], down_weight[0])]
    if len(received) > 1:
        rest = run_expert(jnp.concatenate(received[1:], axis=0), gate_up_weight[0], down_weight[0])
        first = 0
        for size in sizes[1:]:
            results.append(rest[first : first + n_ctx * size])
            first += n_ctx * size

    answers = []
    for size, result in zip(sizes, results):
        if answers:
            result, answers[-1] = lax.optimization_barrier((result, answers[-1]))
        else:
            result, received[-1] = lax.optimization_barrier((result, received[-1]))
        answers.append(exchange(result.reshape(n_ctx, size, width)))

    moe_out = jnp.zeros((width_local, tok_dev), F32)
    for size, scale, answer in zip(sizes, scales, answers):
        if n_exp > 1:
            answer = lax.psum_scatter(answer, "exp", scatter_dimension=2, tiled=True)
        terms = lax.dot_general(
            answer.reshape(n_ctx * size, width_local), scale, (((0,), (1,)), ((), ())),
            preferred_element_type=F32,
        )
        moe_out = moe_out + terms[:, :tok_dev] + terms[:, tok_dev:]
    return (residual_local.astype(F32) + moe_out).astype(BF16).T


def solution(mesh):
    return jax.shard_map(
        per_device,
        mesh=mesh,
        in_specs=(
            P("ctx", "exp"),
            P("ctx", None),
            P("ctx", None),
            P(),
            P(),
            P(None, ("exp", "ctx")),
            P(None, ("exp", "ctx")),
            P(None, ("exp", "ctx")),
            P("exp"),
            P("exp", "ctx"),
            P("ctx", None, None, "exp"),
            P("ctx", "exp", None),
        ),
        out_specs=P("ctx", "exp"),
        check_vma=False,
    )
```

```python
import functools
import math

import jax
import jax.numpy as jnp
from jax import lax
from jax.experimental import pallas as pl
from jax.experimental.pallas import tpu as pltpu
from jax.sharding import PartitionSpec as P

HD = 64
WINDOW = 128
EPSILON = 1e-05
ROPE_BASE = 150000.0
PLANE = 8
BF16 = jnp.bfloat16
F32 = jnp.float32


def rms_norm(values, gain):
    wide = values.astype(F32)
    meansq = jnp.mean(wide * wide, axis=-1, keepdims=True)
    return (wide * lax.rsqrt(meansq + EPSILON) * gain).astype(BF16)


def rotary(values, angles_pos):
    half_dim = values.shape[-1] // 2
    inverse_freq = jnp.exp(
        -(2.0 * jnp.arange(half_dim, dtype=F32) / values.shape[-1]) * math.log(ROPE_BASE)
    )
    angles = angles_pos[:, None] * inverse_freq[None, :]
    cosine = jnp.cos(angles)[:, None, :]
    sine_part = jnp.sin(angles)[:, None, :]
    first_half = values[..., :half_dim]
    second_half = values[..., half_dim:]
    return jnp.concatenate(
        [
            first_half * cosine - second_half * sine_part,
            second_half * cosine + first_half * sine_part,
        ],
        axis=-1,
    )


def sink_softmax(scores, key_mask, sink_col):
    masked = jnp.where(key_mask, scores, -1e30)
    row_top = jnp.maximum(jnp.max(masked, axis=-1, keepdims=True), sink_col)
    weights = jnp.where(key_mask, jnp.exp(masked - row_top), 0.0)
    denominator = jnp.sum(weights, axis=-1, keepdims=True) + jnp.exp(sink_col - row_top)
    return (weights / denominator).astype(BF16)


def attend_block(query_rows, key_rows, value_rows, query_pos, key_pos, sink_col):
    scores = jnp.einsum(
        "qkgd,skd->kgqs", query_rows, key_rows, preferred_element_type=F32
    ) * HD ** (-0.5)
    distance = query_pos[:, None] - key_pos[None, :]
    key_mask = (distance >= 0) & (distance < WINDOW) & (key_pos >= 0)[None, :]
    weights = sink_softmax(scores, key_mask, sink_col)
    mixed_rows = jnp.einsum("kgqs,skd->qkgd", weights, value_rows, preferred_element_type=F32)
    return mixed_rows.astype(BF16).reshape(query_rows.shape[0], -1)


def dot32(a, b):
    return jnp.dot(a, b, preferred_element_type=F32)


def project_whole(tokens, gain_attn, query_weight, key_weight, value_weight, attn_sinks, out_weight):
    tok_dev = tokens.shape[0]
    full_rows = lax.all_gather(tokens, "exp", axis=1, tiled=True)
    normed = rms_norm(full_rows, gain_attn)
    pieces = lax.all_gather((query_weight, key_weight, value_weight), "ctx", axis=1, tiled=True)
    query_lin, key_lin, value_lin = tuple(dot32(normed, piece) for piece in pieces)
    heads_local = query_lin.shape[1] // HD
    kv_local = key_lin.shape[1] // HD
    group_size = heads_local // kv_local
    position_ids = lax.axis_index("ctx") * tok_dev + jnp.arange(tok_dev, dtype=jnp.int32)
    angles_pos = position_ids.astype(F32)
    query = rotary(query_lin.reshape(tok_dev, heads_local, HD), angles_pos).astype(BF16)
    keys_own = rotary(key_lin.reshape(tok_dev, kv_local, HD), angles_pos).astype(BF16)
    key_value = jnp.stack([keys_own.reshape(tok_dev, kv_local * HD), value_lin.astype(BF16)])
    n_ctx = lax.axis_size("ctx")
    previous = lax.ppermute(key_value, "ctx", [(i, i + 1) for i in range(n_ctx - 1)])
    context = jnp.concatenate([previous, key_value], axis=1)
    key_pos = position_ids[0] - WINDOW + jnp.arange(tok_dev + WINDOW, dtype=jnp.int32)
    attended = attend_block(
        query.reshape(tok_dev, kv_local, group_size, HD),
        context[0].reshape(-1, kv_local, HD),
        context[1].reshape(-1, kv_local, HD),
        position_ids,
        key_pos,
        attn_sinks.reshape(kv_local, group_size, 1, 1),
    )
    head_terms = dot32(attended, lax.all_gather(out_weight, "ctx", axis=1, tiled=True))
    attn_proj = lax.psum(head_terms.astype(BF16), "exp").astype(F32)
    return (full_rows.astype(F32) + attn_proj).astype(BF16).T


def dot_nt(a, b):
    return lax.dot_general(a, b, (((1,), (1,)), ((), ())), preferred_element_type=F32)


def turn(values, cosine, signed_sine):
    width = values.shape[1]
    half = HD // 2
    lane = lax.broadcasted_iota(jnp.int32, values.shape, 1) % HD
    partner = jnp.where(
        lane < half,
        pltpu.roll(values, width - half, 1),
        pltpu.roll(values, half, 1),
    )
    return values * cosine + partner * signed_sine


def qkv_kernel(count, *refs):
    blocks, (weight_ref, kv_ref, cos_ref, sin_ref, q_ref, key_value_ref) = refs[:count], refs[count:]
    step = pl.program_id(0)
    rows = blocks[0].shape[0]
    weight = jnp.concatenate([weight_ref[0], weight_ref[1]], axis=1)
    cols = weight_ref.shape[2]
    for r in range(count):
        cosine, signed_sine = cos_ref[r], sin_ref[r]
        query = dot32(blocks[r][...], weight)
        for at in range(0, 2 * cols, cols):
            q_ref[r, :, at : at + cols] = turn(query[:, at : at + cols], cosine, signed_sine).astype(BF16)

    @pl.when(step == 0)
    def _():
        share = kv_ref.shape[1] // 2
        width = PLANE * share
        both = jnp.concatenate(
            [kv_ref[p, :share] for p in range(PLANE)] + [kv_ref[p, share:] for p in range(PLANE)], axis=0
        )
        for r in range(count):
            lines = dot_nt(blocks[r][...], both)
            key_value_ref[r, :, :width] = turn(lines[:, :width], cos_ref[r], sin_ref[r]).astype(BF16)
            key_value_ref[r, :, width:] = lines[:, width:].astype(BF16)


def project_blocks(blocks, weights, kv_all, cosine, signed_sine):
    count = len(blocks)
    rows, width = blocks[0].shape
    cols = weights.shape[2]
    kv_cols = kv_all.shape[1] * PLANE
    whole = lambda p: (0, 0, 0)
    return pl.pallas_call(
        functools.partial(qkv_kernel, count),
        grid=(PLANE // 2,),
        in_specs=[pl.BlockSpec((rows, width), lambda p: (0, 0))] * count
        + [
            pl.BlockSpec((2, width, cols), lambda p: (p, 0, 0)),
            pl.BlockSpec(kv_all.shape, whole),
            pl.BlockSpec(cosine.shape, whole),
            pl.BlockSpec(signed_sine.shape, whole),
        ],
        out_specs=[
            pl.BlockSpec((count, rows, 2 * cols), lambda p: (0, 0, p)),
            pl.BlockSpec((count, rows, kv_cols), whole),
        ],
        out_shape=[
            jax.ShapeDtypeStruct((count, rows, PLANE * cols), BF16),
            jax.ShapeDtypeStruct((count, rows, kv_cols), BF16),
        ],
        compiler_params=pltpu.CompilerParams(vmem_limit_bytes=40 * 2**20),
        cost_estimate=pl.CostEstimate(
            flops=2 * count * rows * width * (PLANE * cols + kv_cols),
            bytes_accessed=2 * width * (PLANE * cols + kv_cols + count * rows),
            transcendentals=0,
        ),
    )(*blocks, weights, kv_all, cosine, signed_sine)


def attend_kernel(
    place_ref, sinks_ref, q_ref, own_ref, previous_ref, even_ref, odd_ref, out_ref, att_ref, total_ref
):
    rows = q_ref.shape[0]
    pair = 2 * HD
    kv_heads = own_ref.shape[1] // pair
    kv_cols = kv_heads * HD
    pairs = q_ref.shape[1] // pair
    lane = lax.broadcasted_iota(jnp.int32, (rows, pair), 1)
    low = lane < HD

    def spread(values, head):
        moved = pltpu.roll(values.astype(F32), HD, 1)
        chunk = values.astype(F32)
        lower, upper = (chunk, moved) if head % 2 == 0 else (moved, chunk)
        zero = jnp.zeros_like(chunk)
        return jnp.concatenate(
            [jnp.where(low, lower, zero), jnp.where(low, zero, upper)], axis=0
        ).astype(BF16)

    def side(ref):
        tables = []
        for head in range(kv_heads):
            at = head // 2 * pair
            keys = spread(ref[:, at : at + pair], head)
            values = spread(ref[:, kv_cols + at : kv_cols + at + pair], head)
            tables.append((keys, values))
        return tables

    own, previous = side(own_ref), side(previous_ref)
    row = lax.broadcasted_iota(jnp.int32, (rows, rows), 0)
    col = lax.broadcasted_iota(jnp.int32, (rows, rows), 1)
    inside = col <= row
    shown = jnp.logical_or(inside, place_ref[0] == 0)
    scale = HD**-0.5
    for p in range(pairs):
        head = p * kv_heads // pairs
        chunk = q_ref[:, p * pair : (p + 1) * pair]
        scores_own = dot_nt(chunk, own[head][0])
        scores_previous = dot_nt(chunk, previous[head][0])
        probs_own, probs_previous = [], []
        for h in range(2):
            at = h * rows
            scores = jnp.where(
                inside, scores_own[:, at : at + rows], scores_previous[:, at : at + rows]
            ) * scale
            scores = jnp.where(shown, scores, -1e30)
            sink = sinks_ref[2 * p + h]
            top = jnp.maximum(jnp.max(scores, axis=1, keepdims=True), sink)
            weights = jnp.exp(scores - top)
            total = jnp.sum(weights, axis=1, keepdims=True) + jnp.exp(sink - top)
            probs = weights / total
            probs_own.append(jnp.where(inside, probs, 0.0).astype(BF16))
            probs_previous.append(jnp.where(inside, 0.0, probs).astype(BF16))
        mixed = dot32(jnp.concatenate(probs_own, axis=1), own[head][1])
        mixed = mixed + dot32(jnp.concatenate(probs_previous, axis=1), previous[head][1])
        att_ref[:, p * pair : (p + 1) * pair] = mixed.astype(BF16)

    half, groups, padded, depth = even_ref.shape
    cols = out_ref.shape[0] // (2 * half * groups)
    attended = att_ref[...]
    for side_at, weight_ref in enumerate((even_ref, odd_ref)):
        for i in range(half):
            terms = dot_nt(weight_ref[i].reshape(groups * padded, depth), attended)
            share = place_ref[1 + 2 * i + side_at]
            for g in range(groups):
                total_ref[g, share] = terms[g * padded : (g + 1) * padded]
    for g in range(groups):
        for p in range(2 * half):
            at = (g * 2 * half + p) * cols
            out_ref[at : at + cols, :] = total_ref[g, p, :cols, :]


def attend_and_project(place, sinks, query, own, previous, even, odd, width):
    rows = query.shape[0]
    half, groups, padded, depth = even.shape
    vmem = pl.BlockSpec(memory_space=pltpu.VMEM)
    smem = pl.BlockSpec(memory_space=pltpu.SMEM)
    return pl.pallas_call(
        attend_kernel,
        in_specs=[smem, smem] + [vmem] * 5,
        out_specs=vmem,
        out_shape=jax.ShapeDtypeStruct((width, rows), F32),
        scratch_shapes=[
            pltpu.VMEM((rows, depth), BF16),
            pltpu.VMEM((groups, 2 * half, padded, rows), F32),
        ],
        compiler_params=pltpu.CompilerParams(vmem_limit_bytes=40 * 2**20),
        cost_estimate=pl.CostEstimate(
            flops=2 * rows * depth * (width + 8 * rows),
            bytes_accessed=2 * (width * depth + 2 * width * rows),
            transcendentals=rows * rows * depth // HD,
        ),
    )(place, sinks, query, own, previous, even, odd)


def project_planes(tokens, gain_attn, query_weight, key_weight, value_weight, attn_sinks, out_weight):
    tok_dev, width = tokens.shape
    n_ctx = lax.axis_size("ctx")
    n_z = n_ctx // PLANE
    index = lax.axis_index("ctx")
    z, j = index // PLANE, index % PLANE
    planes = [[PLANE * a + b for b in range(PLANE)] for a in range(n_z)]

    def shift(block, steps):
        return lax.ppermute(block, "ctx", [(i, (i + steps * PLANE) % n_ctx) for i in range(n_ctx)])

    def behind(block):
        route = [(a * PLANE + b, a * PLANE + (b + 1) % PLANE) for a in range(n_z) for b in range(PLANE)]
        return lax.ppermute(block, "ctx", route)

    def swap(block, bits):
        return lax.ppermute(block, "ctx", [(i, i ^ bits) for i in range(n_ctx)])

    blocks = [rms_norm(tokens, gain_attn)]
    for _ in range(n_z - 1):
        blocks.append(shift(blocks[-1], -1))

    lanes = query_weight.shape[1]
    kv_rows = jnp.concatenate([key_weight.T, value_weight.T], axis=0)
    packed = jnp.concatenate([query_weight, kv_rows.reshape(-1, lanes)], axis=0)
    weights = lax.all_gather(packed, "ctx", axis_index_groups=planes)
    kv_all = weights[:, width:].reshape((PLANE,) + kv_rows.shape)

    cols = out_weight.shape[1]
    padded = -(-cols // 16) * 16
    group_rows = out_weight.shape[0] // n_z
    out_rows = jnp.pad(out_weight.T, ((0, padded - cols), (0, 0)))
    out_groups = jnp.stack(jnp.split(out_rows, n_z, axis=1))
    pieces = [
        shift(lax.dynamic_index_in_dim(out_groups, (z + s) % n_z, 0, keepdims=False), s) if s
        else lax.dynamic_index_in_dim(out_groups, z, 0, keepdims=False)
        for s in range(n_z)
    ]
    ordered = jnp.stack(pieces[::-1] + pieces[:0:-1])
    out_mine = lax.dynamic_slice_in_dim(ordered, n_z - 1 - z, n_z, 0)
    out_x, out_y = swap(out_mine, 2), swap(out_mine, 4)
    out_half = jnp.stack([out_mine, out_x, out_y, swap(out_mine, 6)])
    out_other = swap(out_half, 1)

    heads = PLANE * query_weight.shape[1] // HD
    sinks = lax.dynamic_slice_in_dim(attn_sinks, z * heads, heads)
    own_rows = jnp.arange(tok_dev, dtype=jnp.int32)
    lane = jnp.arange(2 * HD, dtype=jnp.int32) % HD
    half = HD // 2
    inverse_freq = jnp.exp(-(2.0 * (lane % half).astype(F32) / HD) * math.log(ROPE_BASE))
    numbers = ((z + jnp.arange(n_z, dtype=jnp.int32)) % n_z) * PLANE + j
    angles = (numbers[:, None] * tok_dev + own_rows[None, :]).astype(F32)[:, :, None] * inverse_freq
    signed_sine = jnp.where(lane < half, -jnp.sin(angles), jnp.sin(angles))
    queries, key_values = project_blocks(blocks, weights, kv_all, jnp.cos(angles), signed_sine)
    halos = behind(key_values)
    previous = jnp.where(j == 0, jnp.concatenate([halos[-1:], halos[:-1]]), halos)

    relative = jnp.arange(PLANE, dtype=jnp.int32) ^ j
    partial_sums = []
    for r in list(range(1, n_z)) + [0]:
        first = (numbers[r] == 0).astype(jnp.int32).reshape(1)
        partial_sums.append(
            attend_and_project(
                jnp.concatenate([first, relative]), sinks, queries[r], key_values[r], previous[r],
                out_half, out_other, width,
            )
        )
    running = partial_sums[0].astype(BF16)
    for term in partial_sums[1:]:
        running = shift(running, -1).astype(F32) + term
        if term is not partial_sums[-1]:
            running = running.astype(BF16)
    return (tokens.T.astype(F32) + running).astype(BF16)


def expert_kernel(tile, hidden, rows_ref, gate_ref, upper_ref, down_ref, out_ref, total_ref):
    step = pl.program_id(0)
    steps = pl.num_programs(0)

    def add(count, initial):
        rows = rows_ref[...]
        gate = dot32(rows, gate_ref[0, :, :count])
        upper = dot32(rows, upper_ref[0, :, :count])
        activation = (gate * jax.nn.sigmoid(1.702 * gate) * (upper + 1.0)).astype(BF16)
        terms = dot32(activation, down_ref[:count, :])
        total_ref[...] = terms if initial else total_ref[...] + terms

    last = hidden - (-(-hidden // tile) - 1) * tile

    @pl.when(step == 0)
    def _():
        add(tile, True)

    @pl.when(jnp.logical_and(step > 0, step < steps - 1))
    def _():
        add(tile, False)

    @pl.when(step == steps - 1)
    def _():
        add(last, False)
        out_ref[...] = total_ref[...].astype(BF16)


def run_expert(rows, gate_up, down):
    count, width = rows.shape
    hidden = down.shape[0]
    tile = 512 if hidden > 1024 else 256
    return pl.pallas_call(
        functools.partial(expert_kernel, tile, hidden),
        grid=(-(-hidden // tile),),
        in_specs=[
            pl.BlockSpec((count, width), lambda f: (0, 0)),
            pl.BlockSpec((1, width, tile), lambda f: (0, 0, f)),
            pl.BlockSpec((1, width, tile), lambda f: (1, 0, f)),
            pl.BlockSpec((tile, width), lambda f: (f, 0)),
        ],
        out_specs=pl.BlockSpec((count, width), lambda f: (0, 0)),
        out_shape=jax.ShapeDtypeStruct((count, width), BF16),
        scratch_shapes=[pltpu.VMEM((count, width), F32)],
        compiler_params=pltpu.CompilerParams(vmem_limit_bytes=52 * 2**20),
        cost_estimate=pl.CostEstimate(
            flops=6 * count * width * hidden,
            bytes_accessed=6 * width * hidden + 4 * count * width,
            transcendentals=count * hidden,
        ),
    )(rows, gate_up, gate_up, down)


def slot_chunks(capacity):
    first = min(8, capacity)
    return [first, capacity - first] if capacity > first else [first]


def per_device(
    tokens,
    route_ids,
    combine,
    gain_attn,
    gain_moe,
    query_weight,
    key_weight,
    value_weight,
    attn_sinks,
    out_weight,
    gate_up_weight,
    down_weight,
):
    tok_dev, width_local = tokens.shape
    n_ctx = lax.axis_size("ctx")
    n_exp = lax.axis_size("exp")
    project = project_planes if n_exp == 1 and n_ctx % PLANE == 0 else project_whole
    residual = project(
        tokens, gain_attn, query_weight, key_weight, value_weight, attn_sinks, out_weight
    )
    width = residual.shape[0]
    wide = residual.astype(F32)
    meansq = jnp.mean(wide * wide, axis=0, keepdims=True)
    normed_moe = (wide * lax.rsqrt(meansq + EPSILON) * gain_moe[:, None]).astype(BF16)
    exp_index = lax.axis_index("exp")
    residual_local = lax.dynamic_slice_in_dim(residual, exp_index * width_local, width_local, 0)

    top_count = route_ids.shape[1]
    capacity = tok_dev * top_count * 5 // (4 * n_ctx)
    named = route_ids[:, :, None] == jnp.arange(n_ctx, dtype=jnp.int32)[None, None, :]
    member = jnp.any(named, axis=1)
    weight_of = jnp.sum(jnp.where(named, combine[:, :, None], 0.0), axis=1)
    rows = jnp.arange(tok_dev, dtype=jnp.int32)
    earlier = (rows[:, None] > rows[None, :]).astype(BF16)
    slot_of = dot32(earlier, member.astype(BF16)).astype(jnp.int32)
    slot_of = jnp.where(member, slot_of, -1)

    def exchange(rows_of, size):
        shape = (n_ctx, size, width) if size % 8 == 0 or size % 4 else (n_ctx, size // 4, 4, width)
        return lax.all_to_all(rows_of.reshape(shape), "ctx", split_axis=0, concat_axis=0, tiled=True)

    sizes = slot_chunks(capacity)
    outgoing, scales = [], []
    first = 0
    for size in sizes:
        slots = first + jnp.arange(size, dtype=jnp.int32)
        chosen = (slot_of[:, :, None] == slots[None, None, :]).reshape(tok_dev, n_ctx * size)
        rows_out = lax.dot_general(
            chosen.astype(BF16), normed_moe, (((0,), (1,)), ((), ())), preferred_element_type=F32
        ).astype(BF16)
        outgoing.append(rows_out)
        scale = jnp.where(chosen, jnp.repeat(weight_of, size, axis=1), 0.0)
        high = scale.astype(BF16)
        low = (scale - high.astype(F32)).astype(BF16)
        scales.append(jnp.concatenate([high, low], axis=0))
        first += size

    received = []
    for size, rows_out in zip(sizes, outgoing):
        if received:
            rows_out, received[-1] = lax.optimization_barrier((rows_out, received[-1]))
        received.append(exchange(rows_out, size))
    received = [rows_in.reshape(-1, width) for rows_in in received]

    results = [run_expert(rows_in, gate_up_weight[0], down_weight[0]) for rows_in in received]

    answers = []
    for size, result in zip(sizes, results):
        if answers:
            result, answers[-1] = lax.optimization_barrier((result, answers[-1]))
        else:
            result, received[-1] = lax.optimization_barrier((result, received[-1]))
        answers.append(exchange(result, size))

    moe_out = jnp.zeros((width_local, tok_dev), F32)
    for size, scale, answer in zip(sizes, scales, answers):
        if n_exp > 1:
            answer = lax.psum_scatter(answer, "exp", scatter_dimension=answer.ndim - 1, tiled=True)
        terms = lax.dot_general(
            answer.reshape(n_ctx * size, width_local), scale, (((0,), (1,)), ((), ())),
            preferred_element_type=F32,
        )
        moe_out = moe_out + terms[:, :tok_dev] + terms[:, tok_dev:]
    return (residual_local.astype(F32) + moe_out).astype(BF16).T


def solution(mesh):
    return jax.shard_map(
        per_device,
        mesh=mesh,
        in_specs=(
            P("ctx", "exp"),
            P("ctx", None),
            P("ctx", None),
            P(),
            P(),
            P(None, ("exp", "ctx")),
            P(None, ("exp", "ctx")),
            P(None, ("exp", "ctx")),
            P("exp"),
            P("exp", "ctx"),
            P("ctx", None, None, "exp"),
            P("ctx", "exp", None),
        ),
        out_specs=P("ctx", "exp"),
        check_vma=False,
    )
```

```python
import functools
import math

import jax
import jax.numpy as jnp
from jax import lax
from jax.experimental import pallas as pl
from jax.experimental.pallas import tpu as pltpu
from jax.sharding import PartitionSpec as P

HD = 64
WINDOW = 128
EPSILON = 1e-05
ROPE_BASE = 150000.0
PLANE = 8
BF16 = jnp.bfloat16
F32 = jnp.float32


def rms_norm(values, gain):
    wide = values.astype(F32)
    meansq = jnp.mean(wide * wide, axis=-1, keepdims=True)
    return (wide * lax.rsqrt(meansq + EPSILON) * gain).astype(BF16)


def rms_norm_t(values, gain):
    wide = values.astype(F32)
    meansq = jnp.mean(wide * wide, axis=0, keepdims=True)
    return (wide * lax.rsqrt(meansq + EPSILON) * gain[:, None]).astype(BF16)


def rotary(values, angles_pos):
    half_dim = values.shape[-1] // 2
    inverse_freq = jnp.exp(
        -(2.0 * jnp.arange(half_dim, dtype=F32) / values.shape[-1]) * math.log(ROPE_BASE)
    )
    angles = angles_pos[:, None] * inverse_freq[None, :]
    cosine = jnp.cos(angles)[:, None, :]
    sine_part = jnp.sin(angles)[:, None, :]
    first_half = values[..., :half_dim]
    second_half = values[..., half_dim:]
    return jnp.concatenate(
        [
            first_half * cosine - second_half * sine_part,
            second_half * cosine + first_half * sine_part,
        ],
        axis=-1,
    )


def sink_softmax(scores, key_mask, sink_col):
    masked = jnp.where(key_mask, scores, -1e30)
    row_top = jnp.maximum(jnp.max(masked, axis=-1, keepdims=True), sink_col)
    weights = jnp.where(key_mask, jnp.exp(masked - row_top), 0.0)
    denominator = jnp.sum(weights, axis=-1, keepdims=True) + jnp.exp(sink_col - row_top)
    return (weights / denominator).astype(BF16)


def attend_block(query_rows, key_rows, value_rows, query_pos, key_pos, sink_col):
    scores = jnp.einsum(
        "qkgd,skd->kgqs", query_rows, key_rows, preferred_element_type=F32
    ) * HD ** (-0.5)
    distance = query_pos[:, None] - key_pos[None, :]
    key_mask = (distance >= 0) & (distance < WINDOW) & (key_pos >= 0)[None, :]
    weights = sink_softmax(scores, key_mask, sink_col)
    mixed_rows = jnp.einsum("kgqs,skd->qkgd", weights, value_rows, preferred_element_type=F32)
    return mixed_rows.astype(BF16).reshape(query_rows.shape[0], -1)


def dot32(a, b):
    return jnp.dot(a, b, preferred_element_type=F32)


def project_whole(tokens, gain_attn, query_weight, key_weight, value_weight, attn_sinks, out_weight):
    tok_dev = tokens.shape[0]
    full_rows = lax.all_gather(tokens, "exp", axis=1, tiled=True)
    normed = rms_norm(full_rows, gain_attn)
    pieces = lax.all_gather((query_weight, key_weight, value_weight), "ctx", axis=1, tiled=True)
    query_lin, key_lin, value_lin = tuple(dot32(normed, piece) for piece in pieces)
    heads_local = query_lin.shape[1] // HD
    kv_local = key_lin.shape[1] // HD
    group_size = heads_local // kv_local
    position_ids = lax.axis_index("ctx") * tok_dev + jnp.arange(tok_dev, dtype=jnp.int32)
    angles_pos = position_ids.astype(F32)
    query = rotary(query_lin.reshape(tok_dev, heads_local, HD), angles_pos).astype(BF16)
    keys_own = rotary(key_lin.reshape(tok_dev, kv_local, HD), angles_pos).astype(BF16)
    key_value = jnp.stack([keys_own.reshape(tok_dev, kv_local * HD), value_lin.astype(BF16)])
    n_ctx = lax.axis_size("ctx")
    previous = lax.ppermute(key_value, "ctx", [(i, i + 1) for i in range(n_ctx - 1)])
    context = jnp.concatenate([previous, key_value], axis=1)
    key_pos = position_ids[0] - WINDOW + jnp.arange(tok_dev + WINDOW, dtype=jnp.int32)
    attended = attend_block(
        query.reshape(tok_dev, kv_local, group_size, HD),
        context[0].reshape(-1, kv_local, HD),
        context[1].reshape(-1, kv_local, HD),
        position_ids,
        key_pos,
        attn_sinks.reshape(kv_local, group_size, 1, 1),
    )
    head_terms = dot32(attended, lax.all_gather(out_weight, "ctx", axis=1, tiled=True))
    attn_proj = lax.psum(head_terms.astype(BF16), "exp").astype(F32)
    return (full_rows.astype(F32) + attn_proj).astype(BF16).T


def dot_nt(a, b):
    return lax.dot_general(a, b, (((1,), (1,)), ((), ())), preferred_element_type=F32)


def turn(values, cosine, signed_sine):
    width = values.shape[1]
    half = HD // 2
    lane = lax.broadcasted_iota(jnp.int32, values.shape, 1) % HD
    partner = jnp.where(
        lane < half,
        pltpu.roll(values, width - half, 1),
        pltpu.roll(values, half, 1),
    )
    return values * cosine + partner * signed_sine


def qkv_kernel(count, *refs):
    blocks, refs = refs[:count], refs[count:]
    weight_ref, cos_ref, sin_ref, q_ref, key_value_ref, rows_ref, kv_ref = refs
    step = pl.program_id(0)
    width, rows = blocks[0].shape
    cols = weight_ref.shape[2]
    share = kv_ref.shape[2]

    @pl.when(step == 0)
    def _():
        for r in range(count):
            rows_ref[r * rows : (r + 1) * rows, :] = blocks[r][...].T

    for i in range(2):
        for tile in range(-(-width // cols)):
            at, lanes = width + 2 * share * tile, slice(tile * cols, (tile + 1) * cols)
            for part in range(2):
                kv_ref[part, 2 * step + i, :, lanes] = weight_ref[i, at + part * share : at + (part + 1) * share]

    weight = jnp.concatenate([weight_ref[0, :width], weight_ref[1, :width]], axis=1)
    query = dot32(rows_ref[...], weight)
    for r in range(count):
        for at in range(0, 2 * cols, cols):
            piece = query[r * rows : (r + 1) * rows, at : at + cols]
            q_ref[r, :, at : at + cols] = turn(piece, cos_ref[r], sin_ref[r]).astype(BF16)

    @pl.when(step == pl.num_programs(0) - 1)
    def _():
        both = kv_ref[...].reshape(2 * PLANE * share, kv_ref.shape[3])[:, :width]
        lines = dot_nt(rows_ref[...], both)
        half = PLANE * share
        for r in range(count):
            piece = lines[r * rows : (r + 1) * rows]
            key_value_ref[r, :, :half] = turn(piece[:, :half], cos_ref[r], sin_ref[r]).astype(BF16)
            key_value_ref[r, :, half:] = piece[:, half:].astype(BF16)


def project_blocks(blocks, weights, share, cosine, signed_sine):
    count = len(blocks)
    width, rows = blocks[0].shape
    cols = weights.shape[2]
    tiles = -(-width // cols)
    kv_cols = 2 * PLANE * share
    whole = lambda p: (0, 0, 0)
    return pl.pallas_call(
        functools.partial(qkv_kernel, count),
        grid=(PLANE // 2,),
        in_specs=[pl.BlockSpec((width, rows), lambda p: (0, 0))] * count
        + [
            pl.BlockSpec((2,) + weights.shape[1:], lambda p: (p, 0, 0)),
            pl.BlockSpec(cosine.shape, whole),
            pl.BlockSpec(signed_sine.shape, whole),
        ],
        out_specs=[
            pl.BlockSpec((count, rows, 2 * cols), lambda p: (0, 0, p)),
            pl.BlockSpec((count, rows, kv_cols), whole),
        ],
        out_shape=[
            jax.ShapeDtypeStruct((count, rows, PLANE * cols), BF16),
            jax.ShapeDtypeStruct((count, rows, kv_cols), BF16),
        ],
        scratch_shapes=[
            pltpu.VMEM((count * rows, width), BF16),
            pltpu.VMEM((2, PLANE, share, tiles * cols), BF16),
        ],
        compiler_params=pltpu.CompilerParams(vmem_limit_bytes=58 * 2**20),
        cost_estimate=pl.CostEstimate(
            flops=2 * count * rows * width * (PLANE * cols + kv_cols),
            bytes_accessed=2 * width * (PLANE * cols + kv_cols + count * rows),
            transcendentals=0,
        ),
    )(*blocks, weights, cosine, signed_sine)


def attend_kernel(
    place_ref, sinks_ref, q_ref, own_ref, previous_ref, even_ref, odd_ref, out_ref, att_ref, total_ref
):
    rows = q_ref.shape[0]
    pair = 2 * HD
    kv_heads = own_ref.shape[1] // pair
    kv_cols = kv_heads * HD
    pairs = q_ref.shape[1] // pair
    lane = lax.broadcasted_iota(jnp.int32, (rows, pair), 1)
    low = lane < HD

    def spread(values, head):
        moved = pltpu.roll(values.astype(F32), HD, 1)
        chunk = values.astype(F32)
        lower, upper = (chunk, moved) if head % 2 == 0 else (moved, chunk)
        zero = jnp.zeros_like(chunk)
        return jnp.concatenate(
            [jnp.where(low, lower, zero), jnp.where(low, zero, upper)], axis=0
        ).astype(BF16)

    def side(ref):
        tables = []
        for head in range(kv_heads):
            at = head // 2 * pair
            keys = spread(ref[:, at : at + pair], head)
            values = spread(ref[:, kv_cols + at : kv_cols + at + pair], head)
            tables.append((keys, values))
        return tables

    own, previous = side(own_ref), side(previous_ref)
    row = lax.broadcasted_iota(jnp.int32, (rows, rows), 0)
    col = lax.broadcasted_iota(jnp.int32, (rows, rows), 1)
    inside = col <= row
    shown = jnp.logical_or(inside, place_ref[0] == 0)
    scale = HD**-0.5
    for p in range(pairs):
        head = p * kv_heads // pairs
        chunk = q_ref[:, p * pair : (p + 1) * pair]
        scores_own = dot_nt(chunk, own[head][0])
        scores_previous = dot_nt(chunk, previous[head][0])
        probs_own, probs_previous = [], []
        for h in range(2):
            at = h * rows
            scores = jnp.where(
                inside, scores_own[:, at : at + rows], scores_previous[:, at : at + rows]
            ) * scale
            scores = jnp.where(shown, scores, -1e30)
            sink = sinks_ref[2 * p + h]
            top = jnp.maximum(jnp.max(scores, axis=1, keepdims=True), sink)
            weights = jnp.exp(scores - top)
            total = jnp.sum(weights, axis=1, keepdims=True) + jnp.exp(sink - top)
            probs = weights / total
            probs_own.append(jnp.where(inside, probs, 0.0).astype(BF16))
            probs_previous.append(jnp.where(inside, 0.0, probs).astype(BF16))
        mixed = dot32(jnp.concatenate(probs_own, axis=1), own[head][1])
        mixed = mixed + dot32(jnp.concatenate(probs_previous, axis=1), previous[head][1])
        att_ref[:, p * pair : (p + 1) * pair] = mixed.astype(BF16)

    half, groups, padded, depth = even_ref.shape
    cols = out_ref.shape[0] // (2 * half * groups)
    attended = att_ref[...]
    for side_at, weight_ref in enumerate((even_ref, odd_ref)):
        for i in range(half):
            terms = dot_nt(weight_ref[i].reshape(groups * padded, depth), attended)
            share = place_ref[1 + 2 * i + side_at]
            for g in range(groups):
                total_ref[g, share] = terms[g * padded : (g + 1) * padded]
    for g in range(groups):
        for p in range(2 * half):
            at = (g * 2 * half + p) * cols
            out_ref[at : at + cols, :] = total_ref[g, p, :cols, :]


def attend_and_project(place, sinks, query, own, previous, even, odd, width):
    rows = query.shape[0]
    half, groups, padded, depth = even.shape
    vmem = pl.BlockSpec(memory_space=pltpu.VMEM)
    smem = pl.BlockSpec(memory_space=pltpu.SMEM)
    return pl.pallas_call(
        attend_kernel,
        in_specs=[smem, smem] + [vmem] * 5,
        out_specs=vmem,
        out_shape=jax.ShapeDtypeStruct((width, rows), F32),
        scratch_shapes=[
            pltpu.VMEM((rows, depth), BF16),
            pltpu.VMEM((groups, 2 * half, padded, rows), F32),
        ],
        compiler_params=pltpu.CompilerParams(vmem_limit_bytes=40 * 2**20),
        cost_estimate=pl.CostEstimate(
            flops=2 * rows * depth * (width + 8 * rows),
            bytes_accessed=2 * (width * depth + 2 * width * rows),
            transcendentals=rows * rows * depth // HD,
        ),
    )(place, sinks, query, own, previous, even, odd)


def project_planes(tokens, gain_attn, query_weight, key_weight, value_weight, attn_sinks, out_weight):
    tok_dev, width = tokens.shape
    n_ctx = lax.axis_size("ctx")
    n_z = n_ctx // PLANE
    index = lax.axis_index("ctx")
    z, j = index // PLANE, index % PLANE
    planes = [[PLANE * a + b for b in range(PLANE)] for a in range(n_z)]

    def shift(block, steps):
        return lax.ppermute(block, "ctx", [(i, (i + steps * PLANE) % n_ctx) for i in range(n_ctx)])

    def behind(block):
        route = [(a * PLANE + b, a * PLANE + (b + 1) % PLANE) for a in range(n_z) for b in range(PLANE)]
        return lax.ppermute(block, "ctx", route)

    def swap(block, bits):
        return lax.ppermute(block, "ctx", [(i, i ^ bits) for i in range(n_ctx)])

    tokens_t = tokens.T
    blocks = [rms_norm_t(tokens_t, gain_attn)]

    lanes = query_weight.shape[1]
    share = key_weight.shape[1]
    tiles = -(-width // lanes)
    kv_rows = jnp.concatenate([key_weight.T, value_weight.T], axis=0)
    kv_rows = jnp.pad(kv_rows, ((0, 0), (0, tiles * lanes - width))).reshape(2 * share, tiles, lanes)
    packed = jnp.concatenate(
        [query_weight, kv_rows.transpose(1, 0, 2).reshape(tiles * 2 * share, lanes)], axis=0
    )
    weights = lax.all_gather(packed, "ctx", axis_index_groups=planes)

    cols = out_weight.shape[1]
    padded = -(-cols // 16) * 16
    group_rows = out_weight.shape[0] // n_z
    out_rows = jnp.pad(out_weight.T, ((0, padded - cols), (0, 0)))
    out_rows, blocks[0] = lax.optimization_barrier((out_rows, blocks[0]))
    blocks.append(shift(blocks[0], -1))
    out_groups = jnp.stack(jnp.split(out_rows, n_z, axis=1))
    pieces = [
        shift(lax.dynamic_index_in_dim(out_groups, (z + s) % n_z, 0, keepdims=False), s) if s
        else lax.dynamic_index_in_dim(out_groups, z, 0, keepdims=False)
        for s in range(n_z)
    ]
    ordered = jnp.stack(pieces[::-1] + pieces[:0:-1])
    out_mine = lax.dynamic_slice_in_dim(ordered, n_z - 1 - z, n_z, 0)
    out_mine, blocks[1] = lax.optimization_barrier((out_mine, blocks[1]))
    for _ in range(n_z - 2):
        blocks.append(shift(blocks[-1], -1))
    out_half = jnp.stack([out_mine] + [swap(out_mine, bits) for bits in (2, 4, 6)])
    second = min(2, n_z - 1)
    out_half, blocks[second] = lax.optimization_barrier((out_half, blocks[second]))
    out_other = swap(out_half, 1)

    heads = PLANE * query_weight.shape[1] // HD
    sinks = lax.dynamic_slice_in_dim(attn_sinks, z * heads, heads)
    own_rows = jnp.arange(tok_dev, dtype=jnp.int32)
    lane = jnp.arange(2 * HD, dtype=jnp.int32) % HD
    half = HD // 2
    inverse_freq = jnp.exp(-(2.0 * (lane % half).astype(F32) / HD) * math.log(ROPE_BASE))
    numbers = ((z + jnp.arange(n_z, dtype=jnp.int32)) % n_z) * PLANE + j
    angles = (numbers[:, None] * tok_dev + own_rows[None, :]).astype(F32)[:, :, None] * inverse_freq
    signed_sine = jnp.where(lane < half, -jnp.sin(angles), jnp.sin(angles))
    queries, key_values = project_blocks(blocks, weights, share, jnp.cos(angles), signed_sine)
    halos = behind(key_values)
    previous = jnp.where(j == 0, jnp.concatenate([halos[-1:], halos[:-1]]), halos)

    relative = jnp.arange(PLANE, dtype=jnp.int32) ^ j
    partial_sums = []
    for r in list(range(1, n_z)) + [0]:
        first = (numbers[r] == 0).astype(jnp.int32).reshape(1)
        partial_sums.append(
            attend_and_project(
                jnp.concatenate([first, relative]), sinks, queries[r], key_values[r], previous[r],
                out_half, out_other, width,
            )
        )
    running = partial_sums[0].astype(BF16)
    for term in partial_sums[1:]:
        running = shift(running, -1).astype(F32) + term
        if term is not partial_sums[-1]:
            running = running.astype(BF16)
    return (tokens_t.astype(F32) + running).astype(BF16)


def expert_kernel(tile, hidden, rows_ref, gate_ref, upper_ref, down_ref, out_ref, total_ref):
    step = pl.program_id(0)
    steps = pl.num_programs(0)

    def add(count, initial):
        rows = rows_ref[...]
        gate = dot32(rows, gate_ref[0, :, :count])
        upper = dot32(rows, upper_ref[0, :, :count])
        activation = (gate * jax.nn.sigmoid(1.702 * gate) * (upper + 1.0)).astype(BF16)
        terms = dot32(activation, down_ref[:count, :])
        total_ref[...] = terms if initial else total_ref[...] + terms

    last = hidden - (-(-hidden // tile) - 1) * tile

    @pl.when(step == 0)
    def _():
        add(tile, True)

    @pl.when(jnp.logical_and(step > 0, step < steps - 1))
    def _():
        add(tile, False)

    @pl.when(step == steps - 1)
    def _():
        add(last, False)
        out_ref[...] = total_ref[...].astype(BF16)


def run_expert(rows, gate_up, down):
    count, width = rows.shape
    hidden = down.shape[0]
    tile = 512 if hidden > 1024 else 256
    return pl.pallas_call(
        functools.partial(expert_kernel, tile, hidden),
        grid=(-(-hidden // tile),),
        in_specs=[
            pl.BlockSpec((count, width), lambda f: (0, 0)),
            pl.BlockSpec((1, width, tile), lambda f: (0, 0, f)),
            pl.BlockSpec((1, width, tile), lambda f: (1, 0, f)),
            pl.BlockSpec((tile, width), lambda f: (f, 0)),
        ],
        out_specs=pl.BlockSpec((count, width), lambda f: (0, 0)),
        out_shape=jax.ShapeDtypeStruct((count, width), BF16),
        scratch_shapes=[pltpu.VMEM((count, width), F32)],
        compiler_params=pltpu.CompilerParams(vmem_limit_bytes=52 * 2**20),
        cost_estimate=pl.CostEstimate(
            flops=6 * count * width * hidden,
            bytes_accessed=6 * width * hidden + 4 * count * width,
            transcendentals=count * hidden,
        ),
    )(rows, gate_up, gate_up, down)


def slot_chunks(capacity):
    first = min(8, capacity)
    return [first, capacity - first] if capacity > first else [first]


def experts_whole(normed, slot_of, weight_of, capacity, gate_up, down):
    width, tok_dev = normed.shape
    n_ctx, n_exp = lax.axis_size("ctx"), lax.axis_size("exp")
    width_local = width // n_exp

    def exchange(rows_of, size):
        shape = (n_ctx, size, width) if size % 8 == 0 or size % 4 else (n_ctx, size // 4, 4, width)
        return lax.all_to_all(rows_of.reshape(shape), "ctx", split_axis=0, concat_axis=0, tiled=True)

    sizes = slot_chunks(capacity)
    outgoing, scales = [], []
    first = 0
    for size in sizes:
        slots = first + jnp.arange(size, dtype=jnp.int32)
        chosen = (slot_of[:, :, None] == slots[None, None, :]).reshape(tok_dev, n_ctx * size)
        rows_out = lax.dot_general(
            chosen.astype(BF16), normed, (((0,), (1,)), ((), ())), preferred_element_type=F32
        ).astype(BF16)
        outgoing.append(rows_out)
        scale = jnp.where(chosen, jnp.repeat(weight_of, size, axis=1), 0.0)
        high = scale.astype(BF16)
        low = (scale - high.astype(F32)).astype(BF16)
        scales.append(jnp.concatenate([high, low], axis=0))
        first += size

    received = []
    for size, rows_out in zip(sizes, outgoing):
        if received:
            rows_out, received[-1] = lax.optimization_barrier((rows_out, received[-1]))
        received.append(exchange(rows_out, size))
    received = [rows_in.reshape(-1, width) for rows_in in received]

    results = [run_expert(rows_in, gate_up, down) for rows_in in received]

    answers = []
    for size, result in zip(sizes, results):
        if answers:
            result, answers[-1] = lax.optimization_barrier((result, answers[-1]))
        else:
            result, received[-1] = lax.optimization_barrier((result, received[-1]))
        answers.append(exchange(result, size))

    moe_out = jnp.zeros((width_local, tok_dev), F32)
    for size, scale, answer in zip(sizes, scales, answers):
        if n_exp > 1:
            answer = lax.psum_scatter(answer, "exp", scatter_dimension=answer.ndim - 1, tiled=True)
        terms = lax.dot_general(
            answer.reshape(n_ctx * size, width_local), scale, (((0,), (1,)), ((), ())),
            preferred_element_type=F32,
        )
        moe_out = moe_out + terms[:, :tok_dev] + terms[:, tok_dev:]
    return moe_out


def dispatch_kernel(slots_ref, normed_ref, out_ref):
    count, rows = slots_ref.shape
    size = out_ref.shape[0] // count
    slot = lax.broadcasted_iota(jnp.int32, (count, size, rows), 1).astype(F32)
    chosen = jnp.where(slots_ref[...][:, None, :] == slot, 1.0, 0.0).reshape(count * size, rows)
    out_ref[...] = dot_nt(chosen.astype(BF16), normed_ref[...]).astype(BF16)


def dispatch(slots, normed, size):
    width, rows = normed.shape
    total = slots.shape[0] * size
    return pl.pallas_call(
        dispatch_kernel,
        out_shape=jax.ShapeDtypeStruct((total, width), BF16),
        compiler_params=pltpu.CompilerParams(vmem_limit_bytes=16 * 2**20),
        cost_estimate=pl.CostEstimate(
            flops=2 * total * rows * width, bytes_accessed=2 * width * (total + rows), transcendentals=0
        ),
    )(slots, normed)


def experts_planes(normed, slot_of, weight_of, capacity, gate_up, down):
    width, tok_dev = normed.shape
    n_ctx = lax.axis_size("ctx")
    n_z = n_ctx // PLANE
    z = lax.axis_index("ctx") // PLANE
    planes = [[PLANE * a + b for b in range(PLANE)] for a in range(n_z)]
    columns = [[PLANE * a + b for a in range(n_z)] for b in range(PLANE)]
    size = -(-capacity // 8) * 8

    def shift(block):
        return lax.ppermute(block, "ctx", [(i, (i - PLANE) % n_ctx) for i in range(n_ctx)])

    def exchange(rows_of):
        parts = lax.all_to_all(
            rows_of.reshape(PLANE, size, width), "ctx", split_axis=0, concat_axis=0, tiled=True,
            axis_index_groups=planes,
        )
        return parts.reshape(PLANE * size, width)

    table = jnp.concatenate([slot_of.astype(F32).T, weight_of.T], axis=0)
    tables = lax.all_gather(table, "ctx", axis_index_groups=columns)
    tables = tables.reshape(n_z, 2, n_z, PLANE, tok_dev)
    tables = lax.dynamic_index_in_dim(tables, z, 2, keepdims=False)
    twice = jnp.concatenate([tables, tables], axis=0)
    tables = lax.dynamic_slice_in_dim(twice, z, n_z, 0)

    blocks, received, sums = [normed], [], []
    for _ in range(n_z - 1):
        blocks.append(shift(blocks[-1]))
    for r in range(n_z):
        received.append(exchange(dispatch(tables[r, 0], blocks[r], size)))
    for r in range(n_z):
        answer = exchange(run_expert(received[r], gate_up, down))
        slots, weights = tables[r, 0][:, None, :], tables[r, 1][:, None, :]
        chosen = slots == jnp.arange(size, dtype=F32)[None, :, None]
        scale = jnp.where(chosen, weights, 0.0).reshape(PLANE * size, tok_dev)
        high = scale.astype(BF16)
        low = (scale - high.astype(F32)).astype(BF16)
        terms = lax.dot_general(
            answer, jnp.concatenate([high, low], axis=1), (((0,), (0,)), ((), ())),
            preferred_element_type=F32,
        )
        sums.append(terms[:, :tok_dev] + terms[:, tok_dev:])
    running = sums[1].astype(BF16)
    for term in sums[2:]:
        running = (shift(running).astype(F32) + term).astype(BF16)
    return shift(running).astype(F32) + sums[0]


def per_device(
    tokens,
    route_ids,
    combine,
    gain_attn,
    gain_moe,
    query_weight,
    key_weight,
    value_weight,
    attn_sinks,
    out_weight,
    gate_up_weight,
    down_weight,
):
    tok_dev, width_local = tokens.shape
    n_ctx = lax.axis_size("ctx")
    n_exp = lax.axis_size("exp")
    by_planes = n_exp == 1 and n_ctx % PLANE == 0 and n_ctx > PLANE
    project = project_planes if by_planes else project_whole
    residual = project(
        tokens, gain_attn, query_weight, key_weight, value_weight, attn_sinks, out_weight
    )
    width = residual.shape[0]
    normed_moe = rms_norm_t(residual, gain_moe)
    exp_index = lax.axis_index("exp")
    residual_local = lax.dynamic_slice_in_dim(residual, exp_index * width_local, width_local, 0)

    top_count = route_ids.shape[1]
    capacity = tok_dev * top_count * 5 // (4 * n_ctx)
    named = route_ids[:, :, None] == jnp.arange(n_ctx, dtype=jnp.int32)[None, None, :]
    member = jnp.any(named, axis=1)
    weight_of = jnp.sum(jnp.where(named, combine[:, :, None], 0.0), axis=1)
    rows = jnp.arange(tok_dev, dtype=jnp.int32)
    earlier = (rows[:, None] > rows[None, :]).astype(BF16)
    slot_of = dot32(earlier, member.astype(BF16)).astype(jnp.int32)
    slot_of = jnp.where(member, slot_of, -1)

    experts = experts_planes if by_planes else experts_whole
    moe_out = experts(normed_moe, slot_of, weight_of, capacity, gate_up_weight[0], down_weight[0])
    return (residual_local.astype(F32) + moe_out).astype(BF16).T


def solution(mesh):
    return jax.shard_map(
        per_device,
        mesh=mesh,
        in_specs=(
            P("ctx", "exp"),
            P("ctx", None),
            P("ctx", None),
            P(),
            P(),
            P(None, ("exp", "ctx")),
            P(None, ("exp", "ctx")),
            P(None, ("exp", "ctx")),
            P("exp"),
            P("exp", "ctx"),
            P("ctx", None, None, "exp"),
            P("ctx", "exp", None),
        ),
        out_specs=P("ctx", "exp"),
        check_vma=False,
    )
```

```python
import functools
import math

import jax
import jax.numpy as jnp
from jax import lax
from jax.experimental import pallas as pl
from jax.experimental.pallas import tpu as pltpu
from jax.sharding import PartitionSpec as P

HD = 64
WINDOW = 128
EPSILON = 1e-05
ROPE_BASE = 150000.0
PLANE = 8
BF16 = jnp.bfloat16
F32 = jnp.float32


def rms_norm(values, gain):
    wide = values.astype(F32)
    meansq = jnp.mean(wide * wide, axis=-1, keepdims=True)
    return (wide * lax.rsqrt(meansq + EPSILON) * gain).astype(BF16)


def rms_norm_t(values, gain):
    wide = values.astype(F32)
    meansq = jnp.mean(wide * wide, axis=0, keepdims=True)
    return (wide * lax.rsqrt(meansq + EPSILON) * gain[:, None]).astype(BF16)


def rotary(values, angles_pos):
    half_dim = values.shape[-1] // 2
    inverse_freq = jnp.exp(
        -(2.0 * jnp.arange(half_dim, dtype=F32) / values.shape[-1]) * math.log(ROPE_BASE)
    )
    angles = angles_pos[:, None] * inverse_freq[None, :]
    cosine = jnp.cos(angles)[:, None, :]
    sine_part = jnp.sin(angles)[:, None, :]
    first_half = values[..., :half_dim]
    second_half = values[..., half_dim:]
    return jnp.concatenate(
        [
            first_half * cosine - second_half * sine_part,
            second_half * cosine + first_half * sine_part,
        ],
        axis=-1,
    )


def sink_softmax(scores, key_mask, sink_col):
    masked = jnp.where(key_mask, scores, -1e30)
    row_top = jnp.maximum(jnp.max(masked, axis=-1, keepdims=True), sink_col)
    weights = jnp.where(key_mask, jnp.exp(masked - row_top), 0.0)
    denominator = jnp.sum(weights, axis=-1, keepdims=True) + jnp.exp(sink_col - row_top)
    return (weights / denominator).astype(BF16)


def attend_block(query_rows, key_rows, value_rows, query_pos, key_pos, sink_col):
    scores = jnp.einsum(
        "qkgd,skd->kgqs", query_rows, key_rows, preferred_element_type=F32
    ) * HD ** (-0.5)
    distance = query_pos[:, None] - key_pos[None, :]
    key_mask = (distance >= 0) & (distance < WINDOW) & (key_pos >= 0)[None, :]
    weights = sink_softmax(scores, key_mask, sink_col)
    mixed_rows = jnp.einsum("kgqs,skd->qkgd", weights, value_rows, preferred_element_type=F32)
    return mixed_rows.astype(BF16).reshape(query_rows.shape[0], -1)


def dot32(a, b):
    return jnp.dot(a, b, preferred_element_type=F32)


def project_whole(tokens, gain_attn, query_weight, key_weight, value_weight, attn_sinks, out_weight):
    tok_dev = tokens.shape[0]
    full_rows = lax.all_gather(tokens, "exp", axis=1, tiled=True)
    normed = rms_norm(full_rows, gain_attn)
    pieces = lax.all_gather((query_weight, key_weight, value_weight), "ctx", axis=1, tiled=True)
    query_lin, key_lin, value_lin = tuple(dot32(normed, piece) for piece in pieces)
    heads_local = query_lin.shape[1] // HD
    kv_local = key_lin.shape[1] // HD
    group_size = heads_local // kv_local
    position_ids = lax.axis_index("ctx") * tok_dev + jnp.arange(tok_dev, dtype=jnp.int32)
    angles_pos = position_ids.astype(F32)
    query = rotary(query_lin.reshape(tok_dev, heads_local, HD), angles_pos).astype(BF16)
    keys_own = rotary(key_lin.reshape(tok_dev, kv_local, HD), angles_pos).astype(BF16)
    key_value = jnp.stack([keys_own.reshape(tok_dev, kv_local * HD), value_lin.astype(BF16)])
    n_ctx = lax.axis_size("ctx")
    previous = lax.ppermute(key_value, "ctx", [(i, i + 1) for i in range(n_ctx - 1)])
    context = jnp.concatenate([previous, key_value], axis=1)
    key_pos = position_ids[0] - WINDOW + jnp.arange(tok_dev + WINDOW, dtype=jnp.int32)
    attended = attend_block(
        query.reshape(tok_dev, kv_local, group_size, HD),
        context[0].reshape(-1, kv_local, HD),
        context[1].reshape(-1, kv_local, HD),
        position_ids,
        key_pos,
        attn_sinks.reshape(kv_local, group_size, 1, 1),
    )
    head_terms = dot32(attended, lax.all_gather(out_weight, "ctx", axis=1, tiled=True))
    attn_proj = lax.psum(head_terms.astype(BF16), "exp").astype(F32)
    return (full_rows.astype(F32) + attn_proj).astype(BF16).T


def dot_nt(a, b):
    return lax.dot_general(a, b, (((1,), (1,)), ((), ())), preferred_element_type=F32)


def turn(values, cosine, signed_sine):
    width = values.shape[1]
    half = HD // 2
    lane = lax.broadcasted_iota(jnp.int32, values.shape, 1) % HD
    partner = jnp.where(
        lane < half,
        pltpu.roll(values, width - half, 1),
        pltpu.roll(values, half, 1),
    )
    return values * cosine + partner * signed_sine


def qkv_kernel(count, *refs):
    blocks, refs = refs[:count], refs[count:]
    weight_ref, cos_ref, sin_ref, q_ref, key_value_ref, rows_ref, kv_ref = refs
    step = pl.program_id(0)
    width, rows = blocks[0].shape
    cols = weight_ref.shape[2]
    share = kv_ref.shape[2]

    @pl.when(step == 0)
    def _():
        for r in range(count):
            rows_ref[r * rows : (r + 1) * rows, :] = blocks[r][...].T

    for i in range(2):
        for tile in range(-(-width // cols)):
            at, lanes = width + 2 * share * tile, slice(tile * cols, (tile + 1) * cols)
            for part in range(2):
                kv_ref[part, 2 * step + i, :, lanes] = weight_ref[i, at + part * share : at + (part + 1) * share]

    weight = jnp.concatenate([weight_ref[0, :width], weight_ref[1, :width]], axis=1)
    query = dot32(rows_ref[...], weight)
    for r in range(count):
        for at in range(0, 2 * cols, cols):
            piece = query[r * rows : (r + 1) * rows, at : at + cols]
            q_ref[r, :, at : at + cols] = turn(piece, cos_ref[r], sin_ref[r]).astype(BF16)

    @pl.when(step == pl.num_programs(0) - 1)
    def _():
        both = kv_ref[...].reshape(2 * PLANE * share, kv_ref.shape[3])[:, :width]
        lines = dot_nt(rows_ref[...], both)
        half = PLANE * share
        for r in range(count):
            piece = lines[r * rows : (r + 1) * rows]
            key_value_ref[r, :, :half] = turn(piece[:, :half], cos_ref[r], sin_ref[r]).astype(BF16)
            key_value_ref[r, :, half:] = piece[:, half:].astype(BF16)


def project_blocks(blocks, weights, share, cosine, signed_sine):
    count = len(blocks)
    width, rows = blocks[0].shape
    cols = weights.shape[2]
    tiles = -(-width // cols)
    kv_cols = 2 * PLANE * share
    whole = lambda p: (0, 0, 0)
    return pl.pallas_call(
        functools.partial(qkv_kernel, count),
        grid=(PLANE // 2,),
        in_specs=[pl.BlockSpec((width, rows), lambda p: (0, 0))] * count
        + [
            pl.BlockSpec((2,) + weights.shape[1:], lambda p: (p, 0, 0)),
            pl.BlockSpec(cosine.shape, whole),
            pl.BlockSpec(signed_sine.shape, whole),
        ],
        out_specs=[
            pl.BlockSpec((count, rows, 2 * cols), lambda p: (0, 0, p)),
            pl.BlockSpec((count, rows, kv_cols), whole),
        ],
        out_shape=[
            jax.ShapeDtypeStruct((count, rows, PLANE * cols), BF16),
            jax.ShapeDtypeStruct((count, rows, kv_cols), BF16),
        ],
        scratch_shapes=[
            pltpu.VMEM((count * rows, width), BF16),
            pltpu.VMEM((2, PLANE, share, tiles * cols), BF16),
        ],
        compiler_params=pltpu.CompilerParams(vmem_limit_bytes=58 * 2**20),
        cost_estimate=pl.CostEstimate(
            flops=2 * count * rows * width * (PLANE * cols + kv_cols),
            bytes_accessed=2 * width * (PLANE * cols + kv_cols + count * rows),
            transcendentals=0,
        ),
    )(*blocks, weights, cosine, signed_sine)


def attend_kernel(
    r, place_ref, sinks_ref, queries_ref, key_values_ref, halos_ref, even_ref, odd_ref, out_ref, att_ref, total_ref
):
    q_ref, own_ref, previous_ref = queries_ref.at[r], key_values_ref.at[r], halos_ref.at[place_ref[1]]
    rows = q_ref.shape[0]
    pair = 2 * HD
    kv_heads = own_ref.shape[1] // pair
    kv_cols = kv_heads * HD
    pairs = q_ref.shape[1] // pair
    lane = lax.broadcasted_iota(jnp.int32, (rows, pair), 1)
    low = lane < HD

    def spread(values, head):
        moved = pltpu.roll(values.astype(F32), HD, 1)
        chunk = values.astype(F32)
        lower, upper = (chunk, moved) if head % 2 == 0 else (moved, chunk)
        zero = jnp.zeros_like(chunk)
        return jnp.concatenate(
            [jnp.where(low, lower, zero), jnp.where(low, zero, upper)], axis=0
        ).astype(BF16)

    def side(ref):
        tables = []
        for head in range(kv_heads):
            at = head // 2 * pair
            keys = spread(ref[:, at : at + pair], head)
            values = spread(ref[:, kv_cols + at : kv_cols + at + pair], head)
            tables.append((keys, values))
        return tables

    own, previous = side(own_ref), side(previous_ref)
    row = lax.broadcasted_iota(jnp.int32, (rows, rows), 0)
    col = lax.broadcasted_iota(jnp.int32, (rows, rows), 1)
    inside = col <= row
    shown = jnp.logical_or(inside, place_ref[0] == 0)
    scale = HD**-0.5
    for p in range(pairs):
        head = p * kv_heads // pairs
        chunk = q_ref[:, p * pair : (p + 1) * pair]
        scores_own = dot_nt(chunk, own[head][0])
        scores_previous = dot_nt(chunk, previous[head][0])
        probs_own, probs_previous = [], []
        for h in range(2):
            at = h * rows
            scores = jnp.where(
                inside, scores_own[:, at : at + rows], scores_previous[:, at : at + rows]
            ) * scale
            scores = jnp.where(shown, scores, -1e30)
            sink = sinks_ref[2 * p + h]
            top = jnp.maximum(jnp.max(scores, axis=1, keepdims=True), sink)
            weights = jnp.exp(scores - top)
            total = jnp.sum(weights, axis=1, keepdims=True) + jnp.exp(sink - top)
            probs = weights / total
            probs_own.append(jnp.where(inside, probs, 0.0).astype(BF16))
            probs_previous.append(jnp.where(inside, 0.0, probs).astype(BF16))
        mixed = dot32(jnp.concatenate(probs_own, axis=1), own[head][1])
        mixed = mixed + dot32(jnp.concatenate(probs_previous, axis=1), previous[head][1])
        att_ref[:, p * pair : (p + 1) * pair] = mixed.astype(BF16)

    half, groups, padded, depth = even_ref.shape
    cols = out_ref.shape[0] // (2 * half * groups)
    attended = att_ref[...]
    for side_at, weight_ref in enumerate((even_ref, odd_ref)):
        for i in range(half):
            terms = dot_nt(weight_ref[i].reshape(groups * padded, depth), attended)
            share = place_ref[2 + 2 * i + side_at]
            for g in range(groups):
                total_ref[g, share] = terms[g * padded : (g + 1) * padded]
    for g in range(groups):
        for p in range(2 * half):
            at = (g * 2 * half + p) * cols
            out_ref[at : at + cols, :] = total_ref[g, p, :cols, :]


def attend_and_project(r, place, sinks, queries, key_values, halos, even, odd, width):
    rows = queries.shape[1]
    half, groups, padded, depth = even.shape
    vmem = pl.BlockSpec(memory_space=pltpu.VMEM)
    smem = pl.BlockSpec(memory_space=pltpu.SMEM)
    return pl.pallas_call(
        functools.partial(attend_kernel, r),
        in_specs=[smem, smem] + [vmem] * 5,
        out_specs=vmem,
        out_shape=jax.ShapeDtypeStruct((width, rows), F32),
        scratch_shapes=[
            pltpu.VMEM((rows, depth), BF16),
            pltpu.VMEM((groups, 2 * half, padded, rows), F32),
        ],
        compiler_params=pltpu.CompilerParams(vmem_limit_bytes=40 * 2**20),
        cost_estimate=pl.CostEstimate(
            flops=2 * rows * depth * (width + 8 * rows),
            bytes_accessed=2 * (width * depth + 2 * width * rows),
            transcendentals=rows * rows * depth // HD,
        ),
    )(place, sinks, queries, key_values, halos, even, odd)


def project_planes(tokens, gain_attn, query_weight, key_weight, value_weight, attn_sinks, out_weight):
    tok_dev, width = tokens.shape
    n_ctx = lax.axis_size("ctx")
    n_z = n_ctx // PLANE
    index = lax.axis_index("ctx")
    z, j = index // PLANE, index % PLANE
    planes = [[PLANE * a + b for b in range(PLANE)] for a in range(n_z)]
    order = list(range(0, n_z, 2)) + list(range(1, n_z, 2))[::-1]
    place_of = [order.index(a) for a in range(n_z)]
    ring, places = jnp.array(order, jnp.int32), jnp.array(place_of, jnp.int32)

    def shift(block, steps):
        return lax.ppermute(block, "ctx", [(i, (i + steps * PLANE) % n_ctx) for i in range(n_ctx)])

    def pass_on(block):
        route = [
            (a * PLANE + b, order[place_of[a] - 1] * PLANE + b) for a in range(n_z) for b in range(PLANE)
        ]
        return lax.ppermute(block, "ctx", route)

    def behind(block):
        route = [(a * PLANE + b, a * PLANE + (b + 1) % PLANE) for a in range(n_z) for b in range(PLANE)]
        return lax.ppermute(block, "ctx", route)

    def swap(block, bits):
        return lax.ppermute(block, "ctx", [(i, i ^ bits) for i in range(n_ctx)])

    tokens_t = tokens.T
    blocks = [rms_norm_t(tokens_t, gain_attn)]

    lanes = query_weight.shape[1]
    share = key_weight.shape[1]
    tiles = -(-width // lanes)
    kv_rows = jnp.concatenate([key_weight.T, value_weight.T], axis=0)
    kv_rows = jnp.pad(kv_rows, ((0, 0), (0, tiles * lanes - width))).reshape(2 * share, tiles, lanes)
    packed = jnp.concatenate(
        [query_weight, kv_rows.transpose(1, 0, 2).reshape(tiles * 2 * share, lanes)], axis=0
    )
    weights = lax.all_gather(packed, "ctx", axis_index_groups=planes)

    cols = out_weight.shape[1]
    padded = -(-cols // 16) * 16
    group_rows = out_weight.shape[0] // n_z
    out_rows = jnp.pad(out_weight.T, ((0, padded - cols), (0, 0)))
    out_rows, blocks[0] = lax.optimization_barrier((out_rows, blocks[0]))
    blocks.append(pass_on(blocks[0]))
    out_groups = jnp.stack(jnp.split(out_rows, n_z, axis=1))
    pieces = [
        shift(lax.dynamic_index_in_dim(out_groups, (z + s) % n_z, 0, keepdims=False), s) if s
        else lax.dynamic_index_in_dim(out_groups, z, 0, keepdims=False)
        for s in range(n_z)
    ]
    ordered = jnp.stack(pieces[::-1] + pieces[:0:-1])
    out_mine = lax.dynamic_slice_in_dim(ordered, n_z - 1 - z, n_z, 0)
    out_mine, blocks[1] = lax.optimization_barrier((out_mine, blocks[1]))
    for _ in range(n_z - 2):
        blocks.append(pass_on(blocks[-1]))
    out_parts = [out_mine] + [swap(out_mine, bits) for bits in (2, 4, 6)]
    out_parts, blocks[-1] = lax.optimization_barrier((out_parts, blocks[-1]))
    out_half = jnp.stack(out_parts)
    out_other = swap(out_half, 1)

    heads = PLANE * query_weight.shape[1] // HD
    sinks = lax.dynamic_slice_in_dim(attn_sinks, z * heads, heads)
    own_rows = jnp.arange(tok_dev, dtype=jnp.int32)
    lane = jnp.arange(2 * HD, dtype=jnp.int32) % HD
    half = HD // 2
    inverse_freq = jnp.exp(-(2.0 * (lane % half).astype(F32) / HD) * math.log(ROPE_BASE))
    mine = places[z]
    block_z = ring[(mine + jnp.arange(n_z, dtype=jnp.int32)) % n_z]
    numbers = block_z * PLANE + j
    angles = (numbers[:, None] * tok_dev + own_rows[None, :]).astype(F32)[:, :, None] * inverse_freq
    signed_sine = jnp.where(lane < half, -jnp.sin(angles), jnp.sin(angles))
    queries, key_values = project_blocks(blocks, weights, share, jnp.cos(angles), signed_sine)
    halos = behind(key_values)
    below = (places[jnp.maximum(block_z - 1, 0)] - mine) % n_z
    previous_at = jnp.where(j == 0, below, jnp.arange(n_z, dtype=jnp.int32))

    relative = jnp.arange(PLANE, dtype=jnp.int32) ^ j
    partial_sums = []
    for r in list(range(1, n_z)) + [0]:
        first = (numbers[r] == 0).astype(jnp.int32)
        place = jnp.concatenate([jnp.stack([first, previous_at[r]]), relative])
        partial_sums.append(
            attend_and_project(
                r, place, sinks, queries, key_values, halos, out_half, out_other, width
            )
        )
    running = partial_sums[0].astype(BF16)
    for term in partial_sums[1:]:
        running = pass_on(running).astype(F32) + term
        if term is not partial_sums[-1]:
            running = running.astype(BF16)
    return (tokens_t.astype(F32) + running).astype(BF16)


def expert_kernel(tile, hidden, rows_ref, gate_ref, upper_ref, down_ref, out_ref, total_ref):
    step = pl.program_id(0)
    steps = pl.num_programs(0)

    def add(count, initial):
        rows = rows_ref[...]
        gate = dot32(rows, gate_ref[0, :, :count])
        upper = dot32(rows, upper_ref[0, :, :count])
        activation = (gate * jax.nn.sigmoid(1.702 * gate) * (upper + 1.0)).astype(BF16)
        terms = dot32(activation, down_ref[:count, :])
        total_ref[...] = terms if initial else total_ref[...] + terms

    last = hidden - (-(-hidden // tile) - 1) * tile

    @pl.when(step == 0)
    def _():
        add(tile, True)

    @pl.when(jnp.logical_and(step > 0, step < steps - 1))
    def _():
        add(tile, False)

    @pl.when(step == steps - 1)
    def _():
        add(last, False)
        out_ref[...] = total_ref[...].astype(BF16)


def run_expert(rows, gate_up, down):
    count, width = rows.shape
    hidden = down.shape[0]
    tile = 512 if hidden > 1024 else 256
    return pl.pallas_call(
        functools.partial(expert_kernel, tile, hidden),
        grid=(-(-hidden // tile),),
        in_specs=[
            pl.BlockSpec((count, width), lambda f: (0, 0)),
            pl.BlockSpec((1, width, tile), lambda f: (0, 0, f)),
            pl.BlockSpec((1, width, tile), lambda f: (1, 0, f)),
            pl.BlockSpec((tile, width), lambda f: (f, 0)),
        ],
        out_specs=pl.BlockSpec((count, width), lambda f: (0, 0)),
        out_shape=jax.ShapeDtypeStruct((count, width), BF16),
        scratch_shapes=[pltpu.VMEM((count, width), F32)],
        compiler_params=pltpu.CompilerParams(vmem_limit_bytes=52 * 2**20),
        cost_estimate=pl.CostEstimate(
            flops=6 * count * width * hidden,
            bytes_accessed=6 * width * hidden + 4 * count * width,
            transcendentals=count * hidden,
        ),
    )(rows, gate_up, gate_up, down)


def slot_chunks(capacity):
    first = min(8, capacity)
    return [first, capacity - first] if capacity > first else [first]


def dispatch_kernel(chosen_ref, normed_ref, out_ref):
    out_ref[...] = dot_nt(chosen_ref[...], normed_ref[...]).astype(BF16)


def dispatch(chosen, normed):
    total, rows = chosen.shape
    width = normed.shape[0]
    return pl.pallas_call(
        dispatch_kernel,
        out_shape=jax.ShapeDtypeStruct((total, width), BF16),
        compiler_params=pltpu.CompilerParams(vmem_limit_bytes=24 * 2**20),
        cost_estimate=pl.CostEstimate(
            flops=2 * total * rows * width, bytes_accessed=2 * width * (total + rows), transcendentals=0
        ),
    )(chosen, normed)


def routing(route_ids, combine, n_ctx, capacity):
    tok_dev = route_ids.shape[0]
    named = route_ids[:, :, None] == jnp.arange(n_ctx, dtype=jnp.int32)[None, None, :]
    member = jnp.any(named, axis=1)
    weight_of = jnp.sum(jnp.where(named, combine[:, :, None], 0.0), axis=1)
    rows = jnp.arange(tok_dev, dtype=jnp.int32)
    earlier = (rows[:, None] > rows[None, :]).astype(BF16)
    slot_of = dot32(earlier, member.astype(BF16)).astype(jnp.int32)
    slot_of = jnp.where(member, slot_of, -1).T
    weight_of = weight_of.T
    chunks = []
    first = 0
    for size in slot_chunks(capacity):
        slots = first + jnp.arange(size, dtype=jnp.int32)
        chosen = (slot_of[:, None, :] == slots[None, :, None]).reshape(n_ctx * size, tok_dev)
        scale = jnp.where(chosen, jnp.repeat(weight_of, size, axis=0), 0.0)
        high = scale.astype(BF16)
        low = (scale - high.astype(F32)).astype(BF16)
        chunks.append((size, chosen.astype(BF16), jnp.concatenate([high, low], axis=1)))
        first += size
    return chunks


def mix_experts(normed, chunks, gate_up, down):
    width, tok_dev = normed.shape
    n_ctx, n_exp = lax.axis_size("ctx"), lax.axis_size("exp")
    width_local = width // n_exp

    def tiles(rows, size):
        if size % 8 == 0 or size % 4:
            return rows.reshape(n_ctx, size, -1)
        return rows.reshape(n_ctx, size // 4, 4, -1)

    def exchange(parts):
        return lax.all_to_all(parts, "ctx", split_axis=0, concat_axis=0, tiled=True)

    def in_order(parts, earlier):
        return lax.optimization_barrier((parts, earlier))

    outgoing, received = [], []
    for size, chosen, _ in chunks:
        if outgoing:
            chosen, outgoing[-1] = in_order(chosen, outgoing[-1])
        outgoing.append(tiles(dispatch(chosen, normed), size))
    for parts in outgoing:
        if received:
            parts, received[-1] = in_order(parts, received[-1])
        received.append(exchange(parts))

    results = []
    for i, (size, _, _) in enumerate(chunks):
        if results:
            received[i], results[-1] = in_order(received[i], results[-1])
        rows_in = received[i].reshape(n_ctx * size, width)
        results.append(tiles(run_expert(rows_in, gate_up, down), size))

    answers = []
    for parts in results:
        if answers:
            parts, answers[-1] = in_order(parts, answers[-1])
        answers.append(exchange(parts))

    moe_out = jnp.zeros((width_local, tok_dev), F32)
    for (size, _, scale), answer in zip(chunks, answers):
        if n_exp > 1:
            answer = lax.psum_scatter(answer, "exp", scatter_dimension=answer.ndim - 1, tiled=True)
        terms = lax.dot_general(
            answer.reshape(n_ctx * size, width_local), scale, (((0,), (0,)), ((), ())),
            preferred_element_type=F32,
        )
        moe_out = moe_out + terms[:, :tok_dev] + terms[:, tok_dev:]
    return moe_out


def per_device(
    tokens,
    route_ids,
    combine,
    gain_attn,
    gain_moe,
    query_weight,
    key_weight,
    value_weight,
    attn_sinks,
    out_weight,
    gate_up_weight,
    down_weight,
):
    tok_dev, width_local = tokens.shape
    n_ctx = lax.axis_size("ctx")
    n_exp = lax.axis_size("exp")
    capacity = tok_dev * route_ids.shape[1] * 5 // (4 * n_ctx)
    chunks = routing(route_ids, combine, n_ctx, capacity)
    by_planes = n_exp == 1 and n_ctx % PLANE == 0 and n_ctx > PLANE
    project = project_planes if by_planes else project_whole
    residual = project(
        tokens, gain_attn, query_weight, key_weight, value_weight, attn_sinks, out_weight
    )
    width = residual.shape[0]
    normed_moe = rms_norm_t(residual, gain_moe)
    exp_index = lax.axis_index("exp")
    residual_local = lax.dynamic_slice_in_dim(residual, exp_index * width_local, width_local, 0)

    moe_out = mix_experts(normed_moe, chunks, gate_up_weight[0], down_weight[0])
    return (residual_local.astype(F32) + moe_out).astype(BF16).T


def solution(mesh):
    return jax.shard_map(
        per_device,
        mesh=mesh,
        in_specs=(
            P("ctx", "exp"),
            P("ctx", None),
            P("ctx", None),
            P(),
            P(),
            P(None, ("exp", "ctx")),
            P(None, ("exp", "ctx")),
            P(None, ("exp", "ctx")),
            P("exp"),
            P("exp", "ctx"),
            P("ctx", None, None, "exp"),
            P("ctx", "exp", None),
        ),
        out_specs=P("ctx", "exp"),
        check_vma=False,
    )
```

```python
import functools
import math

import jax
import jax.numpy as jnp
from jax import lax
from jax.experimental import pallas as pl
from jax.experimental.pallas import tpu as pltpu
from jax.sharding import PartitionSpec as P

HD = 64
WINDOW = 128
EPSILON = 1e-05
ROPE_BASE = 150000.0
PLANE = 8
BF16 = jnp.bfloat16
F32 = jnp.float32


def rms_norm(values, gain):
    wide = values.astype(F32)
    meansq = jnp.mean(wide * wide, axis=-1, keepdims=True)
    return (wide * lax.rsqrt(meansq + EPSILON) * gain).astype(BF16)


def rms_norm_t(values, gain):
    wide = values.astype(F32)
    meansq = jnp.mean(wide * wide, axis=0, keepdims=True)
    return (wide * lax.rsqrt(meansq + EPSILON) * gain[:, None]).astype(BF16)


def rotary(values, angles_pos):
    half_dim = values.shape[-1] // 2
    inverse_freq = jnp.exp(
        -(2.0 * jnp.arange(half_dim, dtype=F32) / values.shape[-1]) * math.log(ROPE_BASE)
    )
    angles = angles_pos[:, None] * inverse_freq[None, :]
    cosine = jnp.cos(angles)[:, None, :]
    sine_part = jnp.sin(angles)[:, None, :]
    first_half = values[..., :half_dim]
    second_half = values[..., half_dim:]
    return jnp.concatenate(
        [
            first_half * cosine - second_half * sine_part,
            second_half * cosine + first_half * sine_part,
        ],
        axis=-1,
    )


def sink_softmax(scores, key_mask, sink_col):
    masked = jnp.where(key_mask, scores, -1e30)
    row_top = jnp.maximum(jnp.max(masked, axis=-1, keepdims=True), sink_col)
    weights = jnp.where(key_mask, jnp.exp(masked - row_top), 0.0)
    denominator = jnp.sum(weights, axis=-1, keepdims=True) + jnp.exp(sink_col - row_top)
    return (weights / denominator).astype(BF16)


def attend_block(query_rows, key_rows, value_rows, query_pos, key_pos, sink_col):
    scores = jnp.einsum(
        "qkgd,skd->kgqs", query_rows, key_rows, preferred_element_type=F32
    ) * HD ** (-0.5)
    distance = query_pos[:, None] - key_pos[None, :]
    key_mask = (distance >= 0) & (distance < WINDOW) & (key_pos >= 0)[None, :]
    weights = sink_softmax(scores, key_mask, sink_col)
    mixed_rows = jnp.einsum("kgqs,skd->qkgd", weights, value_rows, preferred_element_type=F32)
    return mixed_rows.astype(BF16).reshape(query_rows.shape[0], -1)


def dot32(a, b):
    return jnp.dot(a, b, preferred_element_type=F32)


def project_whole(
    tokens, gain_attn, query_weight, key_weight, value_weight, attn_sinks, out_weight, early
):
    tok_dev = tokens.shape[0]
    full_rows = lax.all_gather(tokens, "exp", axis=1, tiled=True)
    normed = rms_norm(full_rows, gain_attn)
    pieces = lax.all_gather((query_weight, key_weight, value_weight), "ctx", axis=1, tiled=True)
    query_lin, key_lin, value_lin = tuple(dot32(normed, piece) for piece in pieces)
    heads_local = query_lin.shape[1] // HD
    kv_local = key_lin.shape[1] // HD
    group_size = heads_local // kv_local
    position_ids = lax.axis_index("ctx") * tok_dev + jnp.arange(tok_dev, dtype=jnp.int32)
    angles_pos = position_ids.astype(F32)
    query = rotary(query_lin.reshape(tok_dev, heads_local, HD), angles_pos).astype(BF16)
    keys_own = rotary(key_lin.reshape(tok_dev, kv_local, HD), angles_pos).astype(BF16)
    key_value = jnp.stack([keys_own.reshape(tok_dev, kv_local * HD), value_lin.astype(BF16)])
    n_ctx = lax.axis_size("ctx")
    previous = lax.ppermute(key_value, "ctx", [(i, i + 1) for i in range(n_ctx - 1)])
    context = jnp.concatenate([previous, key_value], axis=1)
    key_pos = position_ids[0] - WINDOW + jnp.arange(tok_dev + WINDOW, dtype=jnp.int32)
    attended = attend_block(
        query.reshape(tok_dev, kv_local, group_size, HD),
        context[0].reshape(-1, kv_local, HD),
        context[1].reshape(-1, kv_local, HD),
        position_ids,
        key_pos,
        attn_sinks.reshape(kv_local, group_size, 1, 1),
    )
    head_terms = dot32(attended, lax.all_gather(out_weight, "ctx", axis=1, tiled=True))
    attn_proj = lax.psum(head_terms.astype(BF16), "exp").astype(F32)
    return (full_rows.astype(F32) + attn_proj).astype(BF16).T, early


def dot_nt(a, b):
    return lax.dot_general(a, b, (((1,), (1,)), ((), ())), preferred_element_type=F32)


def turn(values, cosine, signed_sine):
    width = values.shape[1]
    half = HD // 2
    lane = lax.broadcasted_iota(jnp.int32, values.shape, 1) % HD
    partner = jnp.where(
        lane < half,
        pltpu.roll(values, width - half, 1),
        pltpu.roll(values, half, 1),
    )
    return values * cosine + partner * signed_sine


def qkv_kernel(count, *refs):
    blocks, refs = refs[:count], refs[count:]
    weight_ref, cos_ref, sin_ref, q_ref, key_value_ref, rows_ref, kv_ref = refs
    step = pl.program_id(0)
    width, rows = blocks[0].shape
    cols = weight_ref.shape[2]
    share = kv_ref.shape[2]

    @pl.when(step == 0)
    def _():
        for r in range(count):
            rows_ref[r * rows : (r + 1) * rows, :] = blocks[r][...].T

    for i in range(2):
        for tile in range(-(-width // cols)):
            at, lanes = width + 2 * share * tile, slice(tile * cols, (tile + 1) * cols)
            for part in range(2):
                kv_ref[part, 2 * step + i, :, lanes] = weight_ref[i, at + part * share : at + (part + 1) * share]

    weight = jnp.concatenate([weight_ref[0, :width], weight_ref[1, :width]], axis=1)
    query = dot32(rows_ref[...], weight)
    for r in range(count):
        for at in range(0, 2 * cols, cols):
            piece = query[r * rows : (r + 1) * rows, at : at + cols]
            q_ref[r, :, at : at + cols] = turn(piece, cos_ref[r], sin_ref[r]).astype(BF16)

    @pl.when(step == pl.num_programs(0) - 1)
    def _():
        both = kv_ref[...].reshape(2 * PLANE * share, kv_ref.shape[3])[:, :width]
        lines = dot_nt(rows_ref[...], both)
        half = PLANE * share
        for r in range(count):
            piece = lines[r * rows : (r + 1) * rows]
            key_value_ref[r, :, :half] = turn(piece[:, :half], cos_ref[r], sin_ref[r]).astype(BF16)
            key_value_ref[r, :, half:] = piece[:, half:].astype(BF16)


def project_blocks(blocks, weights, share, cosine, signed_sine):
    count = len(blocks)
    width, rows = blocks[0].shape
    cols = weights.shape[2]
    tiles = -(-width // cols)
    kv_cols = 2 * PLANE * share
    whole = lambda p: (0, 0, 0)
    return pl.pallas_call(
        functools.partial(qkv_kernel, count),
        grid=(PLANE // 2,),
        in_specs=[pl.BlockSpec((width, rows), lambda p: (0, 0))] * count
        + [
            pl.BlockSpec((2,) + weights.shape[1:], lambda p: (p, 0, 0)),
            pl.BlockSpec(cosine.shape, whole),
            pl.BlockSpec(signed_sine.shape, whole),
        ],
        out_specs=[
            pl.BlockSpec((count, rows, 2 * cols), lambda p: (0, 0, p)),
            pl.BlockSpec((count, rows, kv_cols), whole),
        ],
        out_shape=[
            jax.ShapeDtypeStruct((count, rows, PLANE * cols), BF16),
            jax.ShapeDtypeStruct((count, rows, kv_cols), BF16),
        ],
        scratch_shapes=[
            pltpu.VMEM((count * rows, width), BF16),
            pltpu.VMEM((2, PLANE, share, tiles * cols), BF16),
        ],
        compiler_params=pltpu.CompilerParams(vmem_limit_bytes=58 * 2**20),
        cost_estimate=pl.CostEstimate(
            flops=2 * count * rows * width * (PLANE * cols + kv_cols),
            bytes_accessed=2 * width * (PLANE * cols + kv_cols + count * rows),
            transcendentals=0,
        ),
    )(*blocks, weights, cosine, signed_sine)


def attend_kernel(
    numbers, place_ref, sinks_ref, queries_ref, key_values_ref, halos_ref, even_ref, odd_ref, out_ref, att_ref, total_ref
):
    count, rows = queries_ref.shape[:2]
    pair = 2 * HD
    kv_heads = key_values_ref.shape[2] // pair
    kv_cols = kv_heads * HD
    pairs = queries_ref.shape[2] // pair
    lane = lax.broadcasted_iota(jnp.int32, (rows, pair), 1)
    low = lane < HD

    def spread(values, head):
        moved = pltpu.roll(values.astype(F32), HD, 1)
        chunk = values.astype(F32)
        lower, upper = (chunk, moved) if head % 2 == 0 else (moved, chunk)
        zero = jnp.zeros_like(chunk)
        return jnp.concatenate(
            [jnp.where(low, lower, zero), jnp.where(low, zero, upper)], axis=0
        ).astype(BF16)

    def side(ref):
        tables = []
        for head in range(kv_heads):
            at = head // 2 * pair
            keys = spread(ref[:, at : at + pair], head)
            values = spread(ref[:, kv_cols + at : kv_cols + at + pair], head)
            tables.append((keys, values))
        return tables

    row = lax.broadcasted_iota(jnp.int32, (rows, rows), 0)
    col = lax.broadcasted_iota(jnp.int32, (rows, rows), 1)
    inside = col <= row
    scale = HD**-0.5
    for i, r in enumerate(numbers):
        own, previous = side(key_values_ref.at[r]), side(halos_ref.at[place_ref[count + r]])
        shown = jnp.logical_or(inside, place_ref[r] == 0)
        for p in range(pairs):
            head = p * kv_heads // pairs
            chunk = queries_ref[r, :, p * pair : (p + 1) * pair]
            scores_own = dot_nt(chunk, own[head][0])
            scores_previous = dot_nt(chunk, previous[head][0])
            probs_own, probs_previous = [], []
            for h in range(2):
                at = h * rows
                scores = jnp.where(
                    inside, scores_own[:, at : at + rows], scores_previous[:, at : at + rows]
                ) * scale
                scores = jnp.where(shown, scores, -1e30)
                sink = sinks_ref[2 * p + h]
                top = jnp.maximum(jnp.max(scores, axis=1, keepdims=True), sink)
                weights = jnp.exp(scores - top)
                total = jnp.sum(weights, axis=1, keepdims=True) + jnp.exp(sink - top)
                probs = weights / total
                probs_own.append(jnp.where(inside, probs, 0.0).astype(BF16))
                probs_previous.append(jnp.where(inside, 0.0, probs).astype(BF16))
            mixed = dot32(jnp.concatenate(probs_own, axis=1), own[head][1])
            mixed = mixed + dot32(jnp.concatenate(probs_previous, axis=1), previous[head][1])
            att_ref[i * rows : (i + 1) * rows, p * pair : (p + 1) * pair] = mixed.astype(BF16)

    half, groups, padded, depth = even_ref.shape
    cols = out_ref.shape[1] // (2 * half * groups)
    attended = att_ref[...]
    for side_at, weight_ref in enumerate((even_ref, odd_ref)):
        for i in range(half):
            terms = dot_nt(weight_ref[i].reshape(groups * padded, depth), attended)
            share = place_ref[2 * count + 2 * i + side_at]
            for g in range(groups):
                total_ref[g, share] = terms[g * padded : (g + 1) * padded]
    for g in range(groups):
        for p in range(2 * half):
            at = (g * 2 * half + p) * cols
            for i in range(len(numbers)):
                out_ref[i, at : at + cols, :] = total_ref[g, p, :cols, i * rows : (i + 1) * rows]


def attend_and_project(numbers, place, sinks, queries, key_values, halos, even, odd, width):
    rows = queries.shape[1]
    count = len(numbers)
    half, groups, padded, depth = even.shape
    vmem = pl.BlockSpec(memory_space=pltpu.VMEM)
    smem = pl.BlockSpec(memory_space=pltpu.SMEM)
    return pl.pallas_call(
        functools.partial(attend_kernel, numbers),
        in_specs=[smem, smem] + [vmem] * 5,
        out_specs=vmem,
        out_shape=jax.ShapeDtypeStruct((count, width, rows), F32),
        scratch_shapes=[
            pltpu.VMEM((count * rows, depth), BF16),
            pltpu.VMEM((groups, 2 * half, padded, count * rows), F32),
        ],
        compiler_params=pltpu.CompilerParams(vmem_limit_bytes=40 * 2**20),
        cost_estimate=pl.CostEstimate(
            flops=2 * count * rows * depth * (width + 8 * rows),
            bytes_accessed=2 * width * (depth + 2 * count * rows),
            transcendentals=count * rows * rows * depth // HD,
        ),
    )(place, sinks, queries, key_values, halos, even, odd)


def project_planes(
    tokens, gain_attn, query_weight, key_weight, value_weight, attn_sinks, out_weight, early
):
    tok_dev, width = tokens.shape
    n_ctx = lax.axis_size("ctx")
    n_z = n_ctx // PLANE
    index = lax.axis_index("ctx")
    z, j = index // PLANE, index % PLANE
    planes = [[PLANE * a + b for b in range(PLANE)] for a in range(n_z)]
    order = list(range(0, n_z, 2)) + list(range(1, n_z, 2))[::-1]
    place_of = [order.index(a) for a in range(n_z)]
    ring, places = jnp.array(order, jnp.int32), jnp.array(place_of, jnp.int32)

    def shift(block, steps):
        return lax.ppermute(block, "ctx", [(i, (i + steps * PLANE) % n_ctx) for i in range(n_ctx)])

    def pass_on(block):
        route = [
            (a * PLANE + b, order[place_of[a] - 1] * PLANE + b) for a in range(n_z) for b in range(PLANE)
        ]
        return lax.ppermute(block, "ctx", route)

    def behind(block):
        route = [(a * PLANE + b, a * PLANE + (b + 1) % PLANE) for a in range(n_z) for b in range(PLANE)]
        return lax.ppermute(block, "ctx", route)

    def swap(block, bits):
        return lax.ppermute(block, "ctx", [(i, i ^ bits) for i in range(n_ctx)])

    tokens_t = tokens.T
    blocks = [rms_norm_t(tokens_t, gain_attn)]

    lanes = query_weight.shape[1]
    share = key_weight.shape[1]
    tiles = -(-width // lanes)
    kv_rows = jnp.concatenate([key_weight.T, value_weight.T], axis=0)
    kv_rows = jnp.pad(kv_rows, ((0, 0), (0, tiles * lanes - width))).reshape(2 * share, tiles, lanes)
    packed = jnp.concatenate(
        [query_weight, kv_rows.transpose(1, 0, 2).reshape(tiles * 2 * share, lanes)], axis=0
    )
    weights = lax.all_gather(packed, "ctx", axis_index_groups=planes)

    cols = out_weight.shape[1]
    padded = -(-cols // 16) * 16
    group_rows = out_weight.shape[0] // n_z
    out_rows = jnp.pad(out_weight.T, ((0, padded - cols), (0, 0)))
    out_rows, blocks[0] = lax.optimization_barrier((out_rows, blocks[0]))
    blocks.append(pass_on(blocks[0]))
    out_groups = jnp.stack(jnp.split(out_rows, n_z, axis=1))
    pieces = [
        shift(lax.dynamic_index_in_dim(out_groups, (z + s) % n_z, 0, keepdims=False), s) if s
        else lax.dynamic_index_in_dim(out_groups, z, 0, keepdims=False)
        for s in range(n_z)
    ]
    ordered = jnp.stack(pieces[::-1] + pieces[:0:-1])
    out_mine = lax.dynamic_slice_in_dim(ordered, n_z - 1 - z, n_z, 0)
    heads = PLANE * query_weight.shape[1] // HD
    sinks = lax.dynamic_slice_in_dim(attn_sinks, z * heads, heads)
    own_rows = jnp.arange(tok_dev, dtype=jnp.int32)
    lane = jnp.arange(2 * HD, dtype=jnp.int32) % HD
    half = HD // 2
    inverse_freq = jnp.exp(-(2.0 * (lane % half).astype(F32) / HD) * math.log(ROPE_BASE))
    mine = places[z]
    block_z = ring[(mine + jnp.arange(n_z, dtype=jnp.int32)) % n_z]
    numbers = block_z * PLANE + j
    angles = (numbers[:, None] * tok_dev + own_rows[None, :]).astype(F32)[:, :, None] * inverse_freq
    signed_sine = jnp.where(lane < half, -jnp.sin(angles), jnp.sin(angles))
    cosine = jnp.cos(angles)
    below = (places[jnp.maximum(block_z - 1, 0)] - mine) % n_z
    previous_at = jnp.where(j == 0, below, jnp.arange(n_z, dtype=jnp.int32))
    relative = jnp.arange(PLANE, dtype=jnp.int32) ^ j
    place = jnp.concatenate([(numbers == 0).astype(jnp.int32), previous_at, relative])
    (out_mine, blocks[1], cosine, signed_sine, place, sinks, early) = lax.optimization_barrier(
        (out_mine, blocks[1], cosine, signed_sine, place, sinks, early)
    )
    for _ in range(n_z - 2):
        blocks.append(pass_on(blocks[-1]))
    out_parts = [out_mine] + [swap(out_mine, bits) for bits in (2, 4, 6)]
    out_parts, blocks[-1] = lax.optimization_barrier((out_parts, blocks[-1]))
    out_half = jnp.stack(out_parts)
    out_other = swap(out_half, 1)
    queries, key_values = project_blocks(blocks, weights, share, cosine, signed_sine)
    halos = behind(key_values)

    def parts_of(numbers):
        return attend_and_project(
            numbers, place, sinks, queries, key_values, halos, out_half, out_other, width
        )

    running = parts_of((1,))[0].astype(BF16)
    others = parts_of(tuple(range(2, n_z)) + (0,))
    for i in range(n_z - 2):
        running = (pass_on(running).astype(F32) + others[i]).astype(BF16)
    total = pass_on(running).astype(F32) + others[n_z - 2]
    return (tokens_t.astype(F32) + total).astype(BF16), early


def expert_kernel(tile, hidden, rows_ref, gate_ref, upper_ref, down_ref, out_ref, total_ref):
    step = pl.program_id(0)
    steps = pl.num_programs(0)

    def add(count, initial):
        rows = rows_ref[...]
        gate = dot32(rows, gate_ref[0, :, :count])
        upper = dot32(rows, upper_ref[0, :, :count])
        activation = (gate * jax.nn.sigmoid(1.702 * gate) * (upper + 1.0)).astype(BF16)
        terms = dot32(activation, down_ref[:count, :])
        total_ref[...] = terms if initial else total_ref[...] + terms

    last = hidden - (-(-hidden // tile) - 1) * tile

    @pl.when(step == 0)
    def _():
        add(tile, True)

    @pl.when(jnp.logical_and(step > 0, step < steps - 1))
    def _():
        add(tile, False)

    @pl.when(step == steps - 1)
    def _():
        add(last, False)
        out_ref[...] = total_ref[...].astype(BF16)


def run_expert(rows, gate_up, down):
    count, width = rows.shape
    hidden = down.shape[0]
    tile = 512 if hidden > 1024 else 256
    return pl.pallas_call(
        functools.partial(expert_kernel, tile, hidden),
        grid=(-(-hidden // tile),),
        in_specs=[
            pl.BlockSpec((count, width), lambda f: (0, 0)),
            pl.BlockSpec((1, width, tile), lambda f: (0, 0, f)),
            pl.BlockSpec((1, width, tile), lambda f: (1, 0, f)),
            pl.BlockSpec((tile, width), lambda f: (f, 0)),
        ],
        out_specs=pl.BlockSpec((count, width), lambda f: (0, 0)),
        out_shape=jax.ShapeDtypeStruct((count, width), BF16),
        scratch_shapes=[pltpu.VMEM((count, width), F32)],
        compiler_params=pltpu.CompilerParams(vmem_limit_bytes=52 * 2**20),
        cost_estimate=pl.CostEstimate(
            flops=6 * count * width * hidden,
            bytes_accessed=6 * width * hidden + 4 * count * width,
            transcendentals=count * hidden,
        ),
    )(rows, gate_up, gate_up, down)


def slot_chunks(capacity):
    return [min(8, capacity - first) for first in range(0, capacity, 8)]


def dispatch_kernel(chosen_ref, normed_ref, out_ref):
    out_ref[...] = dot_nt(chosen_ref[...], normed_ref[...]).astype(BF16)


def dispatch(chosen, normed):
    total, rows = chosen.shape
    width = normed.shape[0]
    return pl.pallas_call(
        dispatch_kernel,
        out_shape=jax.ShapeDtypeStruct((total, width), BF16),
        compiler_params=pltpu.CompilerParams(vmem_limit_bytes=24 * 2**20),
        cost_estimate=pl.CostEstimate(
            flops=2 * total * rows * width, bytes_accessed=2 * width * (total + rows), transcendentals=0
        ),
    )(chosen, normed)


def routing(route_ids, combine, n_ctx, sizes):
    tok_dev = route_ids.shape[0]
    named = route_ids[:, :, None] == jnp.arange(n_ctx, dtype=jnp.int32)[None, None, :]
    member = jnp.any(named, axis=1)
    weight_of = jnp.sum(jnp.where(named, combine[:, :, None], 0.0), axis=1)
    rows = jnp.arange(tok_dev, dtype=jnp.int32)
    earlier = (rows[:, None] > rows[None, :]).astype(BF16)
    slot_of = dot32(earlier, member.astype(BF16)).astype(jnp.int32)
    slot_of = jnp.where(member, slot_of, -1).T
    weight_of = weight_of.T
    chunks = []
    first = 0
    for size in sizes:
        slots = first + jnp.arange(size, dtype=jnp.int32)
        chosen = (slot_of[:, None, :] == slots[None, :, None]).reshape(n_ctx * size, tok_dev)
        scale = jnp.where(chosen, jnp.repeat(weight_of, size, axis=0), 0.0)
        high = scale.astype(BF16)
        low = (scale - high.astype(F32)).astype(BF16)
        chunks.append((chosen.astype(BF16), jnp.concatenate([high, low], axis=1)))
        first += size
    return chunks


def mix_experts(normed, sizes, matrices, gate_up, down):
    width, tok_dev = normed.shape
    n_ctx, n_exp = lax.axis_size("ctx"), lax.axis_size("exp")
    width_local = width // n_exp

    def tiles(rows, size):
        if size % 8 == 0 or size % 4:
            return rows.reshape(n_ctx, size, -1)
        return rows.reshape(n_ctx, size // 4, 4, -1)

    def exchange(parts):
        return lax.all_to_all(parts, "ctx", split_axis=0, concat_axis=0, tiled=True)

    def in_order(parts, earlier):
        return lax.optimization_barrier((parts, earlier))

    outgoing, received = [], []
    for size, (chosen, _) in zip(sizes, matrices):
        if outgoing:
            chosen, outgoing[-1] = in_order(chosen, outgoing[-1])
        outgoing.append(tiles(dispatch(chosen, normed), size))
    for parts in outgoing:
        if received:
            parts, received[-1] = in_order(parts, received[-1])
        received.append(exchange(parts))

    results = []
    for i, size in enumerate(sizes):
        if i > 1 and i == len(sizes) - 1:
            received[i], results[0] = in_order(received[i], results[0])
        if results:
            received[i], results[-1] = in_order(received[i], results[-1])
        rows_in = received[i].reshape(n_ctx * size, width)
        results.append(tiles(run_expert(rows_in, gate_up, down), size))

    answers = []
    for parts in results:
        if answers:
            parts, answers[-1] = in_order(parts, answers[-1])
        answers.append(exchange(parts))

    moe_out = jnp.zeros((width_local, tok_dev), F32)
    for size, (_, scale), answer in zip(sizes, matrices, answers):
        if n_exp > 1:
            answer = lax.psum_scatter(answer, "exp", scatter_dimension=answer.ndim - 1, tiled=True)
        terms = lax.dot_general(
            answer.reshape(n_ctx * size, width_local), scale, (((0,), (0,)), ((), ())),
            preferred_element_type=F32,
        )
        moe_out = moe_out + terms[:, :tok_dev] + terms[:, tok_dev:]
    return moe_out


def per_device(
    tokens,
    route_ids,
    combine,
    gain_attn,
    gain_moe,
    query_weight,
    key_weight,
    value_weight,
    attn_sinks,
    out_weight,
    gate_up_weight,
    down_weight,
):
    tok_dev, width_local = tokens.shape
    n_ctx = lax.axis_size("ctx")
    n_exp = lax.axis_size("exp")
    capacity = tok_dev * route_ids.shape[1] * 5 // (4 * n_ctx)
    sizes = slot_chunks(capacity)
    matrices = routing(route_ids, combine, n_ctx, sizes)
    by_planes = n_exp == 1 and n_ctx % PLANE == 0 and n_ctx > PLANE
    project = project_planes if by_planes else project_whole
    residual, matrices = project(
        tokens, gain_attn, query_weight, key_weight, value_weight, attn_sinks, out_weight, matrices
    )
    width = residual.shape[0]
    normed_moe = rms_norm_t(residual, gain_moe)
    exp_index = lax.axis_index("exp")
    residual_local = lax.dynamic_slice_in_dim(residual, exp_index * width_local, width_local, 0)

    moe_out = mix_experts(normed_moe, sizes, matrices, gate_up_weight[0], down_weight[0])
    return (residual_local.astype(F32) + moe_out).astype(BF16).T


def solution(mesh):
    return jax.shard_map(
        per_device,
        mesh=mesh,
        in_specs=(
            P("ctx", "exp"),
            P("ctx", None),
            P("ctx", None),
            P(),
            P(),
            P(None, ("exp", "ctx")),
            P(None, ("exp", "ctx")),
            P(None, ("exp", "ctx")),
            P("exp"),
            P("exp", "ctx"),
            P("ctx", None, None, "exp"),
            P("ctx", "exp", None),
        ),
        out_specs=P("ctx", "exp"),
        check_vma=False,
    )
```

```python
import functools
import math

import jax
import jax.numpy as jnp
from jax import lax
from jax.experimental import pallas as pl
from jax.experimental.pallas import tpu as pltpu
from jax.sharding import PartitionSpec as P

HD = 64
WINDOW = 128
EPSILON = 1e-05
ROPE_BASE = 150000.0
PLANE = 8
BF16 = jnp.bfloat16
F32 = jnp.float32


def rms_norm(values, gain):
    wide = values.astype(F32)
    meansq = jnp.mean(wide * wide, axis=-1, keepdims=True)
    return (wide * lax.rsqrt(meansq + EPSILON) * gain).astype(BF16)


def rms_norm_t(values, gain):
    wide = values.astype(F32)
    meansq = jnp.mean(wide * wide, axis=0, keepdims=True)
    return (wide * lax.rsqrt(meansq + EPSILON) * gain[:, None]).astype(BF16)


def rotary(values, angles_pos):
    half_dim = values.shape[-1] // 2
    inverse_freq = jnp.exp(
        -(2.0 * jnp.arange(half_dim, dtype=F32) / values.shape[-1]) * math.log(ROPE_BASE)
    )
    angles = angles_pos[:, None] * inverse_freq[None, :]
    cosine = jnp.cos(angles)[:, None, :]
    sine_part = jnp.sin(angles)[:, None, :]
    first_half = values[..., :half_dim]
    second_half = values[..., half_dim:]
    return jnp.concatenate(
        [
            first_half * cosine - second_half * sine_part,
            second_half * cosine + first_half * sine_part,
        ],
        axis=-1,
    )


def sink_softmax(scores, key_mask, sink_col):
    masked = jnp.where(key_mask, scores, -1e30)
    row_top = jnp.maximum(jnp.max(masked, axis=-1, keepdims=True), sink_col)
    weights = jnp.where(key_mask, jnp.exp(masked - row_top), 0.0)
    denominator = jnp.sum(weights, axis=-1, keepdims=True) + jnp.exp(sink_col - row_top)
    return (weights / denominator).astype(BF16)


def attend_block(query_rows, key_rows, value_rows, query_pos, key_pos, sink_col):
    scores = jnp.einsum(
        "qkgd,skd->kgqs", query_rows, key_rows, preferred_element_type=F32
    ) * HD ** (-0.5)
    distance = query_pos[:, None] - key_pos[None, :]
    key_mask = (distance >= 0) & (distance < WINDOW) & (key_pos >= 0)[None, :]
    weights = sink_softmax(scores, key_mask, sink_col)
    mixed_rows = jnp.einsum("kgqs,skd->qkgd", weights, value_rows, preferred_element_type=F32)
    return mixed_rows.astype(BF16).reshape(query_rows.shape[0], -1)


def dot32(a, b):
    return jnp.dot(a, b, preferred_element_type=F32)


def project_whole(
    tokens, gain_attn, query_weight, key_weight, value_weight, attn_sinks, out_weight, early
):
    tok_dev = tokens.shape[0]
    full_rows = lax.all_gather(tokens, "exp", axis=1, tiled=True)
    normed = rms_norm(full_rows, gain_attn)
    pieces = lax.all_gather((query_weight, key_weight, value_weight), "ctx", axis=1, tiled=True)
    query_lin, key_lin, value_lin = tuple(dot32(normed, piece) for piece in pieces)
    heads_local = query_lin.shape[1] // HD
    kv_local = key_lin.shape[1] // HD
    group_size = heads_local // kv_local
    position_ids = lax.axis_index("ctx") * tok_dev + jnp.arange(tok_dev, dtype=jnp.int32)
    angles_pos = position_ids.astype(F32)
    query = rotary(query_lin.reshape(tok_dev, heads_local, HD), angles_pos).astype(BF16)
    keys_own = rotary(key_lin.reshape(tok_dev, kv_local, HD), angles_pos).astype(BF16)
    key_value = jnp.stack([keys_own.reshape(tok_dev, kv_local * HD), value_lin.astype(BF16)])
    n_ctx = lax.axis_size("ctx")
    previous = lax.ppermute(key_value, "ctx", [(i, i + 1) for i in range(n_ctx - 1)])
    context = jnp.concatenate([previous, key_value], axis=1)
    key_pos = position_ids[0] - WINDOW + jnp.arange(tok_dev + WINDOW, dtype=jnp.int32)
    attended = attend_block(
        query.reshape(tok_dev, kv_local, group_size, HD),
        context[0].reshape(-1, kv_local, HD),
        context[1].reshape(-1, kv_local, HD),
        position_ids,
        key_pos,
        attn_sinks.reshape(kv_local, group_size, 1, 1),
    )
    head_terms = dot32(attended, lax.all_gather(out_weight, "ctx", axis=1, tiled=True))
    attn_proj = lax.psum(head_terms.astype(BF16), "exp").astype(F32)
    return (full_rows.astype(F32) + attn_proj).astype(BF16).T, early


def dot_nt(a, b):
    return lax.dot_general(a, b, (((1,), (1,)), ((), ())), preferred_element_type=F32)


def turn(values, cosine, signed_sine):
    width = values.shape[1]
    half = HD // 2
    lane = lax.broadcasted_iota(jnp.int32, values.shape, 1) % HD
    partner = jnp.where(
        lane < half,
        pltpu.roll(values, width - half, 1),
        pltpu.roll(values, half, 1),
    )
    return values * cosine + partner * signed_sine


def qkv_kernel(count, place_ref, *refs):
    blocks, shares, refs = refs[:count], refs[count : count + PLANE], refs[count + PLANE :]
    cos_ref, sin_ref, q_ref, key_value_ref, rows_ref, kv_ref = refs
    width, rows = blocks[0].shape
    cols = shares[0].shape[1]
    share = kv_ref.shape[2]
    for r in range(count):
        rows_ref[r * rows : (r + 1) * rows, :] = blocks[r][...].T

    for i in range(PLANE):
        for tile in range(-(-width // cols)):
            at, lanes = width + 2 * share * tile, slice(tile * cols, (tile + 1) * cols)
            for part in range(2):
                kv_ref[part, place_ref[i], :, lanes] = shares[i][at + part * share : at + (part + 1) * share]
    both = kv_ref[...].reshape(2 * PLANE * share, kv_ref.shape[3])[:, :width]
    lines = dot_nt(rows_ref[...], both)
    half = PLANE * share
    for r in range(count):
        piece = lines[r * rows : (r + 1) * rows]
        key_value_ref[r, :, :half] = turn(piece[:, :half], cos_ref[r], sin_ref[r]).astype(BF16)
        key_value_ref[r, :, half:] = piece[:, half:].astype(BF16)

    for i in range(0, PLANE, 2):
        weight = jnp.concatenate([shares[i][:width], shares[i + 1][:width]], axis=1)
        query = dot32(rows_ref[...], weight)
        for k in range(2):
            lanes = pl.ds(pl.multiple_of(place_ref[i + k] * cols, cols), cols)
            for r in range(count):
                piece = query[r * rows : (r + 1) * rows, k * cols : (k + 1) * cols]
                q_ref[r, :, lanes] = turn(piece, cos_ref[r], sin_ref[r]).astype(BF16)


def project_blocks(place, blocks, shares, share, cosine, signed_sine):
    count = len(blocks)
    width, rows = blocks[0].shape
    cols = shares[0].shape[1]
    tiles = -(-width // cols)
    kv_cols = 2 * PLANE * share
    vmem = pl.BlockSpec(memory_space=pltpu.VMEM)
    return pl.pallas_call(
        functools.partial(qkv_kernel, count),
        in_specs=[pl.BlockSpec(memory_space=pltpu.SMEM)] + [vmem] * (count + PLANE + 2),
        out_specs=[vmem, vmem],
        out_shape=[
            jax.ShapeDtypeStruct((count, rows, PLANE * cols), BF16),
            jax.ShapeDtypeStruct((count, rows, kv_cols), BF16),
        ],
        scratch_shapes=[
            pltpu.VMEM((count * rows, width), BF16),
            pltpu.VMEM((2, PLANE, share, tiles * cols), BF16),
        ],
        compiler_params=pltpu.CompilerParams(vmem_limit_bytes=40 * 2**20),
        cost_estimate=pl.CostEstimate(
            flops=2 * count * rows * width * (PLANE * cols + kv_cols),
            bytes_accessed=2 * width * (PLANE * cols + kv_cols + count * rows),
            transcendentals=0,
        ),
    )(place, *blocks, *shares, cosine, signed_sine)


def attend_kernel(
    numbers, place_ref, sinks_ref, first_ref, last_ref, key_values_ref, halos_ref, weight_ref, out_ref, att_ref
):
    count, rows = key_values_ref.shape[:2]
    pair = 2 * HD
    kv_heads = key_values_ref.shape[2] // pair
    kv_cols = kv_heads * HD
    pairs = first_ref.shape[2] // pair
    lane = lax.broadcasted_iota(jnp.int32, (rows, pair), 1)
    low = lane < HD

    def spread(values, head):
        moved = pltpu.roll(values.astype(F32), HD, 1)
        chunk = values.astype(F32)
        lower, upper = (chunk, moved) if head % 2 == 0 else (moved, chunk)
        zero = jnp.zeros_like(chunk)
        return jnp.concatenate(
            [jnp.where(low, lower, zero), jnp.where(low, zero, upper)], axis=0
        ).astype(BF16)

    def side(ref):
        tables = []
        for head in range(kv_heads):
            at = head // 2 * pair
            keys = spread(ref[:, at : at + pair], head)
            values = spread(ref[:, kv_cols + at : kv_cols + at + pair], head)
            tables.append((keys, values))
        return tables

    row = lax.broadcasted_iota(jnp.int32, (rows, rows), 0)
    col = lax.broadcasted_iota(jnp.int32, (rows, rows), 1)
    inside = col <= row
    scale = HD**-0.5
    for i, r in enumerate(numbers):
        queries_ref, at = (first_ref, r) if r < first_ref.shape[0] else (last_ref, r - first_ref.shape[0])
        own, previous = side(key_values_ref.at[r]), side(halos_ref.at[place_ref[count + r]])
        shown = jnp.logical_or(inside, place_ref[r] == 0)
        for p in range(pairs):
            head = p * kv_heads // pairs
            chunk = queries_ref[at, :, p * pair : (p + 1) * pair]
            scores_own = dot_nt(chunk, own[head][0])
            scores_previous = dot_nt(chunk, previous[head][0])
            probs_own, probs_previous = [], []
            for h in range(2):
                half = slice(h * rows, (h + 1) * rows)
                scores = jnp.where(inside, scores_own[:, half], scores_previous[:, half]) * scale
                scores = jnp.where(shown, scores, -1e30)
                sink = sinks_ref[2 * p + h]
                top = jnp.maximum(jnp.max(scores, axis=1, keepdims=True), sink)
                weights = jnp.exp(scores - top)
                total = jnp.sum(weights, axis=1, keepdims=True) + jnp.exp(sink - top)
                probs = weights / total
                probs_own.append(jnp.where(inside, probs, 0.0).astype(BF16))
                probs_previous.append(jnp.where(inside, 0.0, probs).astype(BF16))
            mixed = dot32(jnp.concatenate(probs_own, axis=1), own[head][1])
            mixed = mixed + dot32(jnp.concatenate(probs_previous, axis=1), previous[head][1])
            att_ref[i * rows : (i + 1) * rows, p * pair : (p + 1) * pair] = mixed.astype(BF16)

    shares, groups, padded, depth = weight_ref.shape
    cols = out_ref.shape[1] // (shares * groups)
    attended = att_ref[...]
    for p in range(shares):
        terms = dot_nt(weight_ref[p].reshape(groups * padded, depth), attended)
        for g in range(groups):
            at = (g * shares + p) * cols
            for i in range(len(numbers)):
                out_ref[i, at : at + cols, :] = terms[g * padded : g * padded + cols, i * rows : (i + 1) * rows]


def attend_and_project(numbers, place, sinks, first, last, key_values, halos, weight, width):
    rows = first.shape[1]
    count = len(numbers)
    depth = weight.shape[3]
    vmem = pl.BlockSpec(memory_space=pltpu.VMEM)
    smem = pl.BlockSpec(memory_space=pltpu.SMEM)
    return pl.pallas_call(
        functools.partial(attend_kernel, numbers),
        in_specs=[smem, smem] + [vmem] * 5,
        out_specs=vmem,
        out_shape=jax.ShapeDtypeStruct((count, width, rows), F32),
        scratch_shapes=[pltpu.VMEM((count * rows, depth), BF16)],
        compiler_params=pltpu.CompilerParams(vmem_limit_bytes=40 * 2**20),
        cost_estimate=pl.CostEstimate(
            flops=2 * count * rows * depth * (width + 8 * rows),
            bytes_accessed=2 * width * (depth + 2 * count * rows),
            transcendentals=count * rows * rows * depth // HD,
        ),
    )(place, sinks, first, last, key_values, halos, weight)


def project_planes(
    tokens, gain_attn, query_weight, key_weight, value_weight, attn_sinks, out_weight, early
):
    tok_dev, width = tokens.shape
    n_ctx = lax.axis_size("ctx")
    n_z = n_ctx // PLANE
    index = lax.axis_index("ctx")
    z, j = index // PLANE, index % PLANE
    planes = [[PLANE * a + b for b in range(PLANE)] for a in range(n_z)]
    order = list(range(0, n_z, 2)) + list(range(1, n_z, 2))[::-1]
    place_of = [order.index(a) for a in range(n_z)]
    ring, places = jnp.array(order, jnp.int32), jnp.array(place_of, jnp.int32)

    def shift(block, steps):
        return lax.ppermute(block, "ctx", [(i, (i + steps * PLANE) % n_ctx) for i in range(n_ctx)])

    def pass_on(block):
        route = [
            (a * PLANE + b, order[place_of[a] - 1] * PLANE + b) for a in range(n_z) for b in range(PLANE)
        ]
        return lax.ppermute(block, "ctx", route)

    def behind(block):
        route = [(a * PLANE + b, a * PLANE + (b + 1) % PLANE) for a in range(n_z) for b in range(PLANE)]
        return lax.ppermute(block, "ctx", route)

    def swap(block, bits):
        return lax.ppermute(block, "ctx", [(i, i ^ bits) for i in range(n_ctx)])

    tokens_t = tokens.T
    blocks = [rms_norm_t(tokens_t, gain_attn)]

    lanes = query_weight.shape[1]
    share = key_weight.shape[1]
    tiles = -(-width // lanes)
    kv_rows = jnp.concatenate([key_weight.T, value_weight.T], axis=0)
    kv_rows = jnp.pad(kv_rows, ((0, 0), (0, tiles * lanes - width))).reshape(2 * share, tiles, lanes)
    packed = jnp.concatenate(
        [query_weight, kv_rows.transpose(1, 0, 2).reshape(tiles * 2 * share, lanes)], axis=0
    )
    near, far = swap(packed, 2), swap(packed, 4)

    cols = out_weight.shape[1]
    padded = -(-cols // 16) * 16
    group_rows = out_weight.shape[0] // n_z
    out_rows = jnp.pad(out_weight.T, ((0, padded - cols), (0, 0)))
    out_rows, blocks[0] = lax.optimization_barrier((out_rows, blocks[0]))
    blocks.append(pass_on(blocks[0]))
    out_groups = jnp.stack(jnp.split(out_rows, n_z, axis=1))
    pieces = [
        shift(lax.dynamic_index_in_dim(out_groups, (z + s) % n_z, 0, keepdims=False), s) if s
        else lax.dynamic_index_in_dim(out_groups, z, 0, keepdims=False)
        for s in range(n_z)
    ]
    ordered = jnp.stack(pieces[::-1] + pieces[:0:-1])
    out_mine = lax.dynamic_slice_in_dim(ordered, n_z - 1 - z, n_z, 0)
    heads = PLANE * query_weight.shape[1] // HD
    sinks = lax.dynamic_slice_in_dim(attn_sinks, z * heads, heads)
    own_rows = jnp.arange(tok_dev, dtype=jnp.int32)
    lane = jnp.arange(2 * HD, dtype=jnp.int32) % HD
    half = HD // 2
    inverse_freq = jnp.exp(-(2.0 * (lane % half).astype(F32) / HD) * math.log(ROPE_BASE))
    mine = places[z]
    block_z = ring[(mine + jnp.arange(n_z, dtype=jnp.int32)) % n_z]
    numbers = block_z * PLANE + j
    angles = (numbers[:, None] * tok_dev + own_rows[None, :]).astype(F32)[:, :, None] * inverse_freq
    signed_sine = jnp.where(lane < half, -jnp.sin(angles), jnp.sin(angles))
    cosine = jnp.cos(angles)
    below = (places[jnp.maximum(block_z - 1, 0)] - mine) % n_z
    previous_at = jnp.where(j == 0, below, jnp.arange(n_z, dtype=jnp.int32))
    relative = jnp.arange(PLANE, dtype=jnp.int32) ^ j
    place = jnp.concatenate([(numbers == 0).astype(jnp.int32), previous_at])
    out_mine, corner = lax.optimization_barrier((out_mine, packed))
    out_all = lax.all_gather(out_mine, "ctx", axis_index_groups=planes)
    (packed, blocks[1], cosine, signed_sine, place, relative, sinks, early) = lax.optimization_barrier(
        (packed, blocks[1], cosine, signed_sine, place, relative, sinks, early)
    )
    for _ in range(n_z - 2):
        blocks.append(pass_on(blocks[-1]))
    shares = []
    for piece in (packed, near, far, swap(corner, 6)):
        shares += [piece, swap(piece, 1)]
    count = n_z - 1
    queries, lines = project_blocks(relative, blocks[:count], shares, share, cosine[:count], signed_sine[:count])
    last, last_lines = project_blocks(relative, blocks[count:], shares, share, cosine[count:], signed_sine[count:])
    halos = jnp.concatenate([behind(lines), behind(last_lines)])
    key_values = jnp.concatenate([lines, last_lines])

    def parts_of(numbers):
        return attend_and_project(numbers, place, sinks, queries, last, key_values, halos, out_all, width)

    running = parts_of((1,))[0].astype(BF16)
    others = parts_of(tuple(range(2, n_z)) + (0,))
    for i in range(n_z - 2):
        running = (pass_on(running).astype(F32) + others[i]).astype(BF16)
    total = pass_on(running).astype(F32) + others[n_z - 2]
    return (tokens_t.astype(F32) + total).astype(BF16), early


def expert_kernel(tile, hidden, rows_ref, gate_ref, upper_ref, down_ref, out_ref, total_ref):
    step = pl.program_id(0)
    steps = pl.num_programs(0)

    def add(count, initial):
        rows = rows_ref[...]
        gate = dot32(rows, gate_ref[0, :, :count])
        upper = dot32(rows, upper_ref[0, :, :count])
        activation = (gate * jax.nn.sigmoid(1.702 * gate) * (upper + 1.0)).astype(BF16)
        terms = dot32(activation, down_ref[:count, :])
        total_ref[...] = terms if initial else total_ref[...] + terms

    last = hidden - (-(-hidden // tile) - 1) * tile

    @pl.when(step == 0)
    def _():
        add(tile, True)

    @pl.when(jnp.logical_and(step > 0, step < steps - 1))
    def _():
        add(tile, False)

    @pl.when(step == steps - 1)
    def _():
        add(last, False)
        out_ref[...] = total_ref[...].astype(BF16)


def run_expert(rows, gate_up, down):
    count, width = rows.shape
    hidden = down.shape[0]
    tile = 512 if hidden > 1024 else 256
    return pl.pallas_call(
        functools.partial(expert_kernel, tile, hidden),
        grid=(-(-hidden // tile),),
        in_specs=[
            pl.BlockSpec((count, width), lambda f: (0, 0)),
            pl.BlockSpec((1, width, tile), lambda f: (0, 0, f)),
            pl.BlockSpec((1, width, tile), lambda f: (1, 0, f)),
            pl.BlockSpec((tile, width), lambda f: (f, 0)),
        ],
        out_specs=pl.BlockSpec((count, width), lambda f: (0, 0)),
        out_shape=jax.ShapeDtypeStruct((count, width), BF16),
        scratch_shapes=[pltpu.VMEM((count, width), F32)],
        compiler_params=pltpu.CompilerParams(vmem_limit_bytes=52 * 2**20),
        cost_estimate=pl.CostEstimate(
            flops=6 * count * width * hidden,
            bytes_accessed=6 * width * hidden + 4 * count * width,
            transcendentals=count * hidden,
        ),
    )(rows, gate_up, gate_up, down)


def slot_chunks(capacity):
    return [capacity - 8, 8] if capacity > 8 else [capacity]


def dispatch_kernel(chosen_ref, normed_ref, out_ref):
    out_ref[...] = dot_nt(chosen_ref[...], normed_ref[...]).astype(BF16)


def dispatch(chosen, normed):
    total, rows = chosen.shape
    width = normed.shape[0]
    return pl.pallas_call(
        dispatch_kernel,
        out_shape=jax.ShapeDtypeStruct((total, width), BF16),
        compiler_params=pltpu.CompilerParams(vmem_limit_bytes=24 * 2**20),
        cost_estimate=pl.CostEstimate(
            flops=2 * total * rows * width, bytes_accessed=2 * width * (total + rows), transcendentals=0
        ),
    )(chosen, normed)


def routing(route_ids, combine, n_ctx, sizes):
    tok_dev = route_ids.shape[0]
    named = route_ids[:, :, None] == jnp.arange(n_ctx, dtype=jnp.int32)[None, None, :]
    member = jnp.any(named, axis=1)
    weight_of = jnp.sum(jnp.where(named, combine[:, :, None], 0.0), axis=1)
    rows = jnp.arange(tok_dev, dtype=jnp.int32)
    earlier = (rows[:, None] > rows[None, :]).astype(BF16)
    slot_of = dot32(earlier, member.astype(BF16)).astype(jnp.int32)
    slot_of = jnp.where(member, slot_of, -1).T
    weight_of = weight_of.T
    chunks = []
    first = 0
    for size in sizes:
        slots = first + jnp.arange(size, dtype=jnp.int32)
        chosen = (slot_of[:, None, :] == slots[None, :, None]).reshape(n_ctx * size, tok_dev)
        scale = jnp.where(chosen, jnp.repeat(weight_of, size, axis=0), 0.0)
        high = scale.astype(BF16)
        low = (scale - high.astype(F32)).astype(BF16)
        chunks.append((chosen.astype(BF16), jnp.concatenate([high, low], axis=1)))
        first += size
    return chunks


def mix_experts(normed, sizes, matrices, gate_up, down):
    width, tok_dev = normed.shape
    n_ctx, n_exp = lax.axis_size("ctx"), lax.axis_size("exp")
    width_local = width // n_exp

    def tiles(rows, size):
        if size % 8 == 0 or size % 4:
            return rows.reshape(n_ctx, size, -1)
        return rows.reshape(n_ctx, size // 4, 4, -1)

    def exchange(parts):
        return lax.all_to_all(parts, "ctx", split_axis=0, concat_axis=0, tiled=True)

    def in_order(parts, earlier):
        return lax.optimization_barrier((parts, earlier))

    outgoing, received = [], []
    for size, (chosen, _) in zip(sizes, matrices):
        if outgoing:
            chosen, outgoing[-1] = in_order(chosen, outgoing[-1])
        outgoing.append(tiles(dispatch(chosen, normed), size))
    for parts in outgoing:
        if received:
            parts, received[-1] = in_order(parts, received[-1])
        received.append(exchange(parts))

    results = []
    for i, size in enumerate(sizes):
        if i > 1 and i == len(sizes) - 1:
            received[i], results[0] = in_order(received[i], results[0])
        if results:
            received[i], results[-1] = in_order(received[i], results[-1])
        rows_in = received[i].reshape(n_ctx * size, width)
        results.append(tiles(run_expert(rows_in, gate_up, down), size))

    answers = []
    for parts in results:
        if answers:
            parts, answers[-1] = in_order(parts, answers[-1])
        answers.append(exchange(parts))

    moe_out = jnp.zeros((width_local, tok_dev), F32)
    for size, (_, scale), answer in zip(sizes, matrices, answers):
        if n_exp > 1:
            answer = lax.psum_scatter(answer, "exp", scatter_dimension=answer.ndim - 1, tiled=True)
        terms = lax.dot_general(
            answer.reshape(n_ctx * size, width_local), scale, (((0,), (0,)), ((), ())),
            preferred_element_type=F32,
        )
        moe_out = moe_out + terms[:, :tok_dev] + terms[:, tok_dev:]
    return moe_out


def per_device(
    tokens,
    route_ids,
    combine,
    gain_attn,
    gain_moe,
    query_weight,
    key_weight,
    value_weight,
    attn_sinks,
    out_weight,
    gate_up_weight,
    down_weight,
):
    tok_dev, width_local = tokens.shape
    n_ctx = lax.axis_size("ctx")
    n_exp = lax.axis_size("exp")
    capacity = tok_dev * route_ids.shape[1] * 5 // (4 * n_ctx)
    sizes = slot_chunks(capacity)
    matrices = routing(route_ids, combine, n_ctx, sizes)
    by_planes = n_exp == 1 and n_ctx % PLANE == 0 and n_ctx > PLANE
    project = project_planes if by_planes else project_whole
    residual, matrices = project(
        tokens, gain_attn, query_weight, key_weight, value_weight, attn_sinks, out_weight, matrices
    )
    width = residual.shape[0]
    normed_moe = rms_norm_t(residual, gain_moe)
    exp_index = lax.axis_index("exp")
    residual_local = lax.dynamic_slice_in_dim(residual, exp_index * width_local, width_local, 0)

    moe_out = mix_experts(normed_moe, sizes, matrices, gate_up_weight[0], down_weight[0])
    return (residual_local.astype(F32) + moe_out).astype(BF16).T


def solution(mesh):
    return jax.shard_map(
        per_device,
        mesh=mesh,
        in_specs=(
            P("ctx", "exp"),
            P("ctx", None),
            P("ctx", None),
            P(),
            P(),
            P(None, ("exp", "ctx")),
            P(None, ("exp", "ctx")),
            P(None, ("exp", "ctx")),
            P("exp"),
            P("exp", "ctx"),
            P("ctx", None, None, "exp"),
            P("ctx", "exp", None),
        ),
        out_specs=P("ctx", "exp"),
        check_vma=False,
    )
```

```python
import functools
import math

import jax
import jax.numpy as jnp
from jax import lax
from jax.experimental import pallas as pl
from jax.experimental.pallas import tpu as pltpu
from jax.sharding import PartitionSpec as P

HD = 64
WINDOW = 128
EPSILON = 1e-05
ROPE_BASE = 150000.0
PLANE = 8
BF16 = jnp.bfloat16
F32 = jnp.float32


def rms_norm(values, gain):
    wide = values.astype(F32)
    meansq = jnp.mean(wide * wide, axis=-1, keepdims=True)
    return (wide * lax.rsqrt(meansq + EPSILON) * gain).astype(BF16)


def rms_norm_t(values, gain):
    wide = values.astype(F32)
    meansq = jnp.mean(wide * wide, axis=0, keepdims=True)
    return (wide * lax.rsqrt(meansq + EPSILON) * gain[:, None]).astype(BF16)


def rotary(values, angles_pos):
    half_dim = values.shape[-1] // 2
    inverse_freq = jnp.exp(
        -(2.0 * jnp.arange(half_dim, dtype=F32) / values.shape[-1]) * math.log(ROPE_BASE)
    )
    angles = angles_pos[:, None] * inverse_freq[None, :]
    cosine = jnp.cos(angles)[:, None, :]
    sine_part = jnp.sin(angles)[:, None, :]
    first_half = values[..., :half_dim]
    second_half = values[..., half_dim:]
    return jnp.concatenate(
        [
            first_half * cosine - second_half * sine_part,
            second_half * cosine + first_half * sine_part,
        ],
        axis=-1,
    )


def sink_softmax(scores, key_mask, sink_col):
    masked = jnp.where(key_mask, scores, -1e30)
    row_top = jnp.maximum(jnp.max(masked, axis=-1, keepdims=True), sink_col)
    weights = jnp.where(key_mask, jnp.exp(masked - row_top), 0.0)
    denominator = jnp.sum(weights, axis=-1, keepdims=True) + jnp.exp(sink_col - row_top)
    return (weights / denominator).astype(BF16)


def attend_block(query_rows, key_rows, value_rows, query_pos, key_pos, sink_col):
    scores = jnp.einsum(
        "qkgd,skd->kgqs", query_rows, key_rows, preferred_element_type=F32
    ) * HD ** (-0.5)
    distance = query_pos[:, None] - key_pos[None, :]
    key_mask = (distance >= 0) & (distance < WINDOW) & (key_pos >= 0)[None, :]
    weights = sink_softmax(scores, key_mask, sink_col)
    mixed_rows = jnp.einsum("kgqs,skd->qkgd", weights, value_rows, preferred_element_type=F32)
    return mixed_rows.astype(BF16).reshape(query_rows.shape[0], -1)


def dot32(a, b):
    return jnp.dot(a, b, preferred_element_type=F32)


def project_whole(
    tokens, gain_attn, query_weight, key_weight, value_weight, attn_sinks, out_weight, early
):
    tok_dev = tokens.shape[0]
    full_rows = lax.all_gather(tokens, "exp", axis=1, tiled=True)
    normed = rms_norm(full_rows, gain_attn)
    pieces = lax.all_gather((query_weight, key_weight, value_weight), "ctx", axis=1, tiled=True)
    query_lin, key_lin, value_lin = tuple(dot32(normed, piece) for piece in pieces)
    heads_local = query_lin.shape[1] // HD
    kv_local = key_lin.shape[1] // HD
    group_size = heads_local // kv_local
    position_ids = lax.axis_index("ctx") * tok_dev + jnp.arange(tok_dev, dtype=jnp.int32)
    angles_pos = position_ids.astype(F32)
    query = rotary(query_lin.reshape(tok_dev, heads_local, HD), angles_pos).astype(BF16)
    keys_own = rotary(key_lin.reshape(tok_dev, kv_local, HD), angles_pos).astype(BF16)
    key_value = jnp.stack([keys_own.reshape(tok_dev, kv_local * HD), value_lin.astype(BF16)])
    n_ctx = lax.axis_size("ctx")
    previous = lax.ppermute(key_value, "ctx", [(i, i + 1) for i in range(n_ctx - 1)])
    context = jnp.concatenate([previous, key_value], axis=1)
    key_pos = position_ids[0] - WINDOW + jnp.arange(tok_dev + WINDOW, dtype=jnp.int32)
    attended = attend_block(
        query.reshape(tok_dev, kv_local, group_size, HD),
        context[0].reshape(-1, kv_local, HD),
        context[1].reshape(-1, kv_local, HD),
        position_ids,
        key_pos,
        attn_sinks.reshape(kv_local, group_size, 1, 1),
    )
    head_terms = dot32(attended, lax.all_gather(out_weight, "ctx", axis=1, tiled=True))
    attn_proj = lax.psum(head_terms.astype(BF16), "exp").astype(F32)
    return (full_rows.astype(F32) + attn_proj).astype(BF16).T, early


def dot_nt(a, b):
    return lax.dot_general(a, b, (((1,), (1,)), ((), ())), preferred_element_type=F32)


def turn(values, cosine, signed_sine):
    width = values.shape[1]
    half = HD // 2
    lane = lax.broadcasted_iota(jnp.int32, values.shape, 1) % HD
    partner = jnp.where(
        lane < half,
        pltpu.roll(values, width - half, 1),
        pltpu.roll(values, half, 1),
    )
    return values * cosine + partner * signed_sine


def qkv_kernel(count, place_ref, *refs):
    blocks, shares, refs = refs[:count], refs[count : count + PLANE], refs[count + PLANE :]
    cos_ref, sin_ref, q_ref, key_value_ref, rows_ref, kv_ref = refs
    width, rows = blocks[0].shape
    cols = shares[0].shape[1]
    share = kv_ref.shape[2]
    for r in range(count):
        rows_ref[r * rows : (r + 1) * rows, :] = blocks[r][...].T

    for i in range(PLANE):
        for tile in range(-(-width // cols)):
            at, lanes = width + 2 * share * tile, slice(tile * cols, (tile + 1) * cols)
            for part in range(2):
                kv_ref[part, place_ref[i], :, lanes] = shares[i][at + part * share : at + (part + 1) * share]
    both = kv_ref[...].reshape(2 * PLANE * share, kv_ref.shape[3])[:, :width]
    lines = dot_nt(rows_ref[...], both)
    half = PLANE * share
    for r in range(count):
        piece = lines[r * rows : (r + 1) * rows]
        key_value_ref[r, :, :half] = turn(piece[:, :half], cos_ref[r], sin_ref[r]).astype(BF16)
        key_value_ref[r, :, half:] = piece[:, half:].astype(BF16)

    for i in range(0, PLANE, 2):
        weight = jnp.concatenate([shares[i][:width], shares[i + 1][:width]], axis=1)
        query = dot32(rows_ref[...], weight)
        for k in range(2):
            lanes = pl.ds(pl.multiple_of(place_ref[i + k] * cols, cols), cols)
            for r in range(count):
                piece = query[r * rows : (r + 1) * rows, k * cols : (k + 1) * cols]
                q_ref[r, :, lanes] = turn(piece, cos_ref[r], sin_ref[r]).astype(BF16)


def project_blocks(place, blocks, shares, share, cosine, signed_sine):
    count = len(blocks)
    width, rows = blocks[0].shape
    cols = shares[0].shape[1]
    tiles = -(-width // cols)
    kv_cols = 2 * PLANE * share
    vmem = pl.BlockSpec(memory_space=pltpu.VMEM)
    return pl.pallas_call(
        functools.partial(qkv_kernel, count),
        in_specs=[pl.BlockSpec(memory_space=pltpu.SMEM)] + [vmem] * (count + PLANE + 2),
        out_specs=[vmem, vmem],
        out_shape=[
            jax.ShapeDtypeStruct((count, rows, PLANE * cols), BF16),
            jax.ShapeDtypeStruct((count, rows, kv_cols), BF16),
        ],
        scratch_shapes=[
            pltpu.VMEM((count * rows, width), BF16),
            pltpu.VMEM((2, PLANE, share, tiles * cols), BF16),
        ],
        compiler_params=pltpu.CompilerParams(vmem_limit_bytes=40 * 2**20),
        cost_estimate=pl.CostEstimate(
            flops=2 * count * rows * width * (PLANE * cols + kv_cols),
            bytes_accessed=2 * width * (PLANE * cols + kv_cols + count * rows),
            transcendentals=0,
        ),
    )(place, *blocks, *shares, cosine, signed_sine)


def attend_kernel(
    numbers, place_ref, sinks_ref, queries_ref, key_values_ref, halos_ref, weight_hbm, out_ref, att_ref, weight_ref, copied
):
    copy = pltpu.make_async_copy(weight_hbm, weight_ref, copied)
    copy.start()
    count, rows = key_values_ref.shape[:2]
    pair = 2 * HD
    kv_heads = key_values_ref.shape[2] // pair
    kv_cols = kv_heads * HD
    pairs = queries_ref.shape[2] // pair
    lane = lax.broadcasted_iota(jnp.int32, (rows, pair), 1)
    low = lane < HD

    def spread(values, head):
        moved = pltpu.roll(values.astype(F32), HD, 1)
        chunk = values.astype(F32)
        lower, upper = (chunk, moved) if head % 2 == 0 else (moved, chunk)
        zero = jnp.zeros_like(chunk)
        return jnp.concatenate(
            [jnp.where(low, lower, zero), jnp.where(low, zero, upper)], axis=0
        ).astype(BF16)

    def side(ref):
        tables = []
        for head in range(kv_heads):
            at = head // 2 * pair
            keys = spread(ref[:, at : at + pair], head)
            values = spread(ref[:, kv_cols + at : kv_cols + at + pair], head)
            tables.append((keys, values))
        return tables

    row = lax.broadcasted_iota(jnp.int32, (rows, rows), 0)
    col = lax.broadcasted_iota(jnp.int32, (rows, rows), 1)
    inside = col <= row
    scale = HD**-0.5
    for i, r in enumerate(numbers):
        own, previous = side(key_values_ref.at[r]), side(halos_ref.at[place_ref[count + r]])
        shown = jnp.logical_or(inside, place_ref[r] == 0)
        for p in range(pairs):
            head = p * kv_heads // pairs
            chunk = queries_ref[r, :, p * pair : (p + 1) * pair]
            scores_own = dot_nt(chunk, own[head][0])
            scores_previous = dot_nt(chunk, previous[head][0])
            probs_own, probs_previous = [], []
            for h in range(2):
                half = slice(h * rows, (h + 1) * rows)
                scores = jnp.where(inside, scores_own[:, half], scores_previous[:, half]) * scale
                scores = jnp.where(shown, scores, -1e30)
                sink = sinks_ref[2 * p + h]
                top = jnp.maximum(jnp.max(scores, axis=1, keepdims=True), sink)
                weights = jnp.exp(scores - top)
                total = jnp.sum(weights, axis=1, keepdims=True) + jnp.exp(sink - top)
                probs = weights / total
                probs_own.append(jnp.where(inside, probs, 0.0).astype(BF16))
                probs_previous.append(jnp.where(inside, 0.0, probs).astype(BF16))
            mixed = dot32(jnp.concatenate(probs_own, axis=1), own[head][1])
            mixed = mixed + dot32(jnp.concatenate(probs_previous, axis=1), previous[head][1])
            att_ref[i * rows : (i + 1) * rows, p * pair : (p + 1) * pair] = mixed.astype(BF16)

    shares, groups, padded, depth = weight_ref.shape
    cols = out_ref.shape[1] // (shares * groups)
    attended = att_ref[...]
    copy.wait()
    for p in range(shares):
        terms = dot_nt(weight_ref[p].reshape(groups * padded, depth), attended)
        for g in range(groups):
            at = (g * shares + p) * cols
            for i in range(len(numbers)):
                out_ref[i, at : at + cols, :] = terms[g * padded : g * padded + cols, i * rows : (i + 1) * rows]


def attend_and_project(numbers, place, sinks, queries, key_values, halos, weight, width):
    rows = queries.shape[1]
    count = len(numbers)
    depth = weight.shape[3]
    vmem = pl.BlockSpec(memory_space=pltpu.VMEM)
    smem = pl.BlockSpec(memory_space=pltpu.SMEM)
    return pl.pallas_call(
        functools.partial(attend_kernel, numbers),
        in_specs=[smem, smem] + [vmem] * 3 + [pl.BlockSpec(memory_space=pl.ANY)],
        out_specs=vmem,
        out_shape=jax.ShapeDtypeStruct((count, width, rows), F32),
        scratch_shapes=[
            pltpu.VMEM((count * rows, depth), BF16),
            pltpu.VMEM(weight.shape, BF16),
            pltpu.SemaphoreType.DMA,
        ],
        compiler_params=pltpu.CompilerParams(vmem_limit_bytes=56 * 2**20),
        cost_estimate=pl.CostEstimate(
            flops=2 * count * rows * depth * (width + 8 * rows),
            bytes_accessed=2 * width * (depth + 2 * count * rows),
            transcendentals=count * rows * rows * depth // HD,
        ),
    )(place, sinks, queries, key_values, halos, weight)


def project_planes(
    tokens, gain_attn, query_weight, key_weight, value_weight, attn_sinks, out_weight, early
):
    tok_dev, width = tokens.shape
    n_ctx = lax.axis_size("ctx")
    n_z = n_ctx // PLANE
    index = lax.axis_index("ctx")
    z, j = index // PLANE, index % PLANE
    planes = [[PLANE * a + b for b in range(PLANE)] for a in range(n_z)]
    order = list(range(0, n_z, 2)) + list(range(1, n_z, 2))[::-1]
    place_of = [order.index(a) for a in range(n_z)]
    ring, places = jnp.array(order, jnp.int32), jnp.array(place_of, jnp.int32)

    def shift(block, steps):
        return lax.ppermute(block, "ctx", [(i, (i + steps * PLANE) % n_ctx) for i in range(n_ctx)])

    def pass_on(block):
        route = [
            (a * PLANE + b, order[place_of[a] - 1] * PLANE + b) for a in range(n_z) for b in range(PLANE)
        ]
        return lax.ppermute(block, "ctx", route)

    def behind(block):
        route = [(a * PLANE + b, a * PLANE + (b + 1) % PLANE) for a in range(n_z) for b in range(PLANE)]
        return lax.ppermute(block, "ctx", route)

    def swap(block, bits):
        return lax.ppermute(block, "ctx", [(i, i ^ bits) for i in range(n_ctx)])

    tokens_t = tokens.T
    blocks = [rms_norm_t(tokens_t, gain_attn)]

    lanes = query_weight.shape[1]
    share = key_weight.shape[1]
    tiles = -(-width // lanes)
    kv_rows = jnp.concatenate([key_weight.T, value_weight.T], axis=0)
    kv_rows = jnp.pad(kv_rows, ((0, 0), (0, tiles * lanes - width))).reshape(2 * share, tiles, lanes)
    packed = jnp.concatenate(
        [query_weight, kv_rows.transpose(1, 0, 2).reshape(tiles * 2 * share, lanes)], axis=0
    )
    near, far = swap(packed, 2), swap(packed, 4)

    cols = out_weight.shape[1]
    padded = -(-cols // 16) * 16
    group_rows = out_weight.shape[0] // n_z
    out_rows = jnp.pad(out_weight.T, ((0, padded - cols), (0, 0)))
    out_rows, blocks[0] = lax.optimization_barrier((out_rows, blocks[0]))
    blocks.append(pass_on(blocks[0]))
    out_groups = jnp.stack(jnp.split(out_rows, n_z, axis=1))
    pieces = [
        shift(lax.dynamic_index_in_dim(out_groups, (z + s) % n_z, 0, keepdims=False), s) if s
        else lax.dynamic_index_in_dim(out_groups, z, 0, keepdims=False)
        for s in range(n_z)
    ]
    ordered = jnp.stack(pieces[::-1] + pieces[:0:-1])
    out_mine = lax.dynamic_slice_in_dim(ordered, n_z - 1 - z, n_z, 0)
    heads = PLANE * query_weight.shape[1] // HD
    sinks = lax.dynamic_slice_in_dim(attn_sinks, z * heads, heads)
    own_rows = jnp.arange(tok_dev, dtype=jnp.int32)
    lane = jnp.arange(2 * HD, dtype=jnp.int32) % HD
    half = HD // 2
    inverse_freq = jnp.exp(-(2.0 * (lane % half).astype(F32) / HD) * math.log(ROPE_BASE))
    mine = places[z]
    block_z = ring[(mine + jnp.arange(n_z, dtype=jnp.int32)) % n_z]
    numbers = block_z * PLANE + j
    angles = (numbers[:, None] * tok_dev + own_rows[None, :]).astype(F32)[:, :, None] * inverse_freq
    signed_sine = jnp.where(lane < half, -jnp.sin(angles), jnp.sin(angles))
    cosine = jnp.cos(angles)
    below = (places[jnp.maximum(block_z - 1, 0)] - mine) % n_z
    previous_at = jnp.where(j == 0, below, jnp.arange(n_z, dtype=jnp.int32))
    relative = jnp.arange(PLANE, dtype=jnp.int32) ^ j
    place = jnp.concatenate([(numbers == 0).astype(jnp.int32), previous_at])
    out_mine, near = lax.optimization_barrier((out_mine, near))
    out_all = lax.all_gather(out_mine, "ctx", axis_index_groups=planes)
    for _ in range(n_z - 2):
        blocks.append(pass_on(blocks[-1]))
    packed, blocks[1] = lax.optimization_barrier((packed, blocks[1]))
    corner = swap(packed, 6)
    second = min(2, n_z - 1)
    (near, far, blocks[second], cosine, signed_sine, place, relative, sinks, early) = lax.optimization_barrier(
        (near, far, blocks[second], cosine, signed_sine, place, relative, sinks, early)
    )
    shares = [packed, swap(packed, 1), near, swap(near, 1), far, swap(far, 1)]
    corner, blocks[-1] = lax.optimization_barrier((corner, blocks[-1]))
    shares += [corner, swap(corner, 1)]
    queries, key_values = project_blocks(relative, blocks, shares, share, cosine, signed_sine)
    halos = behind(key_values)

    def parts_of(numbers):
        return attend_and_project(numbers, place, sinks, queries, key_values, halos, out_all, width)

    running = parts_of((1,))[0].astype(BF16)
    others = parts_of(tuple(range(2, n_z)) + (0,))
    for i in range(n_z - 2):
        running = (pass_on(running).astype(F32) + others[i]).astype(BF16)
    total = pass_on(running).astype(F32) + others[n_z - 2]
    return (tokens_t.astype(F32) + total).astype(BF16), early


def expert_kernel(tile, hidden, rows_ref, gate_ref, upper_ref, down_ref, out_ref, total_ref):
    step = pl.program_id(0)
    steps = pl.num_programs(0)

    def add(count, initial):
        rows = rows_ref[...]
        gate = dot32(rows, gate_ref[0, :, :count])
        upper = dot32(rows, upper_ref[0, :, :count])
        activation = (gate * jax.nn.sigmoid(1.702 * gate) * (upper + 1.0)).astype(BF16)
        terms = dot32(activation, down_ref[:count, :])
        total_ref[...] = terms if initial else total_ref[...] + terms

    last = hidden - (-(-hidden // tile) - 1) * tile

    @pl.when(step == 0)
    def _():
        add(tile, True)

    @pl.when(jnp.logical_and(step > 0, step < steps - 1))
    def _():
        add(tile, False)

    @pl.when(step == steps - 1)
    def _():
        add(last, False)
        out_ref[...] = total_ref[...].astype(BF16)


def run_expert(rows, gate_up, down):
    count, width = rows.shape
    hidden = down.shape[0]
    tile = 512 if hidden > 1024 else 256
    return pl.pallas_call(
        functools.partial(expert_kernel, tile, hidden),
        grid=(-(-hidden // tile),),
        in_specs=[
            pl.BlockSpec((count, width), lambda f: (0, 0)),
            pl.BlockSpec((1, width, tile), lambda f: (0, 0, f)),
            pl.BlockSpec((1, width, tile), lambda f: (1, 0, f)),
            pl.BlockSpec((tile, width), lambda f: (f, 0)),
        ],
        out_specs=pl.BlockSpec((count, width), lambda f: (0, 0)),
        out_shape=jax.ShapeDtypeStruct((count, width), BF16),
        scratch_shapes=[pltpu.VMEM((count, width), F32)],
        compiler_params=pltpu.CompilerParams(vmem_limit_bytes=52 * 2**20),
        cost_estimate=pl.CostEstimate(
            flops=6 * count * width * hidden,
            bytes_accessed=6 * width * hidden + 4 * count * width,
            transcendentals=count * hidden,
        ),
    )(rows, gate_up, gate_up, down)


def slot_chunks(capacity):
    return [capacity - 8, 8] if capacity > 8 else [capacity]


def dispatch_kernel(chosen_ref, normed_ref, out_ref):
    out_ref[...] = dot_nt(chosen_ref[...], normed_ref[...]).astype(BF16)


def dispatch(chosen, normed):
    total, rows = chosen.shape
    width = normed.shape[0]
    return pl.pallas_call(
        dispatch_kernel,
        out_shape=jax.ShapeDtypeStruct((total, width), BF16),
        compiler_params=pltpu.CompilerParams(vmem_limit_bytes=24 * 2**20),
        cost_estimate=pl.CostEstimate(
            flops=2 * total * rows * width, bytes_accessed=2 * width * (total + rows), transcendentals=0
        ),
    )(chosen, normed)


def routing(route_ids, combine, n_ctx, sizes):
    tok_dev = route_ids.shape[0]
    named = route_ids[:, :, None] == jnp.arange(n_ctx, dtype=jnp.int32)[None, None, :]
    member = jnp.any(named, axis=1)
    weight_of = jnp.sum(jnp.where(named, combine[:, :, None], 0.0), axis=1)
    rows = jnp.arange(tok_dev, dtype=jnp.int32)
    earlier = (rows[:, None] > rows[None, :]).astype(BF16)
    slot_of = jnp.where(member, dot32(earlier, member.astype(BF16)), -1.0).T.astype(BF16)
    weight_of = weight_of.T
    high = weight_of.astype(BF16)
    low = (weight_of - high.astype(F32)).astype(BF16)
    table = jnp.concatenate([slot_of, high, low], axis=1)
    chunks = []
    first = 0
    for size in sizes:
        number = jnp.arange(n_ctx * size, dtype=jnp.int32)[:, None]
        device = (number // size == jnp.arange(n_ctx, dtype=jnp.int32)[None, :]).astype(BF16)
        spread = dot32(device, table)
        chosen = spread[:, :tok_dev] == (first + number % size).astype(F32)
        scale = jnp.where(jnp.concatenate([chosen, chosen], axis=1), spread[:, tok_dev:], 0.0).astype(BF16)
        chunks.append((chosen.astype(BF16), scale))
        first += size
    return chunks


def mix_experts(normed, sizes, matrices, gate_up, down):
    width, tok_dev = normed.shape
    n_ctx, n_exp = lax.axis_size("ctx"), lax.axis_size("exp")
    width_local = width // n_exp

    def tiles(rows, size):
        if size % 8 == 0 or size % 4:
            return rows.reshape(n_ctx, size, -1)
        return rows.reshape(n_ctx, size // 4, 4, -1)

    def exchange(parts):
        return lax.all_to_all(parts, "ctx", split_axis=0, concat_axis=0, tiled=True)

    def in_order(parts, earlier):
        return lax.optimization_barrier((parts, earlier))

    outgoing, received = [], []
    for size, (chosen, _) in zip(sizes, matrices):
        if outgoing:
            chosen, outgoing[-1] = in_order(chosen, outgoing[-1])
        outgoing.append(tiles(dispatch(chosen, normed), size))
    for parts in outgoing:
        if received:
            parts, received[-1] = in_order(parts, received[-1])
        received.append(exchange(parts))

    results = []
    for i, size in enumerate(sizes):
        if i > 1 and i == len(sizes) - 1:
            received[i], results[0] = in_order(received[i], results[0])
        if results:
            received[i], results[-1] = in_order(received[i], results[-1])
        rows_in = received[i].reshape(n_ctx * size, width)
        results.append(tiles(run_expert(rows_in, gate_up, down), size))

    answers = []
    for parts in results:
        if answers:
            parts, answers[-1] = in_order(parts, answers[-1])
        answers.append(exchange(parts))

    moe_out = jnp.zeros((width_local, tok_dev), F32)
    for size, (_, scale), answer in zip(sizes, matrices, answers):
        if n_exp > 1:
            answer = lax.psum_scatter(answer, "exp", scatter_dimension=answer.ndim - 1, tiled=True)
        terms = lax.dot_general(
            answer.reshape(n_ctx * size, width_local), scale, (((0,), (0,)), ((), ())),
            preferred_element_type=F32,
        )
        moe_out = moe_out + terms[:, :tok_dev] + terms[:, tok_dev:]
    return moe_out


def per_device(
    tokens,
    route_ids,
    combine,
    gain_attn,
    gain_moe,
    query_weight,
    key_weight,
    value_weight,
    attn_sinks,
    out_weight,
    gate_up_weight,
    down_weight,
):
    tok_dev, width_local = tokens.shape
    n_ctx = lax.axis_size("ctx")
    n_exp = lax.axis_size("exp")
    capacity = tok_dev * route_ids.shape[1] * 5 // (4 * n_ctx)
    sizes = slot_chunks(capacity)
    matrices = routing(route_ids, combine, n_ctx, sizes)
    by_planes = n_exp == 1 and n_ctx % PLANE == 0 and n_ctx > PLANE
    project = project_planes if by_planes else project_whole
    residual, matrices = project(
        tokens, gain_attn, query_weight, key_weight, value_weight, attn_sinks, out_weight, matrices
    )
    width = residual.shape[0]
    normed_moe = rms_norm_t(residual, gain_moe)
    exp_index = lax.axis_index("exp")
    residual_local = lax.dynamic_slice_in_dim(residual, exp_index * width_local, width_local, 0)

    moe_out = mix_experts(normed_moe, sizes, matrices, gate_up_weight[0], down_weight[0])
    return (residual_local.astype(F32) + moe_out).astype(BF16).T


def solution(mesh):
    return jax.shard_map(
        per_device,
        mesh=mesh,
        in_specs=(
            P("ctx", "exp"),
            P("ctx", None),
            P("ctx", None),
            P(),
            P(),
            P(None, ("exp", "ctx")),
            P(None, ("exp", "ctx")),
            P(None, ("exp", "ctx")),
            P("exp"),
            P("exp", "ctx"),
            P("ctx", None, None, "exp"),
            P("ctx", "exp", None),
        ),
        out_specs=P("ctx", "exp"),
        check_vma=False,
    )
```

```python
import functools
import math

import jax
import jax.numpy as jnp
from jax import lax
from jax.experimental import pallas as pl
from jax.experimental.pallas import tpu as pltpu
from jax.sharding import PartitionSpec as P

HD = 64
WINDOW = 128
EPSILON = 1e-05
ROPE_BASE = 150000.0
PLANE = 8
BF16 = jnp.bfloat16
F32 = jnp.float32


def rms_norm(values, gain):
    wide = values.astype(F32)
    meansq = jnp.mean(wide * wide, axis=-1, keepdims=True)
    return (wide * lax.rsqrt(meansq + EPSILON) * gain).astype(BF16)


def rms_norm_t(values, gain):
    wide = values.astype(F32)
    meansq = jnp.mean(wide * wide, axis=0, keepdims=True)
    return (wide * lax.rsqrt(meansq + EPSILON) * gain[:, None]).astype(BF16)


def rotary(values, angles_pos):
    half_dim = values.shape[-1] // 2
    inverse_freq = jnp.exp(
        -(2.0 * jnp.arange(half_dim, dtype=F32) / values.shape[-1]) * math.log(ROPE_BASE)
    )
    angles = angles_pos[:, None] * inverse_freq[None, :]
    cosine = jnp.cos(angles)[:, None, :]
    sine_part = jnp.sin(angles)[:, None, :]
    first_half = values[..., :half_dim]
    second_half = values[..., half_dim:]
    return jnp.concatenate(
        [
            first_half * cosine - second_half * sine_part,
            second_half * cosine + first_half * sine_part,
        ],
        axis=-1,
    )


def sink_softmax(scores, key_mask, sink_col):
    masked = jnp.where(key_mask, scores, -1e30)
    row_top = jnp.maximum(jnp.max(masked, axis=-1, keepdims=True), sink_col)
    weights = jnp.where(key_mask, jnp.exp(masked - row_top), 0.0)
    denominator = jnp.sum(weights, axis=-1, keepdims=True) + jnp.exp(sink_col - row_top)
    return (weights / denominator).astype(BF16)


def attend_block(query_rows, key_rows, value_rows, query_pos, key_pos, sink_col):
    scores = jnp.einsum(
        "qkgd,skd->kgqs", query_rows, key_rows, preferred_element_type=F32
    ) * HD ** (-0.5)
    distance = query_pos[:, None] - key_pos[None, :]
    key_mask = (distance >= 0) & (distance < WINDOW) & (key_pos >= 0)[None, :]
    weights = sink_softmax(scores, key_mask, sink_col)
    mixed_rows = jnp.einsum("kgqs,skd->qkgd", weights, value_rows, preferred_element_type=F32)
    return mixed_rows.astype(BF16).reshape(query_rows.shape[0], -1)


def dot32(a, b):
    return jnp.dot(a, b, preferred_element_type=F32)


def project_whole(
    tokens, gain_attn, query_weight, key_weight, value_weight, attn_sinks, out_weight, early
):
    tok_dev = tokens.shape[0]
    full_rows = lax.all_gather(tokens, "exp", axis=1, tiled=True)
    normed = rms_norm(full_rows, gain_attn)
    pieces = lax.all_gather((query_weight, key_weight, value_weight), "ctx", axis=1, tiled=True)
    query_lin, key_lin, value_lin = tuple(dot32(normed, piece) for piece in pieces)
    heads_local = query_lin.shape[1] // HD
    kv_local = key_lin.shape[1] // HD
    group_size = heads_local // kv_local
    position_ids = lax.axis_index("ctx") * tok_dev + jnp.arange(tok_dev, dtype=jnp.int32)
    angles_pos = position_ids.astype(F32)
    query = rotary(query_lin.reshape(tok_dev, heads_local, HD), angles_pos).astype(BF16)
    keys_own = rotary(key_lin.reshape(tok_dev, kv_local, HD), angles_pos).astype(BF16)
    key_value = jnp.stack([keys_own.reshape(tok_dev, kv_local * HD), value_lin.astype(BF16)])
    n_ctx = lax.axis_size("ctx")
    previous = lax.ppermute(key_value, "ctx", [(i, i + 1) for i in range(n_ctx - 1)])
    context = jnp.concatenate([previous, key_value], axis=1)
    key_pos = position_ids[0] - WINDOW + jnp.arange(tok_dev + WINDOW, dtype=jnp.int32)
    attended = attend_block(
        query.reshape(tok_dev, kv_local, group_size, HD),
        context[0].reshape(-1, kv_local, HD),
        context[1].reshape(-1, kv_local, HD),
        position_ids,
        key_pos,
        attn_sinks.reshape(kv_local, group_size, 1, 1),
    )
    head_terms = dot32(attended, lax.all_gather(out_weight, "ctx", axis=1, tiled=True))
    attn_proj = lax.psum(head_terms.astype(BF16), "exp").astype(F32)
    return (full_rows.astype(F32) + attn_proj).astype(BF16).T, early


def dot_nt(a, b):
    return lax.dot_general(a, b, (((1,), (1,)), ((), ())), preferred_element_type=F32)


def turn(values, cosine, signed_sine):
    width = values.shape[1]
    half = HD // 2
    lane = lax.broadcasted_iota(jnp.int32, values.shape, 1) % HD
    partner = jnp.where(
        lane < half,
        pltpu.roll(values, width - half, 1),
        pltpu.roll(values, half, 1),
    )
    return values * cosine + partner * signed_sine


def kv_kernel(count, *refs):
    blocks, (weights_hbm, cos_ref, sin_ref, rows_ref, key_value_ref, weight_ref, kv_ref, copied) = refs[:count], refs[count:]
    width, rows = blocks[0].shape
    planes, packed_rows, cols = weight_ref.shape
    copy = pltpu.make_async_copy(weights_hbm.at[:, width : width + packed_rows], weight_ref, copied)
    copy.start()
    for r in range(count):
        rows_ref[r * rows : (r + 1) * rows, :] = blocks[r][...].T
    copy.wait()
    share = kv_ref.shape[2]
    for p in range(planes):
        for tile in range(packed_rows // (2 * share)):
            at, lanes = 2 * share * tile, slice(tile * cols, (tile + 1) * cols)
            for part in range(2):
                kv_ref[part, p, :, lanes] = weight_ref[p, at + part * share : at + (part + 1) * share]
    both = kv_ref[...].reshape(2 * planes * share, kv_ref.shape[3])[:, :width]
    lines = dot_nt(rows_ref[...], both)
    half = planes * share
    for r in range(count):
        piece = lines[r * rows : (r + 1) * rows]
        key_value_ref[r, :, :half] = turn(piece[:, :half], cos_ref[r], sin_ref[r]).astype(BF16)
        key_value_ref[r, :, half:] = piece[:, half:].astype(BF16)


def project_keys(blocks, weights, share, cosine, signed_sine):
    count = len(blocks)
    width, rows = blocks[0].shape
    planes, packed, cols = weights.shape
    kv_cols = 2 * planes * share
    vmem = pl.BlockSpec(memory_space=pltpu.VMEM)
    return pl.pallas_call(
        functools.partial(kv_kernel, count),
        in_specs=[vmem] * count + [pl.BlockSpec(memory_space=pl.ANY), vmem, vmem],
        out_specs=[vmem, vmem],
        out_shape=[
            jax.ShapeDtypeStruct((count * rows, width), BF16),
            jax.ShapeDtypeStruct((count, rows, kv_cols), BF16),
        ],
        scratch_shapes=[
            pltpu.VMEM((planes, packed - width, cols), BF16),
            pltpu.VMEM((2, planes, share, (packed - width) // (2 * share) * cols), BF16),
            pltpu.SemaphoreType.DMA,
        ],
        compiler_params=pltpu.CompilerParams(vmem_limit_bytes=40 * 2**20),
        cost_estimate=pl.CostEstimate(
            flops=2 * count * rows * width * kv_cols,
            bytes_accessed=2 * width * (kv_cols + 2 * count * rows),
            transcendentals=0,
        ),
    )(*blocks, weights, cosine, signed_sine)


def query_kernel(rows_ref, weights_hbm, cos_ref, sin_ref, q_ref, weight_ref, copied):
    count, rows = q_ref.shape[:2]
    planes, width, cols = weight_ref.shape
    copies = [
        pltpu.make_async_copy(weights_hbm.at[p : p + 2, :width], weight_ref.at[p : p + 2], copied.at[p // 2])
        for p in range(0, planes, 2)
    ]
    for copy in copies:
        copy.start()
    for p in range(0, planes, 2):
        copies[p // 2].wait()
        query = dot32(rows_ref[...], jnp.concatenate([weight_ref[p], weight_ref[p + 1]], axis=1))
        for k in range(2):
            lanes = slice((p + k) * cols, (p + k + 1) * cols)
            for r in range(count):
                piece = query[r * rows : (r + 1) * rows, k * cols : (k + 1) * cols]
                q_ref[r, :, lanes] = turn(piece, cos_ref[r], sin_ref[r]).astype(BF16)


def project_queries(lines, weights, cosine, signed_sine):
    count, rows, _ = cosine.shape
    width = lines.shape[1]
    planes, _, cols = weights.shape
    vmem = pl.BlockSpec(memory_space=pltpu.VMEM)
    return pl.pallas_call(
        query_kernel,
        in_specs=[vmem, pl.BlockSpec(memory_space=pl.ANY), vmem, vmem],
        out_specs=vmem,
        out_shape=jax.ShapeDtypeStruct((count, rows, planes * cols), BF16),
        scratch_shapes=[pltpu.VMEM((planes, width, cols), BF16), pltpu.SemaphoreType.DMA((planes // 2,))],
        compiler_params=pltpu.CompilerParams(vmem_limit_bytes=40 * 2**20),
        cost_estimate=pl.CostEstimate(
            flops=2 * count * rows * width * planes * cols,
            bytes_accessed=2 * width * (planes * cols + count * rows),
            transcendentals=0,
        ),
    )(lines, weights, cosine, signed_sine)


def attend_kernel(
    numbers, pieces, place_ref, sinks_ref, queries_ref, key_values_ref, halos_ref, *refs
):
    share_refs, (out_ref, att_ref, total_ref) = refs[: len(pieces)], refs[len(pieces) :]
    count, rows = key_values_ref.shape[:2]
    pair = 2 * HD
    kv_heads = key_values_ref.shape[2] // pair
    kv_cols = kv_heads * HD
    pairs = queries_ref.shape[2] // pair
    lane = lax.broadcasted_iota(jnp.int32, (rows, pair), 1)
    low = lane < HD

    def spread(values, head):
        moved = pltpu.roll(values.astype(F32), HD, 1)
        chunk = values.astype(F32)
        lower, upper = (chunk, moved) if head % 2 == 0 else (moved, chunk)
        zero = jnp.zeros_like(chunk)
        return jnp.concatenate(
            [jnp.where(low, lower, zero), jnp.where(low, zero, upper)], axis=0
        ).astype(BF16)

    def side(ref):
        tables = []
        for head in range(kv_heads):
            at = head // 2 * pair
            keys = spread(ref[:, at : at + pair], head)
            values = spread(ref[:, kv_cols + at : kv_cols + at + pair], head)
            tables.append((keys, values))
        return tables

    row = lax.broadcasted_iota(jnp.int32, (rows, rows), 0)
    col = lax.broadcasted_iota(jnp.int32, (rows, rows), 1)
    inside = col <= row
    scale = HD**-0.5
    for i, r in enumerate(numbers):
        own, previous = side(key_values_ref.at[r]), side(halos_ref.at[place_ref[count + r]])
        shown = jnp.logical_or(inside, place_ref[r] == 0)
        for p in range(pairs):
            head = p * kv_heads // pairs
            chunk = queries_ref[r, :, p * pair : (p + 1) * pair]
            scores_own = dot_nt(chunk, own[head][0])
            scores_previous = dot_nt(chunk, previous[head][0])
            probs_own, probs_previous = [], []
            for h in range(2):
                half = slice(h * rows, (h + 1) * rows)
                scores = jnp.where(inside, scores_own[:, half], scores_previous[:, half]) * scale
                scores = jnp.where(shown, scores, -1e30)
                sink = sinks_ref[2 * p + h]
                top = jnp.maximum(jnp.max(scores, axis=1, keepdims=True), sink)
                weights = jnp.exp(scores - top)
                total = jnp.sum(weights, axis=1, keepdims=True) + jnp.exp(sink - top)
                probs = weights / total
                probs_own.append(jnp.where(inside, probs, 0.0).astype(BF16))
                probs_previous.append(jnp.where(inside, 0.0, probs).astype(BF16))
            mixed = dot32(jnp.concatenate(probs_own, axis=1), own[head][1])
            mixed = mixed + dot32(jnp.concatenate(probs_previous, axis=1), previous[head][1])
            att_ref[i * rows : (i + 1) * rows, p * pair : (p + 1) * pair] = mixed.astype(BF16)

    groups, shares, padded, _ = total_ref.shape
    cols = out_ref.shape[1] // (shares * groups)
    attended = att_ref[...]
    for (relative, first), weight_ref in zip(pieces, share_refs):
        size, _, depth = weight_ref.shape
        terms = dot_nt(weight_ref[...].reshape(size * padded, depth), attended)
        for g in range(size):
            total_ref[first + g, place_ref[2 * count + relative]] = terms[g * padded : (g + 1) * padded]
    for g in range(groups):
        for p in range(shares):
            at = (g * shares + p) * cols
            for i in range(len(numbers)):
                out_ref[i, at : at + cols, :] = total_ref[g, p, :cols, i * rows : (i + 1) * rows]


def attend_and_project(numbers, place, sinks, queries, key_values, halos, shares, width):
    rows = queries.shape[1]
    count = len(numbers)
    groups, padded, depth = shares[0][2].shape
    pieces = tuple((relative, first) for relative, first, _ in shares)
    vmem = pl.BlockSpec(memory_space=pltpu.VMEM)
    smem = pl.BlockSpec(memory_space=pltpu.SMEM)
    return pl.pallas_call(
        functools.partial(attend_kernel, numbers, pieces),
        in_specs=[smem, smem] + [vmem] * (3 + len(shares)),
        out_specs=vmem,
        out_shape=jax.ShapeDtypeStruct((count, width, rows), F32),
        scratch_shapes=[
            pltpu.VMEM((count * rows, depth), BF16),
            pltpu.VMEM((groups, PLANE, padded, count * rows), F32),
        ],
        compiler_params=pltpu.CompilerParams(vmem_limit_bytes=40 * 2**20),
        cost_estimate=pl.CostEstimate(
            flops=2 * count * rows * depth * (width + 8 * rows),
            bytes_accessed=2 * width * (depth + 2 * count * rows),
            transcendentals=count * rows * rows * depth // HD,
        ),
    )(place, sinks, queries, key_values, halos, *[weight for _, _, weight in shares])


def project_planes(
    tokens, gain_attn, query_weight, key_weight, value_weight, attn_sinks, out_weight, early
):
    tok_dev, width = tokens.shape
    n_ctx = lax.axis_size("ctx")
    n_z = n_ctx // PLANE
    index = lax.axis_index("ctx")
    z, j = index // PLANE, index % PLANE
    planes = [[PLANE * a + b for b in range(PLANE)] for a in range(n_z)]
    order = list(range(0, n_z, 2)) + list(range(1, n_z, 2))[::-1]
    place_of = [order.index(a) for a in range(n_z)]
    ring, places = jnp.array(order, jnp.int32), jnp.array(place_of, jnp.int32)

    def shift(block, steps):
        return lax.ppermute(block, "ctx", [(i, (i + steps * PLANE) % n_ctx) for i in range(n_ctx)])

    def pass_on(block):
        route = [
            (a * PLANE + b, order[place_of[a] - 1] * PLANE + b) for a in range(n_z) for b in range(PLANE)
        ]
        return lax.ppermute(block, "ctx", route)

    def behind(block):
        route = [(a * PLANE + b, a * PLANE + (b + 1) % PLANE) for a in range(n_z) for b in range(PLANE)]
        return lax.ppermute(block, "ctx", route)

    def swap(block, bits):
        return lax.ppermute(block, "ctx", [(i, i ^ bits) for i in range(n_ctx)])

    tokens_t = tokens.T
    blocks = [rms_norm_t(tokens_t, gain_attn)]

    lanes = query_weight.shape[1]
    share = key_weight.shape[1]
    tiles = -(-width // lanes)
    kv_rows = jnp.concatenate([key_weight.T, value_weight.T], axis=0)
    kv_rows = jnp.pad(kv_rows, ((0, 0), (0, tiles * lanes - width))).reshape(2 * share, tiles, lanes)
    packed = jnp.concatenate(
        [query_weight, kv_rows.transpose(1, 0, 2).reshape(tiles * 2 * share, lanes)], axis=0
    )
    weights = lax.all_gather(packed, "ctx", axis_index_groups=planes)

    cols = out_weight.shape[1]
    padded = -(-cols // 16) * 16
    group_rows = out_weight.shape[0] // n_z
    out_rows = jnp.pad(out_weight.T, ((0, padded - cols), (0, 0)))
    out_rows, blocks[0] = lax.optimization_barrier((out_rows, blocks[0]))
    blocks.append(pass_on(blocks[0]))
    out_groups = jnp.stack(jnp.split(out_rows, n_z, axis=1))
    pieces = [
        shift(lax.dynamic_index_in_dim(out_groups, (z + s) % n_z, 0, keepdims=False), s) if s
        else lax.dynamic_index_in_dim(out_groups, z, 0, keepdims=False)
        for s in range(n_z)
    ]
    ordered = jnp.stack(pieces[::-1] + pieces[:0:-1])
    out_mine = lax.dynamic_slice_in_dim(ordered, n_z - 1 - z, n_z, 0)
    heads = PLANE * query_weight.shape[1] // HD
    sinks = lax.dynamic_slice_in_dim(attn_sinks, z * heads, heads)
    own_rows = jnp.arange(tok_dev, dtype=jnp.int32)
    lane = jnp.arange(2 * HD, dtype=jnp.int32) % HD
    half = HD // 2
    inverse_freq = jnp.exp(-(2.0 * (lane % half).astype(F32) / HD) * math.log(ROPE_BASE))
    mine = places[z]
    block_z = ring[(mine + jnp.arange(n_z, dtype=jnp.int32)) % n_z]
    numbers = block_z * PLANE + j
    angles = (numbers[:, None] * tok_dev + own_rows[None, :]).astype(F32)[:, :, None] * inverse_freq
    signed_sine = jnp.where(lane < half, -jnp.sin(angles), jnp.sin(angles))
    cosine = jnp.cos(angles)
    below = (places[jnp.maximum(block_z - 1, 0)] - mine) % n_z
    previous_at = jnp.where(j == 0, below, jnp.arange(n_z, dtype=jnp.int32))
    relative = jnp.arange(PLANE, dtype=jnp.int32) ^ j
    place = jnp.concatenate([(numbers == 0).astype(jnp.int32), previous_at, relative])
    for _ in range(n_z - 2):
        blocks.append(pass_on(blocks[-1]))
    (blocks[1], cosine, signed_sine, place, sinks, early) = lax.optimization_barrier(
        (blocks[1], cosine, signed_sine, place, sinks, early)
    )
    cut = n_z // 2
    near, far = swap(out_mine, 2), swap(out_mine, 4)
    corner_low, corner_high = swap(near[:cut], 4), swap(far[cut:], 2)
    (near, far, corner_low, corner_high, blocks[-1]) = lax.optimization_barrier(
        (near, far, corner_low, corner_high, blocks[-1])
    )
    shares = []
    for r, first, piece in ((0, 0, out_mine), (2, 0, near), (4, 0, far), (6, 0, corner_low), (6, cut, corner_high)):
        shares += [(r, first, piece), (r + 1, first, swap(piece, 1))]
    lines, key_values = project_keys(blocks, weights, share, cosine, signed_sine)
    halos = behind(key_values)
    queries = project_queries(lines, weights, cosine, signed_sine)

    def parts_of(numbers):
        return attend_and_project(numbers, place, sinks, queries, key_values, halos, shares, width)

    running = parts_of((1,))[0].astype(BF16)
    others = parts_of(tuple(range(2, n_z)) + (0,))
    for i in range(n_z - 2):
        running = (pass_on(running).astype(F32) + others[i]).astype(BF16)
    total = pass_on(running).astype(F32) + others[n_z - 2]
    return (tokens_t.astype(F32) + total).astype(BF16), early


def expert_kernel(tile, hidden, rows_ref, gate_ref, upper_ref, down_ref, out_ref, total_ref):
    step = pl.program_id(0)
    steps = pl.num_programs(0)

    def add(count, initial):
        rows = rows_ref[...]
        gate = dot32(rows, gate_ref[0, :, :count])
        upper = dot32(rows, upper_ref[0, :, :count])
        activation = (gate * jax.nn.sigmoid(1.702 * gate) * (upper + 1.0)).astype(BF16)
        terms = dot32(activation, down_ref[:count, :])
        total_ref[...] = terms if initial else total_ref[...] + terms

    last = hidden - (-(-hidden // tile) - 1) * tile

    @pl.when(step == 0)
    def _():
        add(tile, True)

    @pl.when(jnp.logical_and(step > 0, step < steps - 1))
    def _():
        add(tile, False)

    @pl.when(step == steps - 1)
    def _():
        add(last, False)
        out_ref[...] = total_ref[...].astype(BF16)


def run_expert(rows, gate_up, down):
    count, width = rows.shape
    hidden = down.shape[0]
    tile = 512 if hidden > 1024 else 256
    return pl.pallas_call(
        functools.partial(expert_kernel, tile, hidden),
        grid=(-(-hidden // tile),),
        in_specs=[
            pl.BlockSpec((count, width), lambda f: (0, 0)),
            pl.BlockSpec((1, width, tile), lambda f: (0, 0, f)),
            pl.BlockSpec((1, width, tile), lambda f: (1, 0, f)),
            pl.BlockSpec((tile, width), lambda f: (f, 0)),
        ],
        out_specs=pl.BlockSpec((count, width), lambda f: (0, 0)),
        out_shape=jax.ShapeDtypeStruct((count, width), BF16),
        scratch_shapes=[pltpu.VMEM((count, width), F32)],
        compiler_params=pltpu.CompilerParams(vmem_limit_bytes=52 * 2**20),
        cost_estimate=pl.CostEstimate(
            flops=6 * count * width * hidden,
            bytes_accessed=6 * width * hidden + 4 * count * width,
            transcendentals=count * hidden,
        ),
    )(rows, gate_up, gate_up, down)


def slot_chunks(capacity):
    return [capacity - 8, 8] if capacity > 8 else [capacity]


def dispatch_kernel(chosen_ref, normed_ref, out_ref):
    out_ref[...] = dot_nt(chosen_ref[...], normed_ref[...]).astype(BF16)


def dispatch(chosen, normed):
    total, rows = chosen.shape
    width = normed.shape[0]
    return pl.pallas_call(
        dispatch_kernel,
        out_shape=jax.ShapeDtypeStruct((total, width), BF16),
        compiler_params=pltpu.CompilerParams(vmem_limit_bytes=24 * 2**20),
        cost_estimate=pl.CostEstimate(
            flops=2 * total * rows * width, bytes_accessed=2 * width * (total + rows), transcendentals=0
        ),
    )(chosen, normed)


def routing(route_ids, combine, n_ctx, sizes):
    tok_dev = route_ids.shape[0]
    named = route_ids[:, :, None] == jnp.arange(n_ctx, dtype=jnp.int32)[None, None, :]
    member = jnp.any(named, axis=1)
    weight_of = jnp.sum(jnp.where(named, combine[:, :, None], 0.0), axis=1)
    rows = jnp.arange(tok_dev, dtype=jnp.int32)
    earlier = (rows[:, None] > rows[None, :]).astype(BF16)
    slot_of = jnp.where(member, dot32(earlier, member.astype(BF16)), -1.0).T.astype(BF16)
    weight_of = weight_of.T
    high = weight_of.astype(BF16)
    low = (weight_of - high.astype(F32)).astype(BF16)
    table = jnp.concatenate([slot_of, high, low], axis=1)
    chunks = []
    first = 0
    for size in sizes:
        number = jnp.arange(n_ctx * size, dtype=jnp.int32)[:, None]
        device = (number // size == jnp.arange(n_ctx, dtype=jnp.int32)[None, :]).astype(BF16)
        spread = dot32(device, table)
        chosen = spread[:, :tok_dev] == (first + number % size).astype(F32)
        scale = jnp.where(jnp.concatenate([chosen, chosen], axis=1), spread[:, tok_dev:], 0.0).astype(BF16)
        chunks.append((chosen.astype(BF16), scale))
        first += size
    return chunks


def mix_experts(normed, sizes, matrices, gate_up, down):
    width, tok_dev = normed.shape
    n_ctx, n_exp = lax.axis_size("ctx"), lax.axis_size("exp")
    width_local = width // n_exp

    def tiles(rows, size):
        if size % 8 == 0 or size % 4:
            return rows.reshape(n_ctx, size, -1)
        return rows.reshape(n_ctx, size // 4, 4, -1)

    def exchange(parts):
        return lax.all_to_all(parts, "ctx", split_axis=0, concat_axis=0, tiled=True)

    def in_order(parts, earlier):
        return lax.optimization_barrier((parts, earlier))

    outgoing, received = [], []
    for size, (chosen, _) in zip(sizes, matrices):
        if outgoing:
            chosen, outgoing[-1] = in_order(chosen, outgoing[-1])
        outgoing.append(tiles(dispatch(chosen, normed), size))
    for parts in outgoing:
        if received:
            parts, received[-1] = in_order(parts, received[-1])
        received.append(exchange(parts))

    results = []
    for i, size in enumerate(sizes):
        if i > 1 and i == len(sizes) - 1:
            received[i], results[0] = in_order(received[i], results[0])
        if results:
            received[i], results[-1] = in_order(received[i], results[-1])
        rows_in = received[i].reshape(n_ctx * size, width)
        results.append(tiles(run_expert(rows_in, gate_up, down), size))

    answers = []
    for parts in results:
        if answers:
            parts, answers[-1] = in_order(parts, answers[-1])
        answers.append(exchange(parts))

    moe_out = jnp.zeros((width_local, tok_dev), F32)
    for size, (_, scale), answer in zip(sizes, matrices, answers):
        if n_exp > 1:
            answer = lax.psum_scatter(answer, "exp", scatter_dimension=answer.ndim - 1, tiled=True)
        terms = lax.dot_general(
            answer.reshape(n_ctx * size, width_local), scale, (((0,), (0,)), ((), ())),
            preferred_element_type=F32,
        )
        moe_out = moe_out + terms[:, :tok_dev] + terms[:, tok_dev:]
    return moe_out


def per_device(
    tokens,
    route_ids,
    combine,
    gain_attn,
    gain_moe,
    query_weight,
    key_weight,
    value_weight,
    attn_sinks,
    out_weight,
    gate_up_weight,
    down_weight,
):
    tok_dev, width_local = tokens.shape
    n_ctx = lax.axis_size("ctx")
    n_exp = lax.axis_size("exp")
    capacity = tok_dev * route_ids.shape[1] * 5 // (4 * n_ctx)
    sizes = slot_chunks(capacity)
    matrices = routing(route_ids, combine, n_ctx, sizes)
    by_planes = n_exp == 1 and n_ctx % PLANE == 0 and n_ctx > PLANE
    project = project_planes if by_planes else project_whole
    residual, matrices = project(
        tokens, gain_attn, query_weight, key_weight, value_weight, attn_sinks, out_weight, matrices
    )
    width = residual.shape[0]
    normed_moe = rms_norm_t(residual, gain_moe)
    exp_index = lax.axis_index("exp")
    residual_local = lax.dynamic_slice_in_dim(residual, exp_index * width_local, width_local, 0)

    moe_out = mix_experts(normed_moe, sizes, matrices, gate_up_weight[0], down_weight[0])
    return (residual_local.astype(F32) + moe_out).astype(BF16).T


def solution(mesh):
    return jax.shard_map(
        per_device,
        mesh=mesh,
        in_specs=(
            P("ctx", "exp"),
            P("ctx", None),
            P("ctx", None),
            P(),
            P(),
            P(None, ("exp", "ctx")),
            P(None, ("exp", "ctx")),
            P(None, ("exp", "ctx")),
            P("exp"),
            P("exp", "ctx"),
            P("ctx", None, None, "exp"),
            P("ctx", "exp", None),
        ),
        out_specs=P("ctx", "exp"),
        check_vma=False,
    )
```

```python
import functools
import math

import jax
import jax.numpy as jnp
from jax import lax
from jax.experimental import pallas as pl
from jax.experimental.pallas import tpu as pltpu
from jax.sharding import PartitionSpec as P

HD = 64
WINDOW = 128
EPSILON = 1e-05
ROPE_BASE = 150000.0
PLANE = 8
BF16 = jnp.bfloat16
F32 = jnp.float32


def rms_norm(values, gain):
    wide = values.astype(F32)
    meansq = jnp.mean(wide * wide, axis=-1, keepdims=True)
    return (wide * lax.rsqrt(meansq + EPSILON) * gain).astype(BF16)


def rms_norm_t(values, gain):
    wide = values.astype(F32)
    meansq = jnp.mean(wide * wide, axis=0, keepdims=True)
    return (wide * lax.rsqrt(meansq + EPSILON) * gain[:, None]).astype(BF16)


def rotary(values, angles_pos):
    half_dim = values.shape[-1] // 2
    inverse_freq = jnp.exp(
        -(2.0 * jnp.arange(half_dim, dtype=F32) / values.shape[-1]) * math.log(ROPE_BASE)
    )
    angles = angles_pos[:, None] * inverse_freq[None, :]
    cosine = jnp.cos(angles)[:, None, :]
    sine_part = jnp.sin(angles)[:, None, :]
    first_half = values[..., :half_dim]
    second_half = values[..., half_dim:]
    return jnp.concatenate(
        [
            first_half * cosine - second_half * sine_part,
            second_half * cosine + first_half * sine_part,
        ],
        axis=-1,
    )


def sink_softmax(scores, key_mask, sink_col):
    masked = jnp.where(key_mask, scores, -1e30)
    row_top = jnp.maximum(jnp.max(masked, axis=-1, keepdims=True), sink_col)
    weights = jnp.where(key_mask, jnp.exp(masked - row_top), 0.0)
    denominator = jnp.sum(weights, axis=-1, keepdims=True) + jnp.exp(sink_col - row_top)
    return (weights / denominator).astype(BF16)


def attend_block(query_rows, key_rows, value_rows, query_pos, key_pos, sink_col):
    scores = jnp.einsum(
        "qkgd,skd->kgqs", query_rows, key_rows, preferred_element_type=F32
    ) * HD ** (-0.5)
    distance = query_pos[:, None] - key_pos[None, :]
    key_mask = (distance >= 0) & (distance < WINDOW) & (key_pos >= 0)[None, :]
    weights = sink_softmax(scores, key_mask, sink_col)
    mixed_rows = jnp.einsum("kgqs,skd->qkgd", weights, value_rows, preferred_element_type=F32)
    return mixed_rows.astype(BF16).reshape(query_rows.shape[0], -1)


def dot32(a, b):
    return jnp.dot(a, b, preferred_element_type=F32)


def project_whole(
    tokens, gain_attn, query_weight, key_weight, value_weight, attn_sinks, out_weight, early
):
    tok_dev = tokens.shape[0]
    full_rows = lax.all_gather(tokens, "exp", axis=1, tiled=True)
    normed = rms_norm(full_rows, gain_attn)
    pieces = lax.all_gather((query_weight, key_weight, value_weight), "ctx", axis=1, tiled=True)
    query_lin, key_lin, value_lin = tuple(dot32(normed, piece) for piece in pieces)
    heads_local = query_lin.shape[1] // HD
    kv_local = key_lin.shape[1] // HD
    group_size = heads_local // kv_local
    position_ids = lax.axis_index("ctx") * tok_dev + jnp.arange(tok_dev, dtype=jnp.int32)
    angles_pos = position_ids.astype(F32)
    query = rotary(query_lin.reshape(tok_dev, heads_local, HD), angles_pos).astype(BF16)
    keys_own = rotary(key_lin.reshape(tok_dev, kv_local, HD), angles_pos).astype(BF16)
    key_value = jnp.stack([keys_own.reshape(tok_dev, kv_local * HD), value_lin.astype(BF16)])
    n_ctx = lax.axis_size("ctx")
    previous = lax.ppermute(key_value, "ctx", [(i, i + 1) for i in range(n_ctx - 1)])
    context = jnp.concatenate([previous, key_value], axis=1)
    key_pos = position_ids[0] - WINDOW + jnp.arange(tok_dev + WINDOW, dtype=jnp.int32)
    attended = attend_block(
        query.reshape(tok_dev, kv_local, group_size, HD),
        context[0].reshape(-1, kv_local, HD),
        context[1].reshape(-1, kv_local, HD),
        position_ids,
        key_pos,
        attn_sinks.reshape(kv_local, group_size, 1, 1),
    )
    head_terms = dot32(attended, lax.all_gather(out_weight, "ctx", axis=1, tiled=True))
    attn_proj = lax.psum(head_terms.astype(BF16), "exp").astype(F32)
    return (full_rows.astype(F32) + attn_proj).astype(BF16).T, early


def dot_nt(a, b):
    return lax.dot_general(a, b, (((1,), (1,)), ((), ())), preferred_element_type=F32)


def turn(values, cosine, signed_sine):
    width = values.shape[1]
    half = HD // 2
    lane = lax.broadcasted_iota(jnp.int32, values.shape, 1) % HD
    partner = jnp.where(
        lane < half,
        pltpu.roll(values, width - half, 1),
        pltpu.roll(values, half, 1),
    )
    return values * cosine + partner * signed_sine


def kv_kernel(count, *refs):
    blocks, (weights_hbm, cos_ref, sin_ref, rows_ref, key_value_ref, weight_ref, kv_ref, copied) = refs[:count], refs[count:]
    width, rows = blocks[0].shape
    planes, packed_rows, cols = weight_ref.shape
    copy = pltpu.make_async_copy(weights_hbm.at[:, width : width + packed_rows], weight_ref, copied)
    copy.start()
    for r in range(count):
        rows_ref[r * rows : (r + 1) * rows, :] = blocks[r][...].T
    copy.wait()
    share = kv_ref.shape[2]
    for p in range(planes):
        for tile in range(packed_rows // (2 * share)):
            at, lanes = 2 * share * tile, slice(tile * cols, (tile + 1) * cols)
            for part in range(2):
                kv_ref[part, p, :, lanes] = weight_ref[p, at + part * share : at + (part + 1) * share]
    both = kv_ref[...].reshape(2 * planes * share, kv_ref.shape[3])[:, :width]
    lines = dot_nt(rows_ref[...], both)
    half = planes * share
    for r in range(count):
        piece = lines[r * rows : (r + 1) * rows]
        key_value_ref[r, :, :half] = turn(piece[:, :half], cos_ref[r], sin_ref[r]).astype(BF16)
        key_value_ref[r, :, half:] = piece[:, half:].astype(BF16)


def project_keys(blocks, weights, share, cosine, signed_sine):
    count = len(blocks)
    width, rows = blocks[0].shape
    planes, packed, cols = weights.shape
    kv_cols = 2 * planes * share
    vmem = pl.BlockSpec(memory_space=pltpu.VMEM)
    return pl.pallas_call(
        functools.partial(kv_kernel, count),
        in_specs=[vmem] * count + [pl.BlockSpec(memory_space=pl.ANY), vmem, vmem],
        out_specs=[vmem, vmem],
        out_shape=[
            jax.ShapeDtypeStruct((count * rows, width), BF16),
            jax.ShapeDtypeStruct((count, rows, kv_cols), BF16),
        ],
        scratch_shapes=[
            pltpu.VMEM((planes, packed - width, cols), BF16),
            pltpu.VMEM((2, planes, share, (packed - width) // (2 * share) * cols), BF16),
            pltpu.SemaphoreType.DMA,
        ],
        compiler_params=pltpu.CompilerParams(vmem_limit_bytes=58 * 2**20),
        cost_estimate=pl.CostEstimate(
            flops=2 * count * rows * width * kv_cols,
            bytes_accessed=2 * width * (kv_cols + 2 * count * rows),
            transcendentals=0,
        ),
    )(*blocks, weights, cosine, signed_sine)


def query_kernel(rows_ref, weights_hbm, cos_ref, sin_ref, q_ref, weight_ref, copied):
    count, rows = q_ref.shape[:2]
    planes, width, cols = weight_ref.shape
    copies = [
        pltpu.make_async_copy(weights_hbm.at[p : p + 2, :width], weight_ref.at[p : p + 2], copied.at[p // 2])
        for p in range(0, planes, 2)
    ]
    for copy in copies:
        copy.start()
    for p in range(0, planes, 2):
        copies[p // 2].wait()
        query = dot32(rows_ref[...], jnp.concatenate([weight_ref[p], weight_ref[p + 1]], axis=1))
        for k in range(2):
            lanes = slice((p + k) * cols, (p + k + 1) * cols)
            for r in range(count):
                piece = query[r * rows : (r + 1) * rows, k * cols : (k + 1) * cols]
                q_ref[r, :, lanes] = turn(piece, cos_ref[r], sin_ref[r]).astype(BF16)


def project_queries(lines, weights, cosine, signed_sine):
    count, rows, _ = cosine.shape
    width = lines.shape[1]
    planes, _, cols = weights.shape
    vmem = pl.BlockSpec(memory_space=pltpu.VMEM)
    return pl.pallas_call(
        query_kernel,
        in_specs=[vmem, pl.BlockSpec(memory_space=pl.ANY), vmem, vmem],
        out_specs=vmem,
        out_shape=jax.ShapeDtypeStruct((count, rows, planes * cols), BF16),
        scratch_shapes=[pltpu.VMEM((planes, width, cols), BF16), pltpu.SemaphoreType.DMA((planes // 2,))],
        compiler_params=pltpu.CompilerParams(vmem_limit_bytes=58 * 2**20),
        cost_estimate=pl.CostEstimate(
            flops=2 * count * rows * width * planes * cols,
            bytes_accessed=2 * width * (planes * cols + count * rows),
            transcendentals=0,
        ),
    )(lines, weights, cosine, signed_sine)


def attend_kernel(
    numbers, pieces, place_ref, sinks_ref, queries_ref, key_values_ref, halos_ref, *refs
):
    share_refs, (out_ref, att_ref, total_ref) = refs[: len(pieces)], refs[len(pieces) :]
    count, rows = key_values_ref.shape[:2]
    pair = 2 * HD
    kv_heads = key_values_ref.shape[2] // pair
    kv_cols = kv_heads * HD
    pairs = queries_ref.shape[2] // pair
    lane = lax.broadcasted_iota(jnp.int32, (rows, pair), 1)
    low = lane < HD

    def spread(values, head):
        moved = pltpu.roll(values.astype(F32), HD, 1)
        chunk = values.astype(F32)
        lower, upper = (chunk, moved) if head % 2 == 0 else (moved, chunk)
        zero = jnp.zeros_like(chunk)
        return jnp.concatenate(
            [jnp.where(low, lower, zero), jnp.where(low, zero, upper)], axis=0
        ).astype(BF16)

    def side(ref):
        tables = []
        for head in range(kv_heads):
            at = head // 2 * pair
            keys = spread(ref[:, at : at + pair], head)
            values = spread(ref[:, kv_cols + at : kv_cols + at + pair], head)
            tables.append((keys, values))
        return tables

    row = lax.broadcasted_iota(jnp.int32, (rows, rows), 0)
    col = lax.broadcasted_iota(jnp.int32, (rows, rows), 1)
    inside = col <= row
    scale = HD**-0.5
    for i, r in enumerate(numbers):
        own, previous = side(key_values_ref.at[r]), side(halos_ref.at[place_ref[count + r]])
        shown = jnp.logical_or(inside, place_ref[r] == 0)
        for p in range(pairs):
            head = p * kv_heads // pairs
            chunk = queries_ref[r, :, p * pair : (p + 1) * pair]
            scores_own = dot_nt(chunk, own[head][0])
            scores_previous = dot_nt(chunk, previous[head][0])
            probs_own, probs_previous = [], []
            for h in range(2):
                half = slice(h * rows, (h + 1) * rows)
                scores = jnp.where(inside, scores_own[:, half], scores_previous[:, half]) * scale
                scores = jnp.where(shown, scores, -1e30)
                sink = sinks_ref[2 * p + h]
                top = jnp.maximum(jnp.max(scores, axis=1, keepdims=True), sink)
                weights = jnp.exp(scores - top)
                total = jnp.sum(weights, axis=1, keepdims=True) + jnp.exp(sink - top)
                probs = weights / total
                probs_own.append(jnp.where(inside, probs, 0.0).astype(BF16))
                probs_previous.append(jnp.where(inside, 0.0, probs).astype(BF16))
            mixed = dot32(jnp.concatenate(probs_own, axis=1), own[head][1])
            mixed = mixed + dot32(jnp.concatenate(probs_previous, axis=1), previous[head][1])
            att_ref[i * rows : (i + 1) * rows, p * pair : (p + 1) * pair] = mixed.astype(BF16)

    groups, shares, padded, _ = total_ref.shape
    cols = out_ref.shape[1] // (shares * groups)
    attended = att_ref[...]
    for (relative, first), weight_ref in zip(pieces, share_refs):
        size, _, depth = weight_ref.shape
        terms = dot_nt(weight_ref[...].reshape(size * padded, depth), attended)
        for g in range(size):
            total_ref[first + g, place_ref[2 * count + relative]] = terms[g * padded : (g + 1) * padded]
    for g in range(groups):
        for p in range(shares):
            at = (g * shares + p) * cols
            for i in range(len(numbers)):
                out_ref[i, at : at + cols, :] = total_ref[g, p, :cols, i * rows : (i + 1) * rows]


def attend_and_project(numbers, place, sinks, queries, key_values, halos, shares, width):
    rows = queries.shape[1]
    count = len(numbers)
    groups, padded, depth = shares[0][2].shape
    pieces = tuple((relative, first) for relative, first, _ in shares)
    vmem = pl.BlockSpec(memory_space=pltpu.VMEM)
    smem = pl.BlockSpec(memory_space=pltpu.SMEM)
    return pl.pallas_call(
        functools.partial(attend_kernel, numbers, pieces),
        in_specs=[smem, smem] + [vmem] * (3 + len(shares)),
        out_specs=vmem,
        out_shape=jax.ShapeDtypeStruct((count, width, rows), F32),
        scratch_shapes=[
            pltpu.VMEM((count * rows, depth), BF16),
            pltpu.VMEM((groups, PLANE, padded, count * rows), F32),
        ],
        compiler_params=pltpu.CompilerParams(vmem_limit_bytes=40 * 2**20),
        cost_estimate=pl.CostEstimate(
            flops=2 * count * rows * depth * (width + 8 * rows),
            bytes_accessed=2 * width * (depth + 2 * count * rows),
            transcendentals=count * rows * rows * depth // HD,
        ),
    )(place, sinks, queries, key_values, halos, *[weight for _, _, weight in shares])


def project_planes(
    tokens, gain_attn, query_weight, key_weight, value_weight, attn_sinks, out_weight, early
):
    tok_dev, width = tokens.shape
    n_ctx = lax.axis_size("ctx")
    n_z = n_ctx // PLANE
    index = lax.axis_index("ctx")
    z, j = index // PLANE, index % PLANE
    planes = [[PLANE * a + b for b in range(PLANE)] for a in range(n_z)]
    order = list(range(0, n_z, 2)) + list(range(1, n_z, 2))[::-1]
    place_of = [order.index(a) for a in range(n_z)]
    ring, places = jnp.array(order, jnp.int32), jnp.array(place_of, jnp.int32)

    def shift(block, steps):
        return lax.ppermute(block, "ctx", [(i, (i + steps * PLANE) % n_ctx) for i in range(n_ctx)])

    def pass_on(block):
        route = [
            (a * PLANE + b, order[place_of[a] - 1] * PLANE + b) for a in range(n_z) for b in range(PLANE)
        ]
        return lax.ppermute(block, "ctx", route)

    def behind(block):
        route = [(a * PLANE + b, a * PLANE + (b + 1) % PLANE) for a in range(n_z) for b in range(PLANE)]
        return lax.ppermute(block, "ctx", route)

    def swap(block, bits):
        return lax.ppermute(block, "ctx", [(i, i ^ bits) for i in range(n_ctx)])

    tokens_t = tokens.T
    blocks = [rms_norm_t(tokens_t, gain_attn)]

    lanes = query_weight.shape[1]
    share = key_weight.shape[1]
    tiles = -(-width // lanes)
    kv_rows = jnp.concatenate([key_weight.T, value_weight.T], axis=0)
    kv_rows = jnp.pad(kv_rows, ((0, 0), (0, tiles * lanes - width))).reshape(2 * share, tiles, lanes)
    packed = jnp.concatenate(
        [query_weight, kv_rows.transpose(1, 0, 2).reshape(tiles * 2 * share, lanes)], axis=0
    )
    weights = lax.all_gather(packed, "ctx", axis_index_groups=planes)

    cols = out_weight.shape[1]
    padded = -(-cols // 16) * 16
    group_rows = out_weight.shape[0] // n_z
    out_rows = jnp.pad(out_weight.T, ((0, padded - cols), (0, 0)))
    out_rows, blocks[0] = lax.optimization_barrier((out_rows, blocks[0]))
    blocks.append(pass_on(blocks[0]))
    out_groups = jnp.stack(jnp.split(out_rows, n_z, axis=1))
    pieces = [
        shift(lax.dynamic_index_in_dim(out_groups, (z + s) % n_z, 0, keepdims=False), s) if s
        else lax.dynamic_index_in_dim(out_groups, z, 0, keepdims=False)
        for s in range(n_z)
    ]
    ordered = jnp.stack(pieces[::-1] + pieces[:0:-1])
    out_mine = lax.dynamic_slice_in_dim(ordered, n_z - 1 - z, n_z, 0)
    heads = PLANE * query_weight.shape[1] // HD
    sinks = lax.dynamic_slice_in_dim(attn_sinks, z * heads, heads)
    own_rows = jnp.arange(tok_dev, dtype=jnp.int32)
    lane = jnp.arange(2 * HD, dtype=jnp.int32) % HD
    half = HD // 2
    inverse_freq = jnp.exp(-(2.0 * (lane % half).astype(F32) / HD) * math.log(ROPE_BASE))
    mine = places[z]
    block_z = ring[(mine + jnp.arange(n_z, dtype=jnp.int32)) % n_z]
    numbers = block_z * PLANE + j
    angles = (numbers[:, None] * tok_dev + own_rows[None, :]).astype(F32)[:, :, None] * inverse_freq
    signed_sine = jnp.where(lane < half, -jnp.sin(angles), jnp.sin(angles))
    cosine = jnp.cos(angles)
    below = (places[jnp.maximum(block_z - 1, 0)] - mine) % n_z
    previous_at = jnp.where(j == 0, below, jnp.arange(n_z, dtype=jnp.int32))
    relative = jnp.arange(PLANE, dtype=jnp.int32) ^ j
    place = jnp.concatenate([(numbers == 0).astype(jnp.int32), previous_at, relative])
    for _ in range(n_z - 2):
        blocks.append(pass_on(blocks[-1]))
    (blocks[1], cosine, signed_sine, place, sinks, early) = lax.optimization_barrier(
        (blocks[1], cosine, signed_sine, place, sinks, early)
    )
    cut = n_z // 2
    near, far = swap(out_mine, 2), swap(out_mine, 4)
    corner_low, corner_high = swap(near[:cut], 4), swap(far[cut:], 2)
    (near, far, corner_low, corner_high, blocks[-1]) = lax.optimization_barrier(
        (near, far, corner_low, corner_high, blocks[-1])
    )
    shares = []
    for r, first, piece in ((0, 0, out_mine), (2, 0, near), (4, 0, far), (6, 0, corner_low), (6, cut, corner_high)):
        shares += [(r, first, piece), (r + 1, first, swap(piece, 1))]
    lines, key_values = project_keys(blocks, weights, share, cosine, signed_sine)
    halos = behind(key_values)
    queries = project_queries(lines, weights, cosine, signed_sine)

    def parts_of(numbers):
        return attend_and_project(numbers, place, sinks, queries, key_values, halos, shares, width)

    running = parts_of((1,))[0].astype(BF16)
    others = parts_of(tuple(range(2, n_z)) + (0,))
    for i in range(n_z - 2):
        running = (pass_on(running).astype(F32) + others[i]).astype(BF16)
    total = pass_on(running).astype(F32) + others[n_z - 2]
    return (tokens_t.astype(F32) + total).astype(BF16), early


def expert_kernel(tile, hidden, rows_ref, gate_ref, upper_ref, down_ref, out_ref, total_ref, flat_ref):
    step = pl.program_id(0)
    steps = pl.num_programs(0)

    def add(count, initial):
        rows = flat_ref[...]
        gate = dot32(rows, gate_ref[0, :, :count])
        upper = dot32(rows, upper_ref[0, :, :count])
        activation = (gate * jax.nn.sigmoid(1.702 * gate) * (upper + 1.0)).astype(BF16)
        terms = dot32(activation, down_ref[:count, :])
        total_ref[...] = terms if initial else total_ref[...] + terms

    last = hidden - (-(-hidden // tile) - 1) * tile

    @pl.when(step == 0)
    def _():
        flat_ref[...] = rows_ref[...].reshape(flat_ref.shape)
        add(tile, True)

    @pl.when(jnp.logical_and(step > 0, step < steps - 1))
    def _():
        add(tile, False)

    @pl.when(step == steps - 1)
    def _():
        add(last, False)
        out_ref[...] = total_ref[...].astype(BF16).reshape(out_ref.shape)


def run_expert(rows, gate_up, down):
    width = rows.shape[-1]
    count = rows.size // width
    hidden = down.shape[0]
    tile = 512 if hidden > 1024 else 256
    whole = pl.BlockSpec(rows.shape, lambda f: (0,) * rows.ndim)
    return pl.pallas_call(
        functools.partial(expert_kernel, tile, hidden),
        grid=(-(-hidden // tile),),
        in_specs=[
            whole,
            pl.BlockSpec((1, width, tile), lambda f: (0, 0, f)),
            pl.BlockSpec((1, width, tile), lambda f: (1, 0, f)),
            pl.BlockSpec((tile, width), lambda f: (f, 0)),
        ],
        out_specs=whole,
        out_shape=jax.ShapeDtypeStruct(rows.shape, BF16),
        scratch_shapes=[pltpu.VMEM((count, width), F32), pltpu.VMEM((count, width), BF16)],
        compiler_params=pltpu.CompilerParams(vmem_limit_bytes=52 * 2**20),
        cost_estimate=pl.CostEstimate(
            flops=6 * count * width * hidden,
            bytes_accessed=6 * width * hidden + 4 * count * width,
            transcendentals=count * hidden,
        ),
    )(rows, gate_up, gate_up, down)


def slot_chunks(capacity):
    return [capacity - 8, 8] if capacity > 8 else [capacity]


def dispatch_kernel(chosen_ref, normed_ref, out_ref):
    out_ref[...] = dot_nt(chosen_ref[...], normed_ref[...]).astype(BF16).reshape(out_ref.shape)


def dispatch(chosen, normed, size):
    total, rows = chosen.shape
    width = normed.shape[0]
    shape = (total // 4, 4, width) if size % 8 and size % 4 == 0 else (total, width)
    return pl.pallas_call(
        dispatch_kernel,
        out_shape=jax.ShapeDtypeStruct(shape, BF16),
        compiler_params=pltpu.CompilerParams(vmem_limit_bytes=24 * 2**20),
        cost_estimate=pl.CostEstimate(
            flops=2 * total * rows * width, bytes_accessed=2 * width * (total + rows), transcendentals=0
        ),
    )(chosen, normed)


def routing(route_ids, combine, n_ctx, sizes):
    tok_dev = route_ids.shape[0]
    named = route_ids[:, :, None] == jnp.arange(n_ctx, dtype=jnp.int32)[None, None, :]
    member = jnp.any(named, axis=1)
    weight_of = jnp.sum(jnp.where(named, combine[:, :, None], 0.0), axis=1)
    rows = jnp.arange(tok_dev, dtype=jnp.int32)
    earlier = (rows[:, None] > rows[None, :]).astype(BF16)
    slot_of = jnp.where(member, dot32(earlier, member.astype(BF16)), -1.0).T.astype(BF16)
    weight_of = weight_of.T
    high = weight_of.astype(BF16)
    low = (weight_of - high.astype(F32)).astype(BF16)
    table = jnp.concatenate([slot_of, high, low], axis=1)
    chunks = []
    first = 0
    for size in sizes:
        number = jnp.arange(n_ctx * size, dtype=jnp.int32)[:, None]
        device = (number // size == jnp.arange(n_ctx, dtype=jnp.int32)[None, :]).astype(BF16)
        spread = dot32(device, table)
        chosen = spread[:, :tok_dev] == (first + number % size).astype(F32)
        scale = jnp.where(jnp.concatenate([chosen, chosen], axis=1), spread[:, tok_dev:], 0.0).astype(BF16)
        chunks.append((chosen.astype(BF16), scale))
        first += size
    return chunks


def mix_experts(normed, sizes, matrices, gate_up, down):
    width, tok_dev = normed.shape
    n_ctx, n_exp = lax.axis_size("ctx"), lax.axis_size("exp")
    width_local = width // n_exp

    def exchange(parts):
        by_device = parts.reshape((n_ctx, -1) + parts.shape[1:])
        return lax.all_to_all(by_device, "ctx", split_axis=0, concat_axis=0, tiled=True)

    def in_order(parts, earlier):
        return lax.optimization_barrier((parts, earlier))

    outgoing, received = [], []
    for size, (chosen, _) in zip(sizes, matrices):
        if outgoing:
            chosen, outgoing[-1] = in_order(chosen, outgoing[-1])
        outgoing.append(dispatch(chosen, normed, size))
    for parts in outgoing:
        if received:
            parts, received[-1] = in_order(parts, received[-1])
        received.append(exchange(parts))

    results = []
    for i, size in enumerate(sizes):
        if i > 1 and i == len(sizes) - 1:
            received[i], results[0] = in_order(received[i], results[0])
        if results:
            received[i], results[-1] = in_order(received[i], results[-1])
        rows_in = received[i].reshape(outgoing[i].shape)
        results.append(run_expert(rows_in, gate_up, down))

    answers = []
    for parts in results:
        if answers:
            parts, answers[-1] = in_order(parts, answers[-1])
        answers.append(exchange(parts))

    moe_out = jnp.zeros((width_local, tok_dev), F32)
    for size, (_, scale), answer in zip(sizes, matrices, answers):
        if n_exp > 1:
            answer = lax.psum_scatter(answer, "exp", scatter_dimension=answer.ndim - 1, tiled=True)
        terms = lax.dot_general(
            answer.reshape(n_ctx * size, width_local), scale, (((0,), (0,)), ((), ())),
            preferred_element_type=F32,
        )
        moe_out = moe_out + terms[:, :tok_dev] + terms[:, tok_dev:]
    return moe_out


def per_device(
    tokens,
    route_ids,
    combine,
    gain_attn,
    gain_moe,
    query_weight,
    key_weight,
    value_weight,
    attn_sinks,
    out_weight,
    gate_up_weight,
    down_weight,
):
    tok_dev, width_local = tokens.shape
    n_ctx = lax.axis_size("ctx")
    n_exp = lax.axis_size("exp")
    capacity = tok_dev * route_ids.shape[1] * 5 // (4 * n_ctx)
    sizes = slot_chunks(capacity)
    matrices = routing(route_ids, combine, n_ctx, sizes)
    by_planes = n_exp == 1 and n_ctx % PLANE == 0 and n_ctx > PLANE
    project = project_planes if by_planes else project_whole
    residual, matrices = project(
        tokens, gain_attn, query_weight, key_weight, value_weight, attn_sinks, out_weight, matrices
    )
    width = residual.shape[0]
    normed_moe = rms_norm_t(residual, gain_moe)
    exp_index = lax.axis_index("exp")
    residual_local = lax.dynamic_slice_in_dim(residual, exp_index * width_local, width_local, 0)

    moe_out = mix_experts(normed_moe, sizes, matrices, gate_up_weight[0], down_weight[0])
    return (residual_local.astype(F32) + moe_out).astype(BF16).T


def solution(mesh):
    return jax.shard_map(
        per_device,
        mesh=mesh,
        in_specs=(
            P("ctx", "exp"),
            P("ctx", None),
            P("ctx", None),
            P(),
            P(),
            P(None, ("exp", "ctx")),
            P(None, ("exp", "ctx")),
            P(None, ("exp", "ctx")),
            P("exp"),
            P("exp", "ctx"),
            P("ctx", None, None, "exp"),
            P("ctx", "exp", None),
        ),
        out_specs=P("ctx", "exp"),
        check_vma=False,
    )
```

```python
import functools
import math

import jax
import jax.numpy as jnp
from jax import lax
from jax.experimental import pallas as pl
from jax.experimental.pallas import tpu as pltpu
from jax.sharding import PartitionSpec as P

HD = 64
WINDOW = 128
EPSILON = 1e-05
ROPE_BASE = 150000.0
PLANE = 8
BF16 = jnp.bfloat16
F32 = jnp.float32


def rms_norm(values, gain):
    wide = values.astype(F32)
    meansq = jnp.mean(wide * wide, axis=-1, keepdims=True)
    return (wide * lax.rsqrt(meansq + EPSILON) * gain).astype(BF16)


def rms_norm_t(values, gain):
    wide = values.astype(F32)
    meansq = jnp.mean(wide * wide, axis=0, keepdims=True)
    return (wide * lax.rsqrt(meansq + EPSILON) * gain[:, None]).astype(BF16)


def rotary(values, angles_pos):
    half_dim = values.shape[-1] // 2
    inverse_freq = jnp.exp(
        -(2.0 * jnp.arange(half_dim, dtype=F32) / values.shape[-1]) * math.log(ROPE_BASE)
    )
    angles = angles_pos[:, None] * inverse_freq[None, :]
    cosine = jnp.cos(angles)[:, None, :]
    sine_part = jnp.sin(angles)[:, None, :]
    first_half = values[..., :half_dim]
    second_half = values[..., half_dim:]
    return jnp.concatenate(
        [
            first_half * cosine - second_half * sine_part,
            second_half * cosine + first_half * sine_part,
        ],
        axis=-1,
    )


def sink_softmax(scores, key_mask, sink_col):
    masked = jnp.where(key_mask, scores, -1e30)
    row_top = jnp.maximum(jnp.max(masked, axis=-1, keepdims=True), sink_col)
    weights = jnp.where(key_mask, jnp.exp(masked - row_top), 0.0)
    denominator = jnp.sum(weights, axis=-1, keepdims=True) + jnp.exp(sink_col - row_top)
    return (weights / denominator).astype(BF16)


def attend_block(query_rows, key_rows, value_rows, query_pos, key_pos, sink_col):
    scores = jnp.einsum(
        "qkgd,skd->kgqs", query_rows, key_rows, preferred_element_type=F32
    ) * HD ** (-0.5)
    distance = query_pos[:, None] - key_pos[None, :]
    key_mask = (distance >= 0) & (distance < WINDOW) & (key_pos >= 0)[None, :]
    weights = sink_softmax(scores, key_mask, sink_col)
    mixed_rows = jnp.einsum("kgqs,skd->qkgd", weights, value_rows, preferred_element_type=F32)
    return mixed_rows.astype(BF16).reshape(query_rows.shape[0], -1)


def dot32(a, b):
    return jnp.dot(a, b, preferred_element_type=F32)


def project_whole(
    tokens, gain_attn, query_weight, key_weight, value_weight, attn_sinks, out_weight, early
):
    tok_dev = tokens.shape[0]
    full_rows = lax.all_gather(tokens, "exp", axis=1, tiled=True)
    normed = rms_norm(full_rows, gain_attn)
    pieces = lax.all_gather((query_weight, key_weight, value_weight), "ctx", axis=1, tiled=True)
    query_lin, key_lin, value_lin = tuple(dot32(normed, piece) for piece in pieces)
    heads_local = query_lin.shape[1] // HD
    kv_local = key_lin.shape[1] // HD
    group_size = heads_local // kv_local
    position_ids = lax.axis_index("ctx") * tok_dev + jnp.arange(tok_dev, dtype=jnp.int32)
    angles_pos = position_ids.astype(F32)
    query = rotary(query_lin.reshape(tok_dev, heads_local, HD), angles_pos).astype(BF16)
    keys_own = rotary(key_lin.reshape(tok_dev, kv_local, HD), angles_pos).astype(BF16)
    key_value = jnp.stack([keys_own.reshape(tok_dev, kv_local * HD), value_lin.astype(BF16)])
    n_ctx = lax.axis_size("ctx")
    previous = lax.ppermute(key_value, "ctx", [(i, i + 1) for i in range(n_ctx - 1)])
    context = jnp.concatenate([previous, key_value], axis=1)
    key_pos = position_ids[0] - WINDOW + jnp.arange(tok_dev + WINDOW, dtype=jnp.int32)
    attended = attend_block(
        query.reshape(tok_dev, kv_local, group_size, HD),
        context[0].reshape(-1, kv_local, HD),
        context[1].reshape(-1, kv_local, HD),
        position_ids,
        key_pos,
        attn_sinks.reshape(kv_local, group_size, 1, 1),
    )
    head_terms = dot32(attended, lax.all_gather(out_weight, "ctx", axis=1, tiled=True))
    attn_proj = lax.psum(head_terms.astype(BF16), "exp").astype(F32)
    return (full_rows.astype(F32) + attn_proj).astype(BF16).T, early


def dot_nt(a, b):
    return lax.dot_general(a, b, (((1,), (1,)), ((), ())), preferred_element_type=F32)


def turn(values, cosine, signed_sine):
    width = values.shape[1]
    half = HD // 2
    lane = lax.broadcasted_iota(jnp.int32, values.shape, 1) % HD
    partner = jnp.where(
        lane < half,
        pltpu.roll(values, width - half, 1),
        pltpu.roll(values, half, 1),
    )
    return values * cosine + partner * signed_sine


def qkv_kernel(count, *refs):
    blocks, (weights_hbm, cos_ref, sin_ref, q_ref, key_value_ref, rows_ref, weight_ref, kv_ref, copied) = refs[:count], refs[count:]
    width, rows = blocks[0].shape
    planes, packed, cols = weight_ref.shape
    share = kv_ref.shape[2]
    key_copies = [
        pltpu.make_async_copy(
            weights_hbm.at[p, width:packed], weight_ref.at[p, width:packed], copied.at[planes + p]
        )
        for p in range(planes)
    ]
    query_copies = [
        pltpu.make_async_copy(weights_hbm.at[p, :width], weight_ref.at[p, :width], copied.at[p])
        for p in range(planes)
    ]
    for copy in key_copies + query_copies:
        copy.start()
    for r in range(count):
        rows_ref[r * rows : (r + 1) * rows, :] = blocks[r][...].T

    for p in range(planes):
        key_copies[p].wait()
        for tile in range((packed - width) // (2 * share)):
            at, lanes = width + 2 * share * tile, slice(tile * cols, (tile + 1) * cols)
            for part in range(2):
                kv_ref[part, p, :, lanes] = weight_ref[p, at + part * share : at + (part + 1) * share]
    both = kv_ref[...].reshape(2 * planes * share, kv_ref.shape[3])[:, :width]
    lines = dot_nt(rows_ref[...], both)
    half = planes * share
    for r in range(count):
        piece = lines[r * rows : (r + 1) * rows]
        key_value_ref[r, :, :half] = turn(piece[:, :half], cos_ref[r], sin_ref[r]).astype(BF16)
        key_value_ref[r, :, half:] = piece[:, half:].astype(BF16)

    for p in range(0, planes, 2):
        query_copies[p].wait()
        query_copies[p + 1].wait()
        weight = jnp.concatenate([weight_ref[p, :width], weight_ref[p + 1, :width]], axis=1)
        query = dot32(rows_ref[...], weight)
        for k in range(2):
            lanes = slice((p + k) * cols, (p + k + 1) * cols)
            for r in range(count):
                piece = query[r * rows : (r + 1) * rows, k * cols : (k + 1) * cols]
                q_ref[r, :, lanes] = turn(piece, cos_ref[r], sin_ref[r]).astype(BF16)


def project_blocks(blocks, weights, share, cosine, signed_sine):
    count = len(blocks)
    width, rows = blocks[0].shape
    planes, packed, cols = weights.shape
    kv_cols = 2 * planes * share
    vmem = pl.BlockSpec(memory_space=pltpu.VMEM)
    return pl.pallas_call(
        functools.partial(qkv_kernel, count),
        in_specs=[vmem] * count + [pl.BlockSpec(memory_space=pl.ANY), vmem, vmem],
        out_specs=[vmem, vmem],
        out_shape=[
            jax.ShapeDtypeStruct((count, rows, planes * cols), BF16),
            jax.ShapeDtypeStruct((count, rows, kv_cols), BF16),
        ],
        scratch_shapes=[
            pltpu.VMEM((count * rows, width), BF16),
            pltpu.VMEM(weights.shape, BF16),
            pltpu.VMEM((2, planes, share, (packed - width) // (2 * share) * cols), BF16),
            pltpu.SemaphoreType.DMA((2 * planes,)),
        ],
        compiler_params=pltpu.CompilerParams(vmem_limit_bytes=58 * 2**20),
        cost_estimate=pl.CostEstimate(
            flops=2 * count * rows * width * (planes * cols + kv_cols),
            bytes_accessed=2 * width * (planes * cols + kv_cols + count * rows),
            transcendentals=0,
        ),
    )(*blocks, weights, cosine, signed_sine)


def attend_kernel(
    numbers, pieces, place_ref, sinks_ref, queries_ref, key_values_ref, halos_ref, *refs
):
    share_refs, (out_ref, att_ref, total_ref) = refs[: len(pieces)], refs[len(pieces) :]
    count, rows = key_values_ref.shape[:2]
    pair = 2 * HD
    kv_heads = key_values_ref.shape[2] // pair
    kv_cols = kv_heads * HD
    pairs = queries_ref.shape[2] // pair
    lane = lax.broadcasted_iota(jnp.int32, (rows, pair), 1)
    low = lane < HD

    def spread(values, head):
        moved = pltpu.roll(values.astype(F32), HD, 1)
        chunk = values.astype(F32)
        lower, upper = (chunk, moved) if head % 2 == 0 else (moved, chunk)
        zero = jnp.zeros_like(chunk)
        return jnp.concatenate(
            [jnp.where(low, lower, zero), jnp.where(low, zero, upper)], axis=0
        ).astype(BF16)

    def side(ref):
        tables = []
        for head in range(kv_heads):
            at = head // 2 * pair
            keys = spread(ref[:, at : at + pair], head)
            values = spread(ref[:, kv_cols + at : kv_cols + at + pair], head)
            tables.append((keys, values))
        return tables

    row = lax.broadcasted_iota(jnp.int32, (rows, rows), 0)
    col = lax.broadcasted_iota(jnp.int32, (rows, rows), 1)
    inside = col <= row
    scale = HD**-0.5
    for i, r in enumerate(numbers):
        own, previous = side(key_values_ref.at[r]), side(halos_ref.at[place_ref[count + r]])
        shown = jnp.logical_or(inside, place_ref[r] == 0)
        for p in range(pairs):
            head = p * kv_heads // pairs
            chunk = queries_ref[r, :, p * pair : (p + 1) * pair]
            scores_own = dot_nt(chunk, own[head][0])
            scores_previous = dot_nt(chunk, previous[head][0])
            probs_own, probs_previous = [], []
            for h in range(2):
                half = slice(h * rows, (h + 1) * rows)
                scores = jnp.where(inside, scores_own[:, half], scores_previous[:, half]) * scale
                scores = jnp.where(shown, scores, -1e30)
                sink = sinks_ref[2 * p + h]
                top = jnp.maximum(jnp.max(scores, axis=1, keepdims=True), sink)
                weights = jnp.exp(scores - top)
                total = jnp.sum(weights, axis=1, keepdims=True) + jnp.exp(sink - top)
                probs = weights / total
                probs_own.append(jnp.where(inside, probs, 0.0).astype(BF16))
                probs_previous.append(jnp.where(inside, 0.0, probs).astype(BF16))
            mixed = dot32(jnp.concatenate(probs_own, axis=1), own[head][1])
            mixed = mixed + dot32(jnp.concatenate(probs_previous, axis=1), previous[head][1])
            att_ref[i * rows : (i + 1) * rows, p * pair : (p + 1) * pair] = mixed.astype(BF16)

    groups, shares, padded, _ = total_ref.shape
    cols = out_ref.shape[1] // (shares * groups)
    attended = att_ref[...]
    for (relative, first), weight_ref in zip(pieces, share_refs):
        size, _, depth = weight_ref.shape
        terms = dot_nt(weight_ref[...].reshape(size * padded, depth), attended)
        for g in range(size):
            total_ref[first + g, place_ref[2 * count + relative]] = terms[g * padded : (g + 1) * padded]
    for g in range(groups):
        for p in range(shares):
            at = (g * shares + p) * cols
            for i in range(len(numbers)):
                out_ref[i, at : at + cols, :] = total_ref[g, p, :cols, i * rows : (i + 1) * rows]


def attend_and_project(numbers, place, sinks, queries, key_values, halos, shares, width):
    rows = queries.shape[1]
    count = len(numbers)
    groups, padded, depth = shares[0][2].shape
    pieces = tuple((relative, first) for relative, first, _ in shares)
    vmem = pl.BlockSpec(memory_space=pltpu.VMEM)
    smem = pl.BlockSpec(memory_space=pltpu.SMEM)
    return pl.pallas_call(
        functools.partial(attend_kernel, numbers, pieces),
        in_specs=[smem, smem] + [vmem] * (3 + len(shares)),
        out_specs=vmem,
        out_shape=jax.ShapeDtypeStruct((count, width, rows), F32),
        scratch_shapes=[
            pltpu.VMEM((count * rows, depth), BF16),
            pltpu.VMEM((groups, PLANE, padded, count * rows), F32),
        ],
        compiler_params=pltpu.CompilerParams(vmem_limit_bytes=40 * 2**20),
        cost_estimate=pl.CostEstimate(
            flops=2 * count * rows * depth * (width + 8 * rows),
            bytes_accessed=2 * width * (depth + 2 * count * rows),
            transcendentals=count * rows * rows * depth // HD,
        ),
    )(place, sinks, queries, key_values, halos, *[weight for _, _, weight in shares])


def project_planes(
    tokens, gain_attn, query_weight, key_weight, value_weight, attn_sinks, out_weight, early
):
    tok_dev, width = tokens.shape
    n_ctx = lax.axis_size("ctx")
    n_z = n_ctx // PLANE
    index = lax.axis_index("ctx")
    z, j = index // PLANE, index % PLANE
    planes = [[PLANE * a + b for b in range(PLANE)] for a in range(n_z)]
    order = list(range(0, n_z, 2)) + list(range(1, n_z, 2))[::-1]
    place_of = [order.index(a) for a in range(n_z)]
    ring, places = jnp.array(order, jnp.int32), jnp.array(place_of, jnp.int32)

    def shift(block, steps):
        return lax.ppermute(block, "ctx", [(i, (i + steps * PLANE) % n_ctx) for i in range(n_ctx)])

    def pass_on(block):
        route = [
            (a * PLANE + b, order[place_of[a] - 1] * PLANE + b) for a in range(n_z) for b in range(PLANE)
        ]
        return lax.ppermute(block, "ctx", route)

    def behind(block):
        route = [(a * PLANE + b, a * PLANE + (b + 1) % PLANE) for a in range(n_z) for b in range(PLANE)]
        return lax.ppermute(block, "ctx", route)

    def swap(block, bits):
        return lax.ppermute(block, "ctx", [(i, i ^ bits) for i in range(n_ctx)])

    tokens_t = tokens.T
    blocks = [rms_norm_t(tokens_t, gain_attn)]

    lanes = query_weight.shape[1]
    share = key_weight.shape[1]
    tiles = -(-width // lanes)
    kv_rows = jnp.concatenate([key_weight.T, value_weight.T], axis=0)
    kv_rows = jnp.pad(kv_rows, ((0, 0), (0, tiles * lanes - width))).reshape(2 * share, tiles, lanes)
    packed = jnp.concatenate(
        [query_weight, kv_rows.transpose(1, 0, 2).reshape(tiles * 2 * share, lanes)], axis=0
    )
    weights = lax.all_gather(packed, "ctx", axis_index_groups=planes)

    cols = out_weight.shape[1]
    padded = -(-cols // 16) * 16
    group_rows = out_weight.shape[0] // n_z
    out_rows = jnp.pad(out_weight.T, ((0, padded - cols), (0, 0)))
    out_rows, blocks[0] = lax.optimization_barrier((out_rows, blocks[0]))
    blocks.append(pass_on(blocks[0]))
    out_groups = jnp.stack(jnp.split(out_rows, n_z, axis=1))
    pieces = [
        shift(lax.dynamic_index_in_dim(out_groups, (z + s) % n_z, 0, keepdims=False), s) if s
        else lax.dynamic_index_in_dim(out_groups, z, 0, keepdims=False)
        for s in range(n_z)
    ]
    ordered = jnp.stack(pieces[::-1] + pieces[:0:-1])
    out_mine = lax.dynamic_slice_in_dim(ordered, n_z - 1 - z, n_z, 0)
    heads = PLANE * query_weight.shape[1] // HD
    sinks = lax.dynamic_slice_in_dim(attn_sinks, z * heads, heads)
    own_rows = jnp.arange(tok_dev, dtype=jnp.int32)
    lane = jnp.arange(2 * HD, dtype=jnp.int32) % HD
    half = HD // 2
    inverse_freq = jnp.exp(-(2.0 * (lane % half).astype(F32) / HD) * math.log(ROPE_BASE))
    mine = places[z]
    block_z = ring[(mine + jnp.arange(n_z, dtype=jnp.int32)) % n_z]
    numbers = block_z * PLANE + j
    angles = (numbers[:, None] * tok_dev + own_rows[None, :]).astype(F32)[:, :, None] * inverse_freq
    signed_sine = jnp.where(lane < half, -jnp.sin(angles), jnp.sin(angles))
    cosine = jnp.cos(angles)
    below = (places[jnp.maximum(block_z - 1, 0)] - mine) % n_z
    previous_at = jnp.where(j == 0, below, jnp.arange(n_z, dtype=jnp.int32))
    relative = jnp.arange(PLANE, dtype=jnp.int32) ^ j
    place = jnp.concatenate([(numbers == 0).astype(jnp.int32), previous_at, relative])
    for _ in range(n_z - 2):
        blocks.append(pass_on(blocks[-1]))
    cut = n_z // 2
    near, far = swap(out_mine, 2), swap(out_mine, 4)
    (near, far, cosine, signed_sine, place, sinks, early) = lax.optimization_barrier(
        (near, far, cosine, signed_sine, place, sinks, early)
    )
    corner_low, corner_high = swap(near[:cut], 4), swap(far[cut:], 2)
    (near, far, corner_low, corner_high, blocks[-1]) = lax.optimization_barrier(
        (near, far, corner_low, corner_high, blocks[-1])
    )
    shares = []
    for r, first, piece in ((0, 0, out_mine), (2, 0, near), (4, 0, far), (6, 0, corner_low), (6, cut, corner_high)):
        shares += [(r, first, piece), (r + 1, first, swap(piece, 1))]
    queries, key_values = project_blocks(blocks, weights, share, cosine, signed_sine)
    halos = behind(key_values)

    def parts_of(numbers):
        return attend_and_project(numbers, place, sinks, queries, key_values, halos, shares, width)

    cuts = (slice(0, width // 32 * 16), slice(width // 32 * 16, width))
    first = parts_of((1,))[0]
    others = parts_of(tuple(range(2, n_z)) + (0,))
    halves = [first[cut].astype(BF16) for cut in cuts]
    for i in range(n_z - 1):
        terms = others[i] + tokens_t.astype(F32) if i == n_z - 2 else others[i]
        sums = []
        for half, cut in zip(halves, cuts):
            arrived = pass_on(half)
            if sums:
                arrived, _ = lax.optimization_barrier((arrived, sums[-1]))
            sums.append((arrived.astype(F32) + terms[cut]).astype(BF16))
        halves = sums
    return jnp.concatenate(halves, axis=0), early


def expert_kernel(tile, hidden, rows_ref, gate_ref, upper_ref, down_ref, out_ref, total_ref, flat_ref):
    step = pl.program_id(0)
    steps = pl.num_programs(0)

    def add(count, initial):
        rows = flat_ref[...]
        gate = dot32(rows, gate_ref[0, :, :count])
        upper = dot32(rows, upper_ref[0, :, :count])
        activation = (gate * jax.nn.sigmoid(1.702 * gate) * (upper + 1.0)).astype(BF16)
        terms = dot32(activation, down_ref[:count, :])
        total_ref[...] = terms if initial else total_ref[...] + terms

    last = hidden - (-(-hidden // tile) - 1) * tile

    @pl.when(step == 0)
    def _():
        flat_ref[...] = rows_ref[...].reshape(flat_ref.shape)
        add(tile, True)

    @pl.when(jnp.logical_and(step > 0, step < steps - 1))
    def _():
        add(tile, False)

    @pl.when(step == steps - 1)
    def _():
        add(last, False)
        out_ref[...] = total_ref[...].astype(BF16).reshape(out_ref.shape)


def run_expert(rows, gate_up, down):
    width = rows.shape[-1]
    count = rows.size // width
    hidden = down.shape[0]
    tile = 512 if hidden > 1024 else 256
    whole = pl.BlockSpec(rows.shape, lambda f: (0,) * rows.ndim)
    return pl.pallas_call(
        functools.partial(expert_kernel, tile, hidden),
        grid=(-(-hidden // tile),),
        in_specs=[
            whole,
            pl.BlockSpec((1, width, tile), lambda f: (0, 0, f)),
            pl.BlockSpec((1, width, tile), lambda f: (1, 0, f)),
            pl.BlockSpec((tile, width), lambda f: (f, 0)),
        ],
        out_specs=whole,
        out_shape=jax.ShapeDtypeStruct(rows.shape, BF16),
        scratch_shapes=[pltpu.VMEM((count, width), F32), pltpu.VMEM((count, width), BF16)],
        compiler_params=pltpu.CompilerParams(vmem_limit_bytes=52 * 2**20),
        cost_estimate=pl.CostEstimate(
            flops=6 * count * width * hidden,
            bytes_accessed=6 * width * hidden + 4 * count * width,
            transcendentals=count * hidden,
        ),
    )(rows, gate_up, gate_up, down)


def slot_chunks(capacity):
    return [capacity - 8, 8] if capacity > 8 else [capacity]


def dispatch_kernel(chosen_ref, normed_ref, out_ref):
    out_ref[...] = dot_nt(chosen_ref[...], normed_ref[...]).astype(BF16).reshape(out_ref.shape)


def dispatch(chosen, normed, size):
    total, rows = chosen.shape
    width = normed.shape[0]
    shape = (total // 4, 4, width) if size % 8 and size % 4 == 0 else (total, width)
    return pl.pallas_call(
        dispatch_kernel,
        out_shape=jax.ShapeDtypeStruct(shape, BF16),
        compiler_params=pltpu.CompilerParams(vmem_limit_bytes=24 * 2**20),
        cost_estimate=pl.CostEstimate(
            flops=2 * total * rows * width, bytes_accessed=2 * width * (total + rows), transcendentals=0
        ),
    )(chosen, normed)


def routing(route_ids, combine, n_ctx, sizes):
    tok_dev = route_ids.shape[0]
    named = route_ids[:, :, None] == jnp.arange(n_ctx, dtype=jnp.int32)[None, None, :]
    member = jnp.any(named, axis=1)
    weight_of = jnp.sum(jnp.where(named, combine[:, :, None], 0.0), axis=1)
    rows = jnp.arange(tok_dev, dtype=jnp.int32)
    earlier = (rows[:, None] > rows[None, :]).astype(BF16)
    slot_of = jnp.where(member, dot32(earlier, member.astype(BF16)), -1.0).T.astype(BF16)
    weight_of = weight_of.T
    high = weight_of.astype(BF16)
    low = (weight_of - high.astype(F32)).astype(BF16)
    table = jnp.concatenate([slot_of, high, low], axis=1)
    chunks = []
    first = 0
    for size in sizes:
        number = jnp.arange(n_ctx * size, dtype=jnp.int32)[:, None]
        device = (number // size == jnp.arange(n_ctx, dtype=jnp.int32)[None, :]).astype(BF16)
        spread = dot32(device, table)
        chosen = spread[:, :tok_dev] == (first + number % size).astype(F32)
        scale = jnp.where(jnp.concatenate([chosen, chosen], axis=1), spread[:, tok_dev:], 0.0).astype(BF16)
        chunks.append((chosen.astype(BF16), scale))
        first += size
    return chunks


def mix_experts(normed, sizes, matrices, gate_up, down):
    width, tok_dev = normed.shape
    n_ctx, n_exp = lax.axis_size("ctx"), lax.axis_size("exp")
    width_local = width // n_exp

    def exchange(parts):
        by_device = parts.reshape((n_ctx, -1) + parts.shape[1:])
        return lax.all_to_all(by_device, "ctx", split_axis=0, concat_axis=0, tiled=True)

    def in_order(parts, earlier):
        return lax.optimization_barrier((parts, earlier))

    outgoing, received = [], []
    for size, (chosen, _) in zip(sizes, matrices):
        if outgoing:
            chosen, outgoing[-1] = in_order(chosen, outgoing[-1])
        outgoing.append(dispatch(chosen, normed, size))
    for parts in outgoing:
        if received:
            parts, received[-1] = in_order(parts, received[-1])
        received.append(exchange(parts))

    results = []
    for i, size in enumerate(sizes):
        if i > 1 and i == len(sizes) - 1:
            received[i], results[0] = in_order(received[i], results[0])
        if results:
            received[i], results[-1] = in_order(received[i], results[-1])
        rows_in = received[i].reshape(outgoing[i].shape)
        results.append(run_expert(rows_in, gate_up, down))

    answers = []
    for parts in results:
        if answers:
            parts, answers[-1] = in_order(parts, answers[-1])
        answers.append(exchange(parts))

    moe_out = jnp.zeros((width_local, tok_dev), F32)
    for size, (_, scale), answer in zip(sizes, matrices, answers):
        if n_exp > 1:
            answer = lax.psum_scatter(answer, "exp", scatter_dimension=answer.ndim - 1, tiled=True)
        terms = lax.dot_general(
            answer.reshape(n_ctx * size, width_local), scale, (((0,), (0,)), ((), ())),
            preferred_element_type=F32,
        )
        moe_out = moe_out + terms[:, :tok_dev] + terms[:, tok_dev:]
    return moe_out


def per_device(
    tokens,
    route_ids,
    combine,
    gain_attn,
    gain_moe,
    query_weight,
    key_weight,
    value_weight,
    attn_sinks,
    out_weight,
    gate_up_weight,
    down_weight,
):
    tok_dev, width_local = tokens.shape
    n_ctx = lax.axis_size("ctx")
    n_exp = lax.axis_size("exp")
    capacity = tok_dev * route_ids.shape[1] * 5 // (4 * n_ctx)
    sizes = slot_chunks(capacity)
    matrices = routing(route_ids, combine, n_ctx, sizes)
    by_planes = n_exp == 1 and n_ctx % PLANE == 0 and n_ctx > PLANE
    project = project_planes if by_planes else project_whole
    residual, matrices = project(
        tokens, gain_attn, query_weight, key_weight, value_weight, attn_sinks, out_weight, matrices
    )
    width = residual.shape[0]
    normed_moe = rms_norm_t(residual, gain_moe)
    exp_index = lax.axis_index("exp")
    residual_local = lax.dynamic_slice_in_dim(residual, exp_index * width_local, width_local, 0)

    moe_out = mix_experts(normed_moe, sizes, matrices, gate_up_weight[0], down_weight[0])
    return (residual_local.astype(F32) + moe_out).astype(BF16).T


def solution(mesh):
    return jax.shard_map(
        per_device,
        mesh=mesh,
        in_specs=(
            P("ctx", "exp"),
            P("ctx", None),
            P("ctx", None),
            P(),
            P(),
            P(None, ("exp", "ctx")),
            P(None, ("exp", "ctx")),
            P(None, ("exp", "ctx")),
            P("exp"),
            P("exp", "ctx"),
            P("ctx", None, None, "exp"),
            P("ctx", "exp", None),
        ),
        out_specs=P("ctx", "exp"),
        check_vma=False,
    )
```

```python
import functools
import math

import jax
import jax.numpy as jnp
from jax import lax
from jax.experimental import pallas as pl
from jax.experimental.pallas import tpu as pltpu
from jax.sharding import PartitionSpec as P

HD = 64
WINDOW = 128
EPSILON = 1e-05
ROPE_BASE = 150000.0
PLANE = 8
BF16 = jnp.bfloat16
F32 = jnp.float32


def rms_norm(values, gain):
    wide = values.astype(F32)
    meansq = jnp.mean(wide * wide, axis=-1, keepdims=True)
    return (wide * lax.rsqrt(meansq + EPSILON) * gain).astype(BF16)


def rms_norm_t(values, gain):
    wide = values.astype(F32)
    meansq = jnp.mean(wide * wide, axis=0, keepdims=True)
    return (wide * lax.rsqrt(meansq + EPSILON) * gain[:, None]).astype(BF16)


def rotary(values, angles_pos):
    half_dim = values.shape[-1] // 2
    inverse_freq = jnp.exp(
        -(2.0 * jnp.arange(half_dim, dtype=F32) / values.shape[-1]) * math.log(ROPE_BASE)
    )
    angles = angles_pos[:, None] * inverse_freq[None, :]
    cosine = jnp.cos(angles)[:, None, :]
    sine_part = jnp.sin(angles)[:, None, :]
    first_half = values[..., :half_dim]
    second_half = values[..., half_dim:]
    return jnp.concatenate(
        [
            first_half * cosine - second_half * sine_part,
            second_half * cosine + first_half * sine_part,
        ],
        axis=-1,
    )


def sink_softmax(scores, key_mask, sink_col):
    masked = jnp.where(key_mask, scores, -1e30)
    row_top = jnp.maximum(jnp.max(masked, axis=-1, keepdims=True), sink_col)
    weights = jnp.where(key_mask, jnp.exp(masked - row_top), 0.0)
    denominator = jnp.sum(weights, axis=-1, keepdims=True) + jnp.exp(sink_col - row_top)
    return (weights / denominator).astype(BF16)


def attend_block(query_rows, key_rows, value_rows, query_pos, key_pos, sink_col):
    scores = jnp.einsum(
        "qkgd,skd->kgqs", query_rows, key_rows, preferred_element_type=F32
    ) * HD ** (-0.5)
    distance = query_pos[:, None] - key_pos[None, :]
    key_mask = (distance >= 0) & (distance < WINDOW) & (key_pos >= 0)[None, :]
    weights = sink_softmax(scores, key_mask, sink_col)
    mixed_rows = jnp.einsum("kgqs,skd->qkgd", weights, value_rows, preferred_element_type=F32)
    return mixed_rows.astype(BF16).reshape(query_rows.shape[0], -1)


def dot32(a, b):
    return jnp.dot(a, b, preferred_element_type=F32)


def project_whole(
    tokens, gain_attn, query_weight, key_weight, value_weight, attn_sinks, out_weight, early
):
    tok_dev = tokens.shape[0]
    full_rows = lax.all_gather(tokens, "exp", axis=1, tiled=True)
    normed = rms_norm(full_rows, gain_attn)
    pieces = lax.all_gather((query_weight, key_weight, value_weight), "ctx", axis=1, tiled=True)
    query_lin, key_lin, value_lin = tuple(dot32(normed, piece) for piece in pieces)
    heads_local = query_lin.shape[1] // HD
    kv_local = key_lin.shape[1] // HD
    group_size = heads_local // kv_local
    position_ids = lax.axis_index("ctx") * tok_dev + jnp.arange(tok_dev, dtype=jnp.int32)
    angles_pos = position_ids.astype(F32)
    query = rotary(query_lin.reshape(tok_dev, heads_local, HD), angles_pos).astype(BF16)
    keys_own = rotary(key_lin.reshape(tok_dev, kv_local, HD), angles_pos).astype(BF16)
    key_value = jnp.stack([keys_own.reshape(tok_dev, kv_local * HD), value_lin.astype(BF16)])
    n_ctx = lax.axis_size("ctx")
    previous = lax.ppermute(key_value, "ctx", [(i, i + 1) for i in range(n_ctx - 1)])
    context = jnp.concatenate([previous, key_value], axis=1)
    key_pos = position_ids[0] - WINDOW + jnp.arange(tok_dev + WINDOW, dtype=jnp.int32)
    attended = attend_block(
        query.reshape(tok_dev, kv_local, group_size, HD),
        context[0].reshape(-1, kv_local, HD),
        context[1].reshape(-1, kv_local, HD),
        position_ids,
        key_pos,
        attn_sinks.reshape(kv_local, group_size, 1, 1),
    )
    head_terms = dot32(attended, lax.all_gather(out_weight, "ctx", axis=1, tiled=True))
    attn_proj = lax.psum(head_terms.astype(BF16), "exp").astype(F32)
    return (full_rows.astype(F32) + attn_proj).astype(BF16).T, early


def dot_nt(a, b):
    return lax.dot_general(a, b, (((1,), (1,)), ((), ())), preferred_element_type=F32)


def turn(values, cosine, signed_sine):
    width = values.shape[1]
    half = HD // 2
    lane = lax.broadcasted_iota(jnp.int32, values.shape, 1) % HD
    partner = jnp.where(
        lane < half,
        pltpu.roll(values, width - half, 1),
        pltpu.roll(values, half, 1),
    )
    return values * cosine + partner * signed_sine


def qkv_kernel(count, *refs):
    blocks, (weight_ref, cos_ref, sin_ref, q_ref, key_value_ref, rows_ref, kv_ref) = refs[:count], refs[count:]
    width, rows = blocks[0].shape
    planes, packed, cols = weight_ref.shape
    share = kv_ref.shape[2]
    for r in range(count):
        rows_ref[r * rows : (r + 1) * rows, :] = blocks[r][...].T

    for p in range(planes):
        for tile in range((packed - width) // (2 * share)):
            at, lanes = width + 2 * share * tile, slice(tile * cols, (tile + 1) * cols)
            for part in range(2):
                kv_ref[part, p, :, lanes] = weight_ref[p, at + part * share : at + (part + 1) * share]
    both = kv_ref[...].reshape(2 * planes * share, kv_ref.shape[3])[:, :width]
    lines = dot_nt(rows_ref[...], both)
    half = planes * share
    for r in range(count):
        piece = lines[r * rows : (r + 1) * rows]
        key_value_ref[r, :, :half] = turn(piece[:, :half], cos_ref[r], sin_ref[r]).astype(BF16)
        key_value_ref[r, :, half:] = piece[:, half:].astype(BF16)

    for p in range(0, planes, 2):
        weight = jnp.concatenate([weight_ref[p, :width], weight_ref[p + 1, :width]], axis=1)
        query = dot32(rows_ref[...], weight)
        for k in range(2):
            lanes = slice((p + k) * cols, (p + k + 1) * cols)
            for r in range(count):
                piece = query[r * rows : (r + 1) * rows, k * cols : (k + 1) * cols]
                q_ref[r, :, lanes] = turn(piece, cos_ref[r], sin_ref[r]).astype(BF16)


def project_blocks(blocks, weights, share, cosine, signed_sine):
    count = len(blocks)
    width, rows = blocks[0].shape
    planes, packed, cols = weights.shape
    kv_cols = 2 * planes * share
    vmem = pl.BlockSpec(memory_space=pltpu.VMEM)
    return pl.pallas_call(
        functools.partial(qkv_kernel, count),
        in_specs=[vmem] * (count + 3),
        out_specs=[vmem, vmem],
        out_shape=[
            jax.ShapeDtypeStruct((count, rows, planes * cols), BF16),
            jax.ShapeDtypeStruct((count, rows, kv_cols), BF16),
        ],
        scratch_shapes=[
            pltpu.VMEM((count * rows, width), BF16),
            pltpu.VMEM((2, planes, share, (packed - width) // (2 * share) * cols), BF16),
        ],
        compiler_params=pltpu.CompilerParams(vmem_limit_bytes=36 * 2**20),
        cost_estimate=pl.CostEstimate(
            flops=2 * count * rows * width * (planes * cols + kv_cols),
            bytes_accessed=2 * width * (planes * cols + kv_cols + count * rows),
            transcendentals=0,
        ),
    )(*blocks, weights, cosine, signed_sine)


def attend_kernel(
    numbers, pieces, place_ref, sinks_ref, *refs
):
    queries, key_values, halos, refs = refs[:2], refs[2:4], refs[4:6], refs[6:]
    share_refs, (out_ref, att_ref, total_ref) = refs[: len(pieces)], refs[len(pieces) :]
    early, rows = key_values[0].shape[:2]
    count = early + 1
    pair = 2 * HD
    kv_heads = key_values[0].shape[2] // pair
    kv_cols = kv_heads * HD
    pairs = queries[0].shape[2] // pair
    lane = lax.broadcasted_iota(jnp.int32, (rows, pair), 1)
    low = lane < HD

    def spread(values, head):
        moved = pltpu.roll(values.astype(F32), HD, 1)
        chunk = values.astype(F32)
        lower, upper = (chunk, moved) if head % 2 == 0 else (moved, chunk)
        zero = jnp.zeros_like(chunk)
        return jnp.concatenate(
            [jnp.where(low, lower, zero), jnp.where(low, zero, upper)], axis=0
        ).astype(BF16)

    def block(refs, r):
        return (refs[0], r) if r < early else (refs[1], 0)

    def own_columns(r, lanes):
        ref, at = block(key_values, r)
        return ref[at, :, lanes]

    def previous_columns(r, lanes):
        at = place_ref[count + r]
        return jnp.where(at < early, halos[0][jnp.minimum(at, early - 1), :, lanes], halos[1][0, :, lanes])

    def side(columns, r):
        tables = []
        for head in range(kv_heads):
            at = head // 2 * pair
            keys = spread(columns(r, slice(at, at + pair)), head)
            values = spread(columns(r, slice(kv_cols + at, kv_cols + at + pair)), head)
            tables.append((keys, values))
        return tables

    row = lax.broadcasted_iota(jnp.int32, (rows, rows), 0)
    col = lax.broadcasted_iota(jnp.int32, (rows, rows), 1)
    inside = col <= row
    scale = HD**-0.5
    for i, r in enumerate(numbers):
        own, previous = side(own_columns, r), side(previous_columns, r)
        queries_ref, query_at = block(queries, r)
        shown = jnp.logical_or(inside, place_ref[r] == 0)
        for p in range(pairs):
            head = p * kv_heads // pairs
            chunk = queries_ref[query_at, :, p * pair : (p + 1) * pair]
            scores_own = dot_nt(chunk, own[head][0])
            scores_previous = dot_nt(chunk, previous[head][0])
            probs_own, probs_previous = [], []
            for h in range(2):
                half = slice(h * rows, (h + 1) * rows)
                scores = jnp.where(inside, scores_own[:, half], scores_previous[:, half]) * scale
                scores = jnp.where(shown, scores, -1e30)
                sink = sinks_ref[2 * p + h]
                top = jnp.maximum(jnp.max(scores, axis=1, keepdims=True), sink)
                weights = jnp.exp(scores - top)
                total = jnp.sum(weights, axis=1, keepdims=True) + jnp.exp(sink - top)
                probs = weights / total
                probs_own.append(jnp.where(inside, probs, 0.0).astype(BF16))
                probs_previous.append(jnp.where(inside, 0.0, probs).astype(BF16))
            mixed = dot32(jnp.concatenate(probs_own, axis=1), own[head][1])
            mixed = mixed + dot32(jnp.concatenate(probs_previous, axis=1), previous[head][1])
            att_ref[i * rows : (i + 1) * rows, p * pair : (p + 1) * pair] = mixed.astype(BF16)

    groups, shares, padded, _ = total_ref.shape
    cols = out_ref.shape[1] // (shares * groups)
    attended = att_ref[...]
    for (relative, first), weight_ref in zip(pieces, share_refs):
        size, _, depth = weight_ref.shape
        terms = dot_nt(weight_ref[...].reshape(size * padded, depth), attended)
        for g in range(size):
            total_ref[first + g, place_ref[2 * count + relative]] = terms[g * padded : (g + 1) * padded]
    for g in range(groups):
        for p in range(shares):
            at = (g * shares + p) * cols
            for i in range(len(numbers)):
                out_ref[i, at : at + cols, :] = total_ref[g, p, :cols, i * rows : (i + 1) * rows]


def attend_and_project(numbers, place, sinks, queries, key_values, halos, shares, width):
    rows = queries[0].shape[1]
    count = len(numbers)
    groups, padded, depth = shares[0][2].shape
    pieces = tuple((relative, first) for relative, first, _ in shares)
    vmem = pl.BlockSpec(memory_space=pltpu.VMEM)
    smem = pl.BlockSpec(memory_space=pltpu.SMEM)
    return pl.pallas_call(
        functools.partial(attend_kernel, numbers, pieces),
        in_specs=[smem, smem] + [vmem] * (6 + len(shares)),
        out_specs=vmem,
        out_shape=jax.ShapeDtypeStruct((count, width, rows), F32),
        scratch_shapes=[
            pltpu.VMEM((count * rows, depth), BF16),
            pltpu.VMEM((groups, PLANE, padded, count * rows), F32),
        ],
        compiler_params=pltpu.CompilerParams(vmem_limit_bytes=40 * 2**20),
        cost_estimate=pl.CostEstimate(
            flops=2 * count * rows * depth * (width + 8 * rows),
            bytes_accessed=2 * width * (depth + 2 * count * rows),
            transcendentals=count * rows * rows * depth // HD,
        ),
    )(place, sinks, *queries, *key_values, *halos, *[weight for _, _, weight in shares])


def project_planes(
    tokens, gain_attn, query_weight, key_weight, value_weight, attn_sinks, out_weight, early
):
    tok_dev, width = tokens.shape
    n_ctx = lax.axis_size("ctx")
    n_z = n_ctx // PLANE
    index = lax.axis_index("ctx")
    z, j = index // PLANE, index % PLANE
    planes = [[PLANE * a + b for b in range(PLANE)] for a in range(n_z)]
    order = list(range(0, n_z, 2)) + list(range(1, n_z, 2))[::-1]
    place_of = [order.index(a) for a in range(n_z)]
    ring, places = jnp.array(order, jnp.int32), jnp.array(place_of, jnp.int32)

    def shift(block, steps):
        return lax.ppermute(block, "ctx", [(i, (i + steps * PLANE) % n_ctx) for i in range(n_ctx)])

    def pass_on(block):
        route = [
            (a * PLANE + b, order[place_of[a] - 1] * PLANE + b) for a in range(n_z) for b in range(PLANE)
        ]
        return lax.ppermute(block, "ctx", route)

    def behind(block):
        route = [(a * PLANE + b, a * PLANE + (b + 1) % PLANE) for a in range(n_z) for b in range(PLANE)]
        return lax.ppermute(block, "ctx", route)

    def swap(block, bits):
        return lax.ppermute(block, "ctx", [(i, i ^ bits) for i in range(n_ctx)])

    tokens_t = tokens.T
    blocks = [rms_norm_t(tokens_t, gain_attn)]

    lanes = query_weight.shape[1]
    share = key_weight.shape[1]
    tiles = -(-width // lanes)
    kv_rows = jnp.concatenate([key_weight.T, value_weight.T], axis=0)
    kv_rows = jnp.pad(kv_rows, ((0, 0), (0, tiles * lanes - width))).reshape(2 * share, tiles, lanes)
    packed = jnp.concatenate(
        [query_weight, kv_rows.transpose(1, 0, 2).reshape(tiles * 2 * share, lanes)], axis=0
    )
    weights = lax.all_gather(packed, "ctx", axis_index_groups=planes)

    cols = out_weight.shape[1]
    padded = -(-cols // 16) * 16
    group_rows = out_weight.shape[0] // n_z
    out_rows = jnp.pad(out_weight.T, ((0, padded - cols), (0, 0)))
    out_rows, blocks[0] = lax.optimization_barrier((out_rows, blocks[0]))
    blocks.append(pass_on(blocks[0]))
    out_groups = jnp.stack(jnp.split(out_rows, n_z, axis=1))
    pieces = [
        shift(lax.dynamic_index_in_dim(out_groups, (z + s) % n_z, 0, keepdims=False), s) if s
        else lax.dynamic_index_in_dim(out_groups, z, 0, keepdims=False)
        for s in range(n_z)
    ]
    ordered = jnp.stack(pieces[::-1] + pieces[:0:-1])
    out_mine = lax.dynamic_slice_in_dim(ordered, n_z - 1 - z, n_z, 0)
    heads = PLANE * query_weight.shape[1] // HD
    sinks = lax.dynamic_slice_in_dim(attn_sinks, z * heads, heads)
    own_rows = jnp.arange(tok_dev, dtype=jnp.int32)
    lane = jnp.arange(2 * HD, dtype=jnp.int32) % HD
    half = HD // 2
    inverse_freq = jnp.exp(-(2.0 * (lane % half).astype(F32) / HD) * math.log(ROPE_BASE))
    mine = places[z]
    block_z = ring[(mine + jnp.arange(n_z, dtype=jnp.int32)) % n_z]
    numbers = block_z * PLANE + j
    angles = (numbers[:, None] * tok_dev + own_rows[None, :]).astype(F32)[:, :, None] * inverse_freq
    signed_sine = jnp.where(lane < half, -jnp.sin(angles), jnp.sin(angles))
    cosine = jnp.cos(angles)
    below = (places[jnp.maximum(block_z - 1, 0)] - mine) % n_z
    previous_at = jnp.where(j == 0, below, jnp.arange(n_z, dtype=jnp.int32))
    relative = jnp.arange(PLANE, dtype=jnp.int32) ^ j
    place = jnp.concatenate([(numbers == 0).astype(jnp.int32), previous_at, relative])
    for _ in range(n_z - 2):
        blocks.append(pass_on(blocks[-1]))
    cut = n_z // 2
    near, far = swap(out_mine, 2), swap(out_mine, 4)
    (near, far, cosine, signed_sine, place, sinks, early) = lax.optimization_barrier(
        (near, far, cosine, signed_sine, place, sinks, early)
    )
    corner_low, corner_high = swap(near[:cut], 4), swap(far[cut:], 2)
    early_count = n_z - 1
    query, key_value = project_blocks(
        blocks[:early_count], weights, share, cosine[:early_count], signed_sine[:early_count]
    )
    (near, far, corner_low, corner_high, blocks[-1], key_value) = lax.optimization_barrier(
        (near, far, corner_low, corner_high, blocks[-1], key_value)
    )
    shares = []
    for r, first, piece in ((0, 0, out_mine), (2, 0, near), (4, 0, far), (6, 0, corner_low), (6, cut, corner_high)):
        shares += [(r, first, piece), (r + 1, first, swap(piece, 1))]
    last_query, last_key_value = project_blocks(
        blocks[early_count:], weights, share, cosine[early_count:], signed_sine[early_count:]
    )
    queries, key_values = (query, last_query), (key_value, last_key_value)
    halos = (behind(key_value), behind(last_key_value))

    def parts_of(numbers):
        return attend_and_project(numbers, place, sinks, queries, key_values, halos, shares, width)

    cuts = (slice(0, width // 32 * 16), slice(width // 32 * 16, width))
    first = parts_of((1,))[0]
    others = parts_of(tuple(range(2, n_z)) + (0,))
    halves = [first[cut].astype(BF16) for cut in cuts]
    for i in range(n_z - 1):
        terms = others[i] + tokens_t.astype(F32) if i == n_z - 2 else others[i]
        sums = []
        for half, cut in zip(halves, cuts):
            arrived = pass_on(half)
            if sums:
                arrived, _ = lax.optimization_barrier((arrived, sums[-1]))
            sums.append((arrived.astype(F32) + terms[cut]).astype(BF16))
        halves = sums
    return jnp.concatenate(halves, axis=0), early


def expert_kernel(tile, hidden, rows_ref, gate_ref, upper_ref, down_ref, out_ref, total_ref, flat_ref):
    step = pl.program_id(0)
    steps = pl.num_programs(0)

    def add(count, initial):
        rows = flat_ref[...]
        gate = dot32(rows, gate_ref[0, :, :count])
        upper = dot32(rows, upper_ref[0, :, :count])
        activation = (gate * jax.nn.sigmoid(1.702 * gate) * (upper + 1.0)).astype(BF16)
        terms = dot32(activation, down_ref[:count, :])
        total_ref[...] = terms if initial else total_ref[...] + terms

    last = hidden - (-(-hidden // tile) - 1) * tile

    @pl.when(step == 0)
    def _():
        flat_ref[...] = rows_ref[...].reshape(flat_ref.shape)
        add(tile, True)

    @pl.when(jnp.logical_and(step > 0, step < steps - 1))
    def _():
        add(tile, False)

    @pl.when(step == steps - 1)
    def _():
        add(last, False)
        out_ref[...] = total_ref[...].astype(BF16).reshape(out_ref.shape)


def run_expert(rows, gate_up, down):
    width = rows.shape[-1]
    count = rows.size // width
    hidden = down.shape[0]
    tile = 512 if hidden > 1024 else 256
    whole = pl.BlockSpec(rows.shape, lambda f: (0,) * rows.ndim)
    return pl.pallas_call(
        functools.partial(expert_kernel, tile, hidden),
        grid=(-(-hidden // tile),),
        in_specs=[
            whole,
            pl.BlockSpec((1, width, tile), lambda f: (0, 0, f)),
            pl.BlockSpec((1, width, tile), lambda f: (1, 0, f)),
            pl.BlockSpec((tile, width), lambda f: (f, 0)),
        ],
        out_specs=whole,
        out_shape=jax.ShapeDtypeStruct(rows.shape, BF16),
        scratch_shapes=[pltpu.VMEM((count, width), F32), pltpu.VMEM((count, width), BF16)],
        compiler_params=pltpu.CompilerParams(vmem_limit_bytes=52 * 2**20),
        cost_estimate=pl.CostEstimate(
            flops=6 * count * width * hidden,
            bytes_accessed=6 * width * hidden + 4 * count * width,
            transcendentals=count * hidden,
        ),
    )(rows, gate_up, gate_up, down)


def slot_chunks(capacity):
    return [capacity - 8, 8] if capacity > 8 else [capacity]


def dispatch_kernel(chosen_ref, normed_ref, out_ref):
    out_ref[...] = dot_nt(chosen_ref[...], normed_ref[...]).astype(BF16).reshape(out_ref.shape)


def dispatch(chosen, normed, size):
    total, rows = chosen.shape
    width = normed.shape[0]
    shape = (total // 4, 4, width) if size % 8 and size % 4 == 0 else (total, width)
    return pl.pallas_call(
        dispatch_kernel,
        out_shape=jax.ShapeDtypeStruct(shape, BF16),
        compiler_params=pltpu.CompilerParams(vmem_limit_bytes=24 * 2**20),
        cost_estimate=pl.CostEstimate(
            flops=2 * total * rows * width, bytes_accessed=2 * width * (total + rows), transcendentals=0
        ),
    )(chosen, normed)


def routing(route_ids, combine, n_ctx, sizes):
    tok_dev = route_ids.shape[0]
    named = route_ids[:, :, None] == jnp.arange(n_ctx, dtype=jnp.int32)[None, None, :]
    member = jnp.any(named, axis=1)
    weight_of = jnp.sum(jnp.where(named, combine[:, :, None], 0.0), axis=1)
    rows = jnp.arange(tok_dev, dtype=jnp.int32)
    earlier = (rows[:, None] > rows[None, :]).astype(BF16)
    slot_of = jnp.where(member, dot32(earlier, member.astype(BF16)), -1.0).T.astype(BF16)
    weight_of = weight_of.T
    high = weight_of.astype(BF16)
    low = (weight_of - high.astype(F32)).astype(BF16)
    table = jnp.concatenate([slot_of, high, low], axis=1)
    chunks = []
    first = 0
    for size in sizes:
        number = jnp.arange(n_ctx * size, dtype=jnp.int32)[:, None]
        device = (number // size == jnp.arange(n_ctx, dtype=jnp.int32)[None, :]).astype(BF16)
        spread = dot32(device, table)
        chosen = spread[:, :tok_dev] == (first + number % size).astype(F32)
        scale = jnp.where(jnp.concatenate([chosen, chosen], axis=1), spread[:, tok_dev:], 0.0).astype(BF16)
        chunks.append((chosen.astype(BF16), scale))
        first += size
    return chunks


def mix_experts(normed, sizes, matrices, gate_up, down):
    width, tok_dev = normed.shape
    n_ctx, n_exp = lax.axis_size("ctx"), lax.axis_size("exp")
    width_local = width // n_exp

    def exchange(parts):
        by_device = parts.reshape((n_ctx, -1) + parts.shape[1:])
        return lax.all_to_all(by_device, "ctx", split_axis=0, concat_axis=0, tiled=True)

    def in_order(parts, earlier):
        return lax.optimization_barrier((parts, earlier))

    outgoing, received = [], []
    for size, (chosen, _) in zip(sizes, matrices):
        if outgoing:
            chosen, outgoing[-1] = in_order(chosen, outgoing[-1])
        outgoing.append(dispatch(chosen, normed, size))
    for parts in outgoing:
        if received:
            parts, received[-1] = in_order(parts, received[-1])
        received.append(exchange(parts))

    results = []
    for i, size in enumerate(sizes):
        if i > 1 and i == len(sizes) - 1:
            received[i], results[0] = in_order(received[i], results[0])
        if results:
            received[i], results[-1] = in_order(received[i], results[-1])
        rows_in = received[i].reshape(outgoing[i].shape)
        results.append(run_expert(rows_in, gate_up, down))

    answers = []
    for parts in results:
        if answers:
            parts, answers[-1] = in_order(parts, answers[-1])
        answers.append(exchange(parts))

    moe_out = jnp.zeros((width_local, tok_dev), F32)
    for size, (_, scale), answer in zip(sizes, matrices, answers):
        if n_exp > 1:
            answer = lax.psum_scatter(answer, "exp", scatter_dimension=answer.ndim - 1, tiled=True)
        terms = lax.dot_general(
            answer.reshape(n_ctx * size, width_local), scale, (((0,), (0,)), ((), ())),
            preferred_element_type=F32,
        )
        moe_out = moe_out + terms[:, :tok_dev] + terms[:, tok_dev:]
    return moe_out


def per_device(
    tokens,
    route_ids,
    combine,
    gain_attn,
    gain_moe,
    query_weight,
    key_weight,
    value_weight,
    attn_sinks,
    out_weight,
    gate_up_weight,
    down_weight,
):
    tok_dev, width_local = tokens.shape
    n_ctx = lax.axis_size("ctx")
    n_exp = lax.axis_size("exp")
    capacity = tok_dev * route_ids.shape[1] * 5 // (4 * n_ctx)
    sizes = slot_chunks(capacity)
    matrices = routing(route_ids, combine, n_ctx, sizes)
    by_planes = n_exp == 1 and n_ctx % PLANE == 0 and n_ctx > PLANE
    project = project_planes if by_planes else project_whole
    residual, matrices = project(
        tokens, gain_attn, query_weight, key_weight, value_weight, attn_sinks, out_weight, matrices
    )
    width = residual.shape[0]
    normed_moe = rms_norm_t(residual, gain_moe)
    exp_index = lax.axis_index("exp")
    residual_local = lax.dynamic_slice_in_dim(residual, exp_index * width_local, width_local, 0)

    moe_out = mix_experts(normed_moe, sizes, matrices, gate_up_weight[0], down_weight[0])
    return (residual_local.astype(F32) + moe_out).astype(BF16).T


def solution(mesh):
    return jax.shard_map(
        per_device,
        mesh=mesh,
        in_specs=(
            P("ctx", "exp"),
            P("ctx", None),
            P("ctx", None),
            P(),
            P(),
            P(None, ("exp", "ctx")),
            P(None, ("exp", "ctx")),
            P(None, ("exp", "ctx")),
            P("exp"),
            P("exp", "ctx"),
            P("ctx", None, None, "exp"),
            P("ctx", "exp", None),
        ),
        out_specs=P("ctx", "exp"),
        check_vma=False,
    )
```

```python
import functools
import math

import jax
import jax.numpy as jnp
from jax import lax
from jax.experimental import pallas as pl
from jax.experimental.pallas import tpu as pltpu
from jax.sharding import PartitionSpec as P

HD = 64
WINDOW = 128
EPSILON = 1e-05
ROPE_BASE = 150000.0
PLANE = 8
BF16 = jnp.bfloat16
F32 = jnp.float32


def rms_norm(values, gain):
    wide = values.astype(F32)
    meansq = jnp.mean(wide * wide, axis=-1, keepdims=True)
    return (wide * lax.rsqrt(meansq + EPSILON) * gain).astype(BF16)


def rms_norm_t(values, gain):
    wide = values.astype(F32)
    meansq = jnp.mean(wide * wide, axis=0, keepdims=True)
    return (wide * lax.rsqrt(meansq + EPSILON) * gain[:, None]).astype(BF16)


def rotary(values, angles_pos):
    half_dim = values.shape[-1] // 2
    inverse_freq = jnp.exp(
        -(2.0 * jnp.arange(half_dim, dtype=F32) / values.shape[-1]) * math.log(ROPE_BASE)
    )
    angles = angles_pos[:, None] * inverse_freq[None, :]
    cosine = jnp.cos(angles)[:, None, :]
    sine_part = jnp.sin(angles)[:, None, :]
    first_half = values[..., :half_dim]
    second_half = values[..., half_dim:]
    return jnp.concatenate(
        [
            first_half * cosine - second_half * sine_part,
            second_half * cosine + first_half * sine_part,
        ],
        axis=-1,
    )


def sink_softmax(scores, key_mask, sink_col):
    masked = jnp.where(key_mask, scores, -1e30)
    row_top = jnp.maximum(jnp.max(masked, axis=-1, keepdims=True), sink_col)
    weights = jnp.where(key_mask, jnp.exp(masked - row_top), 0.0)
    denominator = jnp.sum(weights, axis=-1, keepdims=True) + jnp.exp(sink_col - row_top)
    return (weights / denominator).astype(BF16)


def attend_block(query_rows, key_rows, value_rows, query_pos, key_pos, sink_col):
    scores = jnp.einsum(
        "qkgd,skd->kgqs", query_rows, key_rows, preferred_element_type=F32
    ) * HD ** (-0.5)
    distance = query_pos[:, None] - key_pos[None, :]
    key_mask = (distance >= 0) & (distance < WINDOW) & (key_pos >= 0)[None, :]
    weights = sink_softmax(scores, key_mask, sink_col)
    mixed_rows = jnp.einsum("kgqs,skd->qkgd", weights, value_rows, preferred_element_type=F32)
    return mixed_rows.astype(BF16).reshape(query_rows.shape[0], -1)


def dot32(a, b):
    return jnp.dot(a, b, preferred_element_type=F32)


def project_whole(
    tokens, gain_attn, query_weight, key_weight, value_weight, attn_sinks, out_weight, early
):
    tok_dev = tokens.shape[0]
    full_rows = lax.all_gather(tokens, "exp", axis=1, tiled=True)
    normed = rms_norm(full_rows, gain_attn)
    pieces = lax.all_gather((query_weight, key_weight, value_weight), "ctx", axis=1, tiled=True)
    query_lin, key_lin, value_lin = tuple(dot32(normed, piece) for piece in pieces)
    heads_local = query_lin.shape[1] // HD
    kv_local = key_lin.shape[1] // HD
    group_size = heads_local // kv_local
    position_ids = lax.axis_index("ctx") * tok_dev + jnp.arange(tok_dev, dtype=jnp.int32)
    angles_pos = position_ids.astype(F32)
    query = rotary(query_lin.reshape(tok_dev, heads_local, HD), angles_pos).astype(BF16)
    keys_own = rotary(key_lin.reshape(tok_dev, kv_local, HD), angles_pos).astype(BF16)
    key_value = jnp.stack([keys_own.reshape(tok_dev, kv_local * HD), value_lin.astype(BF16)])
    n_ctx = lax.axis_size("ctx")
    previous = lax.ppermute(key_value, "ctx", [(i, i + 1) for i in range(n_ctx - 1)])
    context = jnp.concatenate([previous, key_value], axis=1)
    key_pos = position_ids[0] - WINDOW + jnp.arange(tok_dev + WINDOW, dtype=jnp.int32)
    attended = attend_block(
        query.reshape(tok_dev, kv_local, group_size, HD),
        context[0].reshape(-1, kv_local, HD),
        context[1].reshape(-1, kv_local, HD),
        position_ids,
        key_pos,
        attn_sinks.reshape(kv_local, group_size, 1, 1),
    )
    head_terms = dot32(attended, lax.all_gather(out_weight, "ctx", axis=1, tiled=True))
    attn_proj = lax.psum(head_terms.astype(BF16), "exp").astype(F32)
    return (full_rows.astype(F32) + attn_proj).astype(BF16).T, early


def dot_nt(a, b):
    return lax.dot_general(a, b, (((1,), (1,)), ((), ())), preferred_element_type=F32)


def turn(values, cosine, signed_sine):
    width = values.shape[1]
    half = HD // 2
    lane = lax.broadcasted_iota(jnp.int32, values.shape, 1) % HD
    partner = jnp.where(
        lane < half,
        pltpu.roll(values, width - half, 1),
        pltpu.roll(values, half, 1),
    )
    return values * cosine + partner * signed_sine


def qkv_kernel(count, start, *refs):
    blocks, (weight_ref, cos_ref, sin_ref, q_ref, key_value_ref, rows_ref, kv_ref) = refs[:count], refs[count:]
    width, rows = blocks[0].shape
    planes, packed, cols = weight_ref.shape
    share = kv_ref.shape[2]
    for r in range(count):
        rows_ref[r * rows : (r + 1) * rows, :] = blocks[r][...].T

    for p in range(planes):
        for tile in range((packed - width) // (2 * share)):
            at, lanes = width + 2 * share * tile, slice(tile * cols, (tile + 1) * cols)
            for part in range(2):
                kv_ref[part, p, :, lanes] = weight_ref[p, at + part * share : at + (part + 1) * share]
    both = kv_ref[...].reshape(2 * planes * share, kv_ref.shape[3])[:, :width]
    lines = dot_nt(rows_ref[...], both)
    half = planes * share
    for r in range(count):
        piece = lines[r * rows : (r + 1) * rows]
        key_value_ref[r, :, :half] = turn(piece[:, :half], cos_ref[start + r], sin_ref[start + r]).astype(BF16)
        key_value_ref[r, :, half:] = piece[:, half:].astype(BF16)

    for p in range(0, planes, 2):
        weight = jnp.concatenate([weight_ref[p, :width], weight_ref[p + 1, :width]], axis=1)
        query = dot32(rows_ref[...], weight)
        for k in range(2):
            lanes = slice((p + k) * cols, (p + k + 1) * cols)
            for r in range(count):
                piece = query[r * rows : (r + 1) * rows, k * cols : (k + 1) * cols]
                q_ref[r, :, lanes] = turn(piece, cos_ref[start + r], sin_ref[start + r]).astype(BF16)


def project_blocks(start, blocks, weights, share, cosine, signed_sine):
    count = len(blocks)
    width, rows = blocks[0].shape
    planes, packed, cols = weights.shape
    kv_cols = 2 * planes * share
    vmem = pl.BlockSpec(memory_space=pltpu.VMEM)
    return pl.pallas_call(
        functools.partial(qkv_kernel, count, start),
        in_specs=[vmem] * (count + 3),
        out_specs=[vmem, vmem],
        out_shape=[
            jax.ShapeDtypeStruct((count, rows, planes * cols), BF16),
            jax.ShapeDtypeStruct((count, rows, kv_cols), BF16),
        ],
        scratch_shapes=[
            pltpu.VMEM((count * rows, width), BF16),
            pltpu.VMEM((2, planes, share, (packed - width) // (2 * share) * cols), BF16),
        ],
        compiler_params=pltpu.CompilerParams(vmem_limit_bytes=36 * 2**20),
        cost_estimate=pl.CostEstimate(
            flops=2 * count * rows * width * (planes * cols + kv_cols),
            bytes_accessed=2 * width * (planes * cols + kv_cols + count * rows),
            transcendentals=0,
        ),
    )(*blocks, weights, cosine, signed_sine)


def attend_kernel(
    numbers, pieces, place_ref, sinks_ref, *refs
):
    queries, key_values, halos, refs = refs[:2], refs[2:4], refs[4:6], refs[6:]
    share_refs, (out_ref, att_ref, total_ref) = refs[: len(pieces)], refs[len(pieces) :]
    early, rows = key_values[0].shape[:2]
    count = early + 1
    pair = 2 * HD
    kv_heads = key_values[0].shape[2] // pair
    kv_cols = kv_heads * HD
    pairs = queries[0].shape[2] // pair
    lane = lax.broadcasted_iota(jnp.int32, (rows, pair), 1)
    low = lane < HD

    def spread(values, head):
        moved = pltpu.roll(values.astype(F32), HD, 1)
        chunk = values.astype(F32)
        lower, upper = (chunk, moved) if head % 2 == 0 else (moved, chunk)
        zero = jnp.zeros_like(chunk)
        return jnp.concatenate(
            [jnp.where(low, lower, zero), jnp.where(low, zero, upper)], axis=0
        ).astype(BF16)

    def block(refs, r):
        return (refs[0], r) if r < early else (refs[1], 0)

    def own_columns(r, lanes):
        ref, at = block(key_values, r)
        return ref[at, :, lanes]

    def previous_columns(r, lanes):
        at = place_ref[count + r]
        return jnp.where(at < early, halos[0][jnp.minimum(at, early - 1), :, lanes], halos[1][0, :, lanes])

    def side(columns, r):
        tables = []
        for head in range(kv_heads):
            at = head // 2 * pair
            keys = spread(columns(r, slice(at, at + pair)), head)
            values = spread(columns(r, slice(kv_cols + at, kv_cols + at + pair)), head)
            tables.append((keys, values))
        return tables

    row = lax.broadcasted_iota(jnp.int32, (rows, rows), 0)
    col = lax.broadcasted_iota(jnp.int32, (rows, rows), 1)
    inside = col <= row
    scale = HD**-0.5
    for i, r in enumerate(numbers):
        own, previous = side(own_columns, r), side(previous_columns, r)
        queries_ref, query_at = block(queries, r)
        shown = jnp.logical_or(inside, place_ref[r] == 0)
        for p in range(pairs):
            head = p * kv_heads // pairs
            chunk = queries_ref[query_at, :, p * pair : (p + 1) * pair]
            scores_own = dot_nt(chunk, own[head][0])
            scores_previous = dot_nt(chunk, previous[head][0])
            probs_own, probs_previous = [], []
            for h in range(2):
                half = slice(h * rows, (h + 1) * rows)
                scores = jnp.where(inside, scores_own[:, half], scores_previous[:, half]) * scale
                scores = jnp.where(shown, scores, -1e30)
                sink = sinks_ref[2 * p + h]
                top = jnp.maximum(jnp.max(scores, axis=1, keepdims=True), sink)
                weights = jnp.exp(scores - top)
                total = jnp.sum(weights, axis=1, keepdims=True) + jnp.exp(sink - top)
                probs = weights / total
                probs_own.append(jnp.where(inside, probs, 0.0).astype(BF16))
                probs_previous.append(jnp.where(inside, 0.0, probs).astype(BF16))
            mixed = dot32(jnp.concatenate(probs_own, axis=1), own[head][1])
            mixed = mixed + dot32(jnp.concatenate(probs_previous, axis=1), previous[head][1])
            att_ref[i * rows : (i + 1) * rows, p * pair : (p + 1) * pair] = mixed.astype(BF16)

    groups, shares, padded, _ = total_ref.shape
    cols = out_ref.shape[1] // (shares * groups)
    attended = att_ref[...]
    for (relative, first), weight_ref in zip(pieces, share_refs):
        size, _, depth = weight_ref.shape
        terms = dot_nt(weight_ref[...].reshape(size * padded, depth), attended)
        for g in range(size):
            total_ref[first + g, place_ref[2 * count + relative]] = terms[g * padded : (g + 1) * padded]
    for g in range(groups):
        for p in range(shares):
            at = (g * shares + p) * cols
            for i in range(len(numbers)):
                out_ref[i, at : at + cols, :] = total_ref[g, p, :cols, i * rows : (i + 1) * rows]


def attend_and_project(numbers, place, sinks, queries, key_values, halos, shares, width):
    rows = queries[0].shape[1]
    count = len(numbers)
    groups, padded, depth = shares[0][2].shape
    pieces = tuple((relative, first) for relative, first, _ in shares)
    vmem = pl.BlockSpec(memory_space=pltpu.VMEM)
    smem = pl.BlockSpec(memory_space=pltpu.SMEM)
    return pl.pallas_call(
        functools.partial(attend_kernel, numbers, pieces),
        in_specs=[smem, smem] + [vmem] * (6 + len(shares)),
        out_specs=vmem,
        out_shape=jax.ShapeDtypeStruct((count, width, rows), F32),
        scratch_shapes=[
            pltpu.VMEM((count * rows, depth), BF16),
            pltpu.VMEM((groups, PLANE, padded, count * rows), F32),
        ],
        compiler_params=pltpu.CompilerParams(vmem_limit_bytes=40 * 2**20),
        cost_estimate=pl.CostEstimate(
            flops=2 * count * rows * depth * (width + 8 * rows),
            bytes_accessed=2 * width * (depth + 2 * count * rows),
            transcendentals=count * rows * rows * depth // HD,
        ),
    )(place, sinks, *queries, *key_values, *halos, *[weight for _, _, weight in shares])


def project_planes(
    tokens, gain_attn, query_weight, key_weight, value_weight, attn_sinks, out_weight, early
):
    tok_dev, width = tokens.shape
    n_ctx = lax.axis_size("ctx")
    n_z = n_ctx // PLANE
    index = lax.axis_index("ctx")
    z, j = index // PLANE, index % PLANE
    planes = [[PLANE * a + b for b in range(PLANE)] for a in range(n_z)]
    order = list(range(0, n_z, 2)) + list(range(1, n_z, 2))[::-1]
    place_of = [order.index(a) for a in range(n_z)]
    ring, places = jnp.array(order, jnp.int32), jnp.array(place_of, jnp.int32)

    def shift(block, steps):
        return lax.ppermute(block, "ctx", [(i, (i + steps * PLANE) % n_ctx) for i in range(n_ctx)])

    def pass_on(block):
        route = [
            (a * PLANE + b, order[place_of[a] - 1] * PLANE + b) for a in range(n_z) for b in range(PLANE)
        ]
        return lax.ppermute(block, "ctx", route)

    def behind(block):
        route = [(a * PLANE + b, a * PLANE + (b + 1) % PLANE) for a in range(n_z) for b in range(PLANE)]
        return lax.ppermute(block, "ctx", route)

    def swap(block, bits):
        return lax.ppermute(block, "ctx", [(i, i ^ bits) for i in range(n_ctx)])

    tokens_t = tokens.T
    blocks = [rms_norm_t(tokens_t, gain_attn)]

    lanes = query_weight.shape[1]
    share = key_weight.shape[1]
    tiles = -(-width // lanes)
    kv_rows = jnp.concatenate([key_weight.T, value_weight.T], axis=0)
    kv_rows = jnp.pad(kv_rows, ((0, 0), (0, tiles * lanes - width))).reshape(2 * share, tiles, lanes)
    packed = jnp.concatenate(
        [query_weight, kv_rows.transpose(1, 0, 2).reshape(tiles * 2 * share, lanes)], axis=0
    )
    weights = lax.all_gather(packed, "ctx", axis_index_groups=planes)

    cols = out_weight.shape[1]
    padded = -(-cols // 16) * 16
    group_rows = out_weight.shape[0] // n_z
    out_rows = jnp.pad(out_weight.T, ((0, padded - cols), (0, 0)))
    out_rows, blocks[0] = lax.optimization_barrier((out_rows, blocks[0]))
    blocks.append(pass_on(blocks[0]))
    out_groups = jnp.stack(jnp.split(out_rows, n_z, axis=1))
    pieces = [
        shift(lax.dynamic_index_in_dim(out_groups, (z + s) % n_z, 0, keepdims=False), s) if s
        else lax.dynamic_index_in_dim(out_groups, z, 0, keepdims=False)
        for s in range(n_z)
    ]
    ordered = jnp.stack(pieces[::-1] + pieces[:0:-1])
    out_mine = lax.dynamic_slice_in_dim(ordered, n_z - 1 - z, n_z, 0)
    heads = PLANE * query_weight.shape[1] // HD
    sinks = lax.dynamic_slice_in_dim(attn_sinks, z * heads, heads)
    own_rows = jnp.arange(tok_dev, dtype=jnp.int32)
    lane = jnp.arange(2 * HD, dtype=jnp.int32) % HD
    half = HD // 2
    inverse_freq = jnp.exp(-(2.0 * (lane % half).astype(F32) / HD) * math.log(ROPE_BASE))
    mine = places[z]
    block_z = ring[(mine + jnp.arange(n_z, dtype=jnp.int32)) % n_z]
    numbers = block_z * PLANE + j
    angles = (numbers[:, None] * tok_dev + own_rows[None, :]).astype(F32)[:, :, None] * inverse_freq
    signed_sine = jnp.where(lane < half, -jnp.sin(angles), jnp.sin(angles))
    cosine = jnp.cos(angles)
    below = (places[jnp.maximum(block_z - 1, 0)] - mine) % n_z
    previous_at = jnp.where(j == 0, below, jnp.arange(n_z, dtype=jnp.int32))
    relative = jnp.arange(PLANE, dtype=jnp.int32) ^ j
    place = jnp.concatenate([(numbers == 0).astype(jnp.int32), previous_at, relative])
    for _ in range(n_z - 2):
        blocks.append(pass_on(blocks[-1]))
    cut = n_z // 2
    near, far = swap(out_mine, 2), swap(out_mine, 4)
    (near, far, weights, cosine, signed_sine, place, sinks, early) = lax.optimization_barrier(
        (near, far, weights, cosine, signed_sine, place, sinks, early)
    )
    corner_low, corner_high = swap(near[:cut], 4), swap(far[cut:], 2)
    early_count = n_z - 1
    query, key_value = project_blocks(0, blocks[:early_count], weights, share, cosine, signed_sine)
    halo = behind(key_value)
    (near, far, corner_low, corner_high, blocks[-1], halo) = lax.optimization_barrier(
        (near, far, corner_low, corner_high, blocks[-1], halo)
    )
    shares = []
    for r, first, piece in ((0, 0, out_mine), (2, 0, near), (4, 0, far), (6, 0, corner_low), (6, cut, corner_high)):
        shares += [(r, first, piece), (r + 1, first, swap(piece, 1))]
    last_query, last_key_value = project_blocks(
        early_count, blocks[early_count:], weights, share, cosine, signed_sine
    )
    queries, key_values = (query, last_query), (key_value, last_key_value)
    halos = (halo, behind(last_key_value))

    def parts_of(numbers):
        return attend_and_project(numbers, place, sinks, queries, key_values, halos, shares, width)

    cuts = (slice(0, width // 32 * 16), slice(width // 32 * 16, width))
    first = parts_of((1,))[0]
    others = parts_of(tuple(range(2, n_z)) + (0,))
    halves = [first[cut].astype(BF16) for cut in cuts]
    for i in range(n_z - 1):
        terms = others[i] + tokens_t.astype(F32) if i == n_z - 2 else others[i]
        sums = []
        for half, cut in zip(halves, cuts):
            arrived = pass_on(half)
            if sums:
                arrived, _ = lax.optimization_barrier((arrived, sums[-1]))
            sums.append((arrived.astype(F32) + terms[cut]).astype(BF16))
        halves = sums
    return jnp.concatenate(halves, axis=0), early


def expert_kernel(tile, hidden, rows_ref, gate_ref, upper_ref, down_ref, out_ref, total_ref, flat_ref):
    step = pl.program_id(0)
    steps = pl.num_programs(0)

    def add(count, initial):
        rows = flat_ref[...]
        gate = dot32(rows, gate_ref[0, :, :count])
        upper = dot32(rows, upper_ref[0, :, :count])
        activation = (gate * jax.nn.sigmoid(1.702 * gate) * (upper + 1.0)).astype(BF16)
        terms = dot32(activation, down_ref[:count, :])
        total_ref[...] = terms if initial else total_ref[...] + terms

    last = hidden - (-(-hidden // tile) - 1) * tile

    @pl.when(step == 0)
    def _():
        flat_ref[...] = rows_ref[...].reshape(flat_ref.shape)
        add(tile, True)

    @pl.when(jnp.logical_and(step > 0, step < steps - 1))
    def _():
        add(tile, False)

    @pl.when(step == steps - 1)
    def _():
        add(last, False)
        out_ref[...] = total_ref[...].astype(BF16).reshape(out_ref.shape)


def run_expert(rows, gate_up, down):
    width = rows.shape[-1]
    count = rows.size // width
    hidden = down.shape[0]
    tile = 512 if hidden > 1024 else 256
    whole = pl.BlockSpec(rows.shape, lambda f: (0,) * rows.ndim)
    return pl.pallas_call(
        functools.partial(expert_kernel, tile, hidden),
        grid=(-(-hidden // tile),),
        in_specs=[
            whole,
            pl.BlockSpec((1, width, tile), lambda f: (0, 0, f)),
            pl.BlockSpec((1, width, tile), lambda f: (1, 0, f)),
            pl.BlockSpec((tile, width), lambda f: (f, 0)),
        ],
        out_specs=whole,
        out_shape=jax.ShapeDtypeStruct(rows.shape, BF16),
        scratch_shapes=[pltpu.VMEM((count, width), F32), pltpu.VMEM((count, width), BF16)],
        compiler_params=pltpu.CompilerParams(vmem_limit_bytes=52 * 2**20),
        cost_estimate=pl.CostEstimate(
            flops=6 * count * width * hidden,
            bytes_accessed=6 * width * hidden + 4 * count * width,
            transcendentals=count * hidden,
        ),
    )(rows, gate_up, gate_up, down)


def slot_chunks(capacity):
    return [capacity - 8, 8] if capacity > 8 else [capacity]


def dispatch_kernel(chosen_ref, normed_ref, out_ref):
    out_ref[...] = dot_nt(chosen_ref[...], normed_ref[...]).astype(BF16).reshape(out_ref.shape)


def dispatch(chosen, normed, size):
    total, rows = chosen.shape
    width = normed.shape[0]
    shape = (total // 4, 4, width) if size % 8 and size % 4 == 0 else (total, width)
    return pl.pallas_call(
        dispatch_kernel,
        out_shape=jax.ShapeDtypeStruct(shape, BF16),
        compiler_params=pltpu.CompilerParams(vmem_limit_bytes=24 * 2**20),
        cost_estimate=pl.CostEstimate(
            flops=2 * total * rows * width, bytes_accessed=2 * width * (total + rows), transcendentals=0
        ),
    )(chosen, normed)


def routing(route_ids, combine, n_ctx, sizes):
    tok_dev = route_ids.shape[0]
    named = route_ids[:, :, None] == jnp.arange(n_ctx, dtype=jnp.int32)[None, None, :]
    member = jnp.any(named, axis=1)
    weight_of = jnp.sum(jnp.where(named, combine[:, :, None], 0.0), axis=1)
    rows = jnp.arange(tok_dev, dtype=jnp.int32)
    earlier = (rows[:, None] > rows[None, :]).astype(BF16)
    slot_of = jnp.where(member, dot32(earlier, member.astype(BF16)), -1.0).T.astype(BF16)
    weight_of = weight_of.T
    high = weight_of.astype(BF16)
    low = (weight_of - high.astype(F32)).astype(BF16)
    table = jnp.concatenate([slot_of, high, low], axis=1)
    chunks = []
    first = 0
    for size in sizes:
        number = jnp.arange(n_ctx * size, dtype=jnp.int32)[:, None]
        device = (number // size == jnp.arange(n_ctx, dtype=jnp.int32)[None, :]).astype(BF16)
        spread = dot32(device, table)
        chosen = spread[:, :tok_dev] == (first + number % size).astype(F32)
        scale = jnp.where(jnp.concatenate([chosen, chosen], axis=1), spread[:, tok_dev:], 0.0).astype(BF16)
        chunks.append((chosen.astype(BF16), scale))
        first += size
    return chunks


def mix_experts(normed, sizes, matrices, gate_up, down):
    width, tok_dev = normed.shape
    n_ctx, n_exp = lax.axis_size("ctx"), lax.axis_size("exp")
    width_local = width // n_exp

    def exchange(parts):
        by_device = parts.reshape((n_ctx, -1) + parts.shape[1:])
        return lax.all_to_all(by_device, "ctx", split_axis=0, concat_axis=0, tiled=True)

    def in_order(parts, earlier):
        return lax.optimization_barrier((parts, earlier))

    outgoing, received = [], []
    for size, (chosen, _) in zip(sizes, matrices):
        if outgoing:
            chosen, outgoing[-1] = in_order(chosen, outgoing[-1])
        outgoing.append(dispatch(chosen, normed, size))
    for parts in outgoing:
        if received:
            parts, received[-1] = in_order(parts, received[-1])
        received.append(exchange(parts))

    results = []
    for i, size in enumerate(sizes):
        if i > 1 and i == len(sizes) - 1:
            received[i], results[0] = in_order(received[i], results[0])
        if results:
            received[i], results[-1] = in_order(received[i], results[-1])
        rows_in = received[i].reshape(outgoing[i].shape)
        results.append(run_expert(rows_in, gate_up, down))

    answers = []
    for parts in results:
        if answers:
            parts, answers[-1] = in_order(parts, answers[-1])
        answers.append(exchange(parts))

    moe_out = jnp.zeros((width_local, tok_dev), F32)
    for size, (_, scale), answer in zip(sizes, matrices, answers):
        if n_exp > 1:
            answer = lax.psum_scatter(answer, "exp", scatter_dimension=answer.ndim - 1, tiled=True)
        terms = lax.dot_general(
            answer.reshape(n_ctx * size, width_local), scale, (((0,), (0,)), ((), ())),
            preferred_element_type=F32,
        )
        moe_out = moe_out + terms[:, :tok_dev] + terms[:, tok_dev:]
    return moe_out


def per_device(
    tokens,
    route_ids,
    combine,
    gain_attn,
    gain_moe,
    query_weight,
    key_weight,
    value_weight,
    attn_sinks,
    out_weight,
    gate_up_weight,
    down_weight,
):
    tok_dev, width_local = tokens.shape
    n_ctx = lax.axis_size("ctx")
    n_exp = lax.axis_size("exp")
    capacity = tok_dev * route_ids.shape[1] * 5 // (4 * n_ctx)
    sizes = slot_chunks(capacity)
    matrices = routing(route_ids, combine, n_ctx, sizes)
    by_planes = n_exp == 1 and n_ctx % PLANE == 0 and n_ctx > PLANE
    project = project_planes if by_planes else project_whole
    residual, matrices = project(
        tokens, gain_attn, query_weight, key_weight, value_weight, attn_sinks, out_weight, matrices
    )
    width = residual.shape[0]
    normed_moe = rms_norm_t(residual, gain_moe)
    exp_index = lax.axis_index("exp")
    residual_local = lax.dynamic_slice_in_dim(residual, exp_index * width_local, width_local, 0)

    moe_out = mix_experts(normed_moe, sizes, matrices, gate_up_weight[0], down_weight[0])
    return (residual_local.astype(F32) + moe_out).astype(BF16).T


def solution(mesh):
    return jax.shard_map(
        per_device,
        mesh=mesh,
        in_specs=(
            P("ctx", "exp"),
            P("ctx", None),
            P("ctx", None),
            P(),
            P(),
            P(None, ("exp", "ctx")),
            P(None, ("exp", "ctx")),
            P(None, ("exp", "ctx")),
            P("exp"),
            P("exp", "ctx"),
            P("ctx", None, None, "exp"),
            P("ctx", "exp", None),
        ),
        out_specs=P("ctx", "exp"),
        check_vma=False,
    )
```

```python
import functools
import math

import jax
import jax.numpy as jnp
from jax import lax
from jax.experimental import pallas as pl
from jax.experimental.pallas import tpu as pltpu
from jax.sharding import PartitionSpec as P

HD = 64
WINDOW = 128
EPSILON = 1e-05
ROPE_BASE = 150000.0
PLANE = 8
BF16 = jnp.bfloat16
F32 = jnp.float32


def rms_norm(values, gain):
    wide = values.astype(F32)
    meansq = jnp.mean(wide * wide, axis=-1, keepdims=True)
    return (wide * lax.rsqrt(meansq + EPSILON) * gain).astype(BF16)


def rms_norm_t(values, gain):
    wide = values.astype(F32)
    meansq = jnp.mean(wide * wide, axis=0, keepdims=True)
    return (wide * lax.rsqrt(meansq + EPSILON) * gain[:, None]).astype(BF16)


def rotary(values, angles_pos):
    half_dim = values.shape[-1] // 2
    inverse_freq = jnp.exp(
        -(2.0 * jnp.arange(half_dim, dtype=F32) / values.shape[-1]) * math.log(ROPE_BASE)
    )
    angles = angles_pos[:, None] * inverse_freq[None, :]
    cosine = jnp.cos(angles)[:, None, :]
    sine_part = jnp.sin(angles)[:, None, :]
    first_half = values[..., :half_dim]
    second_half = values[..., half_dim:]
    return jnp.concatenate(
        [
            first_half * cosine - second_half * sine_part,
            second_half * cosine + first_half * sine_part,
        ],
        axis=-1,
    )


def sink_softmax(scores, key_mask, sink_col):
    masked = jnp.where(key_mask, scores, -1e30)
    row_top = jnp.maximum(jnp.max(masked, axis=-1, keepdims=True), sink_col)
    weights = jnp.where(key_mask, jnp.exp(masked - row_top), 0.0)
    denominator = jnp.sum(weights, axis=-1, keepdims=True) + jnp.exp(sink_col - row_top)
    return (weights / denominator).astype(BF16)


def attend_block(query_rows, key_rows, value_rows, query_pos, key_pos, sink_col):
    scores = jnp.einsum(
        "qkgd,skd->kgqs", query_rows, key_rows, preferred_element_type=F32
    ) * HD ** (-0.5)
    distance = query_pos[:, None] - key_pos[None, :]
    key_mask = (distance >= 0) & (distance < WINDOW) & (key_pos >= 0)[None, :]
    weights = sink_softmax(scores, key_mask, sink_col)
    mixed_rows = jnp.einsum("kgqs,skd->qkgd", weights, value_rows, preferred_element_type=F32)
    return mixed_rows.astype(BF16).reshape(query_rows.shape[0], -1)


def dot32(a, b):
    return jnp.dot(a, b, preferred_element_type=F32)


def project_whole(
    tokens, gain_attn, query_weight, key_weight, value_weight, attn_sinks, out_weight, early
):
    tok_dev = tokens.shape[0]
    full_rows = lax.all_gather(tokens, "exp", axis=1, tiled=True)
    normed = rms_norm(full_rows, gain_attn)
    pieces = lax.all_gather((query_weight, key_weight, value_weight), "ctx", axis=1, tiled=True)
    query_lin, key_lin, value_lin = tuple(dot32(normed, piece) for piece in pieces)
    heads_local = query_lin.shape[1] // HD
    kv_local = key_lin.shape[1] // HD
    group_size = heads_local // kv_local
    position_ids = lax.axis_index("ctx") * tok_dev + jnp.arange(tok_dev, dtype=jnp.int32)
    angles_pos = position_ids.astype(F32)
    query = rotary(query_lin.reshape(tok_dev, heads_local, HD), angles_pos).astype(BF16)
    keys_own = rotary(key_lin.reshape(tok_dev, kv_local, HD), angles_pos).astype(BF16)
    key_value = jnp.stack([keys_own.reshape(tok_dev, kv_local * HD), value_lin.astype(BF16)])
    n_ctx = lax.axis_size("ctx")
    previous = lax.ppermute(key_value, "ctx", [(i, i + 1) for i in range(n_ctx - 1)])
    context = jnp.concatenate([previous, key_value], axis=1)
    key_pos = position_ids[0] - WINDOW + jnp.arange(tok_dev + WINDOW, dtype=jnp.int32)
    attended = attend_block(
        query.reshape(tok_dev, kv_local, group_size, HD),
        context[0].reshape(-1, kv_local, HD),
        context[1].reshape(-1, kv_local, HD),
        position_ids,
        key_pos,
        attn_sinks.reshape(kv_local, group_size, 1, 1),
    )
    head_terms = dot32(attended, lax.all_gather(out_weight, "ctx", axis=1, tiled=True))
    attn_proj = lax.psum(head_terms.astype(BF16), "exp").astype(F32)
    return (full_rows.astype(F32) + attn_proj).astype(BF16).T, early


def dot_nt(a, b):
    return lax.dot_general(a, b, (((1,), (1,)), ((), ())), preferred_element_type=F32)


def turn(values, cosine, signed_sine):
    width = values.shape[1]
    half = HD // 2
    lane = lax.broadcasted_iota(jnp.int32, values.shape, 1) % HD
    partner = jnp.where(
        lane < half,
        pltpu.roll(values, width - half, 1),
        pltpu.roll(values, half, 1),
    )
    return values * cosine + partner * signed_sine


def qkv_kernel(count, start, *refs):
    blocks, (weight_ref, cos_ref, sin_ref, q_ref, key_value_ref, rows_ref, kv_ref) = refs[:count], refs[count:]
    width, rows = blocks[0].shape
    planes, packed, cols = weight_ref.shape
    share = kv_ref.shape[2]
    for r in range(count):
        rows_ref[r * rows : (r + 1) * rows, :] = blocks[r][...].T

    for p in range(planes):
        for tile in range((packed - width) // (2 * share)):
            at, lanes = width + 2 * share * tile, slice(tile * cols, (tile + 1) * cols)
            for part in range(2):
                kv_ref[part, p, :, lanes] = weight_ref[p, at + part * share : at + (part + 1) * share]
    both = kv_ref[...].reshape(2 * planes * share, kv_ref.shape[3])[:, :width]
    lines = dot_nt(rows_ref[...], both)
    half = planes * share
    for r in range(count):
        piece = lines[r * rows : (r + 1) * rows]
        key_value_ref[r, :, :half] = turn(piece[:, :half], cos_ref[start + r], sin_ref[start + r]).astype(BF16)
        key_value_ref[r, :, half:] = piece[:, half:].astype(BF16)

    for p in range(0, planes, 2):
        weight = jnp.concatenate([weight_ref[p, :width], weight_ref[p + 1, :width]], axis=1)
        query = dot32(rows_ref[...], weight)
        for k in range(2):
            lanes = slice((p + k) * cols, (p + k + 1) * cols)
            for r in range(count):
                piece = query[r * rows : (r + 1) * rows, k * cols : (k + 1) * cols]
                q_ref[r, :, lanes] = turn(piece, cos_ref[start + r], sin_ref[start + r]).astype(BF16)


def project_blocks(start, blocks, weights, share, cosine, signed_sine):
    count = len(blocks)
    width, rows = blocks[0].shape
    planes, packed, cols = weights.shape
    kv_cols = 2 * planes * share
    vmem = pl.BlockSpec(memory_space=pltpu.VMEM)
    return pl.pallas_call(
        functools.partial(qkv_kernel, count, start),
        in_specs=[vmem] * (count + 3),
        out_specs=[vmem, vmem],
        out_shape=[
            jax.ShapeDtypeStruct((count, rows, planes * cols), BF16),
            jax.ShapeDtypeStruct((count, rows, kv_cols), BF16),
        ],
        scratch_shapes=[
            pltpu.VMEM((count * rows, width), BF16),
            pltpu.VMEM((2, planes, share, (packed - width) // (2 * share) * cols), BF16),
        ],
        compiler_params=pltpu.CompilerParams(vmem_limit_bytes=36 * 2**20),
        cost_estimate=pl.CostEstimate(
            flops=2 * count * rows * width * (planes * cols + kv_cols),
            bytes_accessed=2 * width * (planes * cols + kv_cols + count * rows),
            transcendentals=0,
        ),
    )(*blocks, weights, cosine, signed_sine)


def attend_kernel(
    numbers, pieces, place_ref, sinks_ref, *refs
):
    queries, key_values, halos, refs = refs[:2], refs[2:4], refs[4:6], refs[6:]
    share_refs, (out_ref, att_ref, total_ref) = refs[: len(pieces)], refs[len(pieces) :]
    early, rows = key_values[0].shape[:2]
    count = early + 1
    pair = 2 * HD
    kv_heads = key_values[0].shape[2] // pair
    kv_cols = kv_heads * HD
    pairs = queries[0].shape[2] // pair
    lane = lax.broadcasted_iota(jnp.int32, (rows, pair), 1)
    low = lane < HD

    def spread(values, head):
        moved = pltpu.roll(values.astype(F32), HD, 1)
        chunk = values.astype(F32)
        lower, upper = (chunk, moved) if head % 2 == 0 else (moved, chunk)
        zero = jnp.zeros_like(chunk)
        return jnp.concatenate(
            [jnp.where(low, lower, zero), jnp.where(low, zero, upper)], axis=0
        ).astype(BF16)

    def block(refs, r):
        return (refs[0], r) if r < early else (refs[1], 0)

    def own_columns(r, lanes):
        ref, at = block(key_values, r)
        return ref[at, :, lanes]

    def previous_columns(r, lanes):
        at = place_ref[count + r]
        return jnp.where(at < early, halos[0][jnp.minimum(at, early - 1), :, lanes], halos[1][0, :, lanes])

    def side(columns, r):
        tables = []
        for head in range(kv_heads):
            at = head // 2 * pair
            keys = spread(columns(r, slice(at, at + pair)), head)
            values = spread(columns(r, slice(kv_cols + at, kv_cols + at + pair)), head)
            tables.append((keys, values))
        return tables

    row = lax.broadcasted_iota(jnp.int32, (rows, rows), 0)
    col = lax.broadcasted_iota(jnp.int32, (rows, rows), 1)
    inside = col <= row
    scale = HD**-0.5
    for i, r in enumerate(numbers):
        own, previous = side(own_columns, r), side(previous_columns, r)
        queries_ref, query_at = block(queries, r)
        shown = jnp.logical_or(inside, place_ref[r] == 0)
        for p in range(pairs):
            head = p * kv_heads // pairs
            chunk = queries_ref[query_at, :, p * pair : (p + 1) * pair]
            scores_own = dot_nt(chunk, own[head][0])
            scores_previous = dot_nt(chunk, previous[head][0])
            probs_own, probs_previous = [], []
            for h in range(2):
                half = slice(h * rows, (h + 1) * rows)
                scores = jnp.where(inside, scores_own[:, half], scores_previous[:, half]) * scale
                scores = jnp.where(shown, scores, -1e30)
                sink = sinks_ref[2 * p + h]
                top = jnp.maximum(jnp.max(scores, axis=1, keepdims=True), sink)
                weights = jnp.exp(scores - top)
                total = jnp.sum(weights, axis=1, keepdims=True) + jnp.exp(sink - top)
                probs = weights / total
                probs_own.append(jnp.where(inside, probs, 0.0).astype(BF16))
                probs_previous.append(jnp.where(inside, 0.0, probs).astype(BF16))
            mixed = dot32(jnp.concatenate(probs_own, axis=1), own[head][1])
            mixed = mixed + dot32(jnp.concatenate(probs_previous, axis=1), previous[head][1])
            att_ref[i * rows : (i + 1) * rows, p * pair : (p + 1) * pair] = mixed.astype(BF16)

    groups, shares, padded, _ = total_ref.shape
    cols = out_ref.shape[1] // (shares * groups)
    attended = att_ref[...]
    for (relative, first), weight_ref in zip(pieces, share_refs):
        size, _, depth = weight_ref.shape
        terms = dot_nt(weight_ref[...].reshape(size * padded, depth), attended)
        for g in range(size):
            total_ref[first + g, place_ref[2 * count + relative]] = terms[g * padded : (g + 1) * padded]
    for g in range(groups):
        for p in range(shares):
            at = (g * shares + p) * cols
            for i in range(len(numbers)):
                out_ref[i, at : at + cols, :] = total_ref[g, p, :cols, i * rows : (i + 1) * rows]


def attend_and_project(numbers, place, sinks, queries, key_values, halos, shares, width):
    rows = queries[0].shape[1]
    count = len(numbers)
    groups, padded, depth = shares[0][2].shape
    pieces = tuple((relative, first) for relative, first, _ in shares)
    vmem = pl.BlockSpec(memory_space=pltpu.VMEM)
    smem = pl.BlockSpec(memory_space=pltpu.SMEM)
    return pl.pallas_call(
        functools.partial(attend_kernel, numbers, pieces),
        in_specs=[smem, smem] + [vmem] * (6 + len(shares)),
        out_specs=vmem,
        out_shape=jax.ShapeDtypeStruct((count, width, rows), F32),
        scratch_shapes=[
            pltpu.VMEM((count * rows, depth), BF16),
            pltpu.VMEM((groups, PLANE, padded, count * rows), F32),
        ],
        compiler_params=pltpu.CompilerParams(vmem_limit_bytes=40 * 2**20),
        cost_estimate=pl.CostEstimate(
            flops=2 * count * rows * depth * (width + 8 * rows),
            bytes_accessed=2 * width * (depth + 2 * count * rows),
            transcendentals=count * rows * rows * depth // HD,
        ),
    )(place, sinks, *queries, *key_values, *halos, *[weight for _, _, weight in shares])


def project_planes(
    tokens, gain_attn, query_weight, key_weight, value_weight, attn_sinks, out_weight, early
):
    tok_dev, width = tokens.shape
    n_ctx = lax.axis_size("ctx")
    n_z = n_ctx // PLANE
    index = lax.axis_index("ctx")
    z, j = index // PLANE, index % PLANE
    planes = [[PLANE * a + b for b in range(PLANE)] for a in range(n_z)]
    order = list(range(0, n_z, 2)) + list(range(1, n_z, 2))[::-1]
    place_of = [order.index(a) for a in range(n_z)]
    ring, places = jnp.array(order, jnp.int32), jnp.array(place_of, jnp.int32)

    def shift(block, steps):
        return lax.ppermute(block, "ctx", [(i, (i + steps * PLANE) % n_ctx) for i in range(n_ctx)])

    def pass_on(block):
        route = [
            (a * PLANE + b, order[place_of[a] - 1] * PLANE + b) for a in range(n_z) for b in range(PLANE)
        ]
        return lax.ppermute(block, "ctx", route)

    def behind(block):
        route = [(a * PLANE + b, a * PLANE + (b + 1) % PLANE) for a in range(n_z) for b in range(PLANE)]
        return lax.ppermute(block, "ctx", route)

    def swap(block, bits):
        return lax.ppermute(block, "ctx", [(i, i ^ bits) for i in range(n_ctx)])

    tokens_t = tokens.T
    blocks = [rms_norm_t(tokens_t, gain_attn)]

    lanes = query_weight.shape[1]
    share = key_weight.shape[1]
    tiles = -(-width // lanes)
    kv_rows = jnp.concatenate([key_weight.T, value_weight.T], axis=0)
    kv_rows = jnp.pad(kv_rows, ((0, 0), (0, tiles * lanes - width))).reshape(2 * share, tiles, lanes)
    packed = jnp.concatenate(
        [query_weight, kv_rows.transpose(1, 0, 2).reshape(tiles * 2 * share, lanes)], axis=0
    )
    weights = lax.all_gather(packed, "ctx", axis_index_groups=planes)

    cols = out_weight.shape[1]
    padded = -(-cols // 16) * 16
    group_rows = out_weight.shape[0] // n_z
    out_rows = jnp.pad(out_weight.T, ((0, padded - cols), (0, 0)))
    out_rows, blocks[0] = lax.optimization_barrier((out_rows, blocks[0]))
    blocks.append(pass_on(blocks[0]))
    out_groups = jnp.stack(jnp.split(out_rows, n_z, axis=1))
    pieces = [
        shift(lax.dynamic_index_in_dim(out_groups, (z + s) % n_z, 0, keepdims=False), s) if s
        else lax.dynamic_index_in_dim(out_groups, z, 0, keepdims=False)
        for s in range(n_z)
    ]
    ordered = jnp.stack(pieces[::-1] + pieces[:0:-1])
    out_mine = lax.dynamic_slice_in_dim(ordered, n_z - 1 - z, n_z, 0)
    heads = PLANE * query_weight.shape[1] // HD
    sinks = lax.dynamic_slice_in_dim(attn_sinks, z * heads, heads)
    own_rows = jnp.arange(tok_dev, dtype=jnp.int32)
    lane = jnp.arange(2 * HD, dtype=jnp.int32) % HD
    half = HD // 2
    inverse_freq = jnp.exp(-(2.0 * (lane % half).astype(F32) / HD) * math.log(ROPE_BASE))
    mine = places[z]
    block_z = ring[(mine + jnp.arange(n_z, dtype=jnp.int32)) % n_z]
    numbers = block_z * PLANE + j
    angles = (numbers[:, None] * tok_dev + own_rows[None, :]).astype(F32)[:, :, None] * inverse_freq
    signed_sine = jnp.where(lane < half, -jnp.sin(angles), jnp.sin(angles))
    cosine = jnp.cos(angles)
    below = (places[jnp.maximum(block_z - 1, 0)] - mine) % n_z
    previous_at = jnp.where(j == 0, below, jnp.arange(n_z, dtype=jnp.int32))
    relative = jnp.arange(PLANE, dtype=jnp.int32) ^ j
    place = jnp.concatenate([(numbers == 0).astype(jnp.int32), previous_at, relative])
    for _ in range(n_z - 2):
        blocks.append(pass_on(blocks[-1]))
    cut = n_z // 2
    near, far = swap(out_mine, 2), swap(out_mine, 4)
    early_count = n_z - 1
    query, key_value = project_blocks(0, blocks[:early_count], weights, share, cosine, signed_sine)
    halo = behind(key_value)
    (near, far, key_value, place, sinks, early) = lax.optimization_barrier(
        (near, far, key_value, place, sinks, early)
    )
    corner_low, corner_high = swap(near[:cut], 4), swap(far[cut:], 2)
    (near, far, corner_low, corner_high, blocks[-1], halo) = lax.optimization_barrier(
        (near, far, corner_low, corner_high, blocks[-1], halo)
    )
    shares = []
    for r, first, piece in ((0, 0, out_mine), (2, 0, near), (4, 0, far), (6, 0, corner_low), (6, cut, corner_high)):
        shares += [(r, first, piece), (r + 1, first, swap(piece, 1))]
    last_query, last_key_value = project_blocks(
        early_count, blocks[early_count:], weights, share, cosine, signed_sine
    )
    queries, key_values = (query, last_query), (key_value, last_key_value)
    halos = (halo, behind(last_key_value))

    def parts_of(numbers):
        return attend_and_project(numbers, place, sinks, queries, key_values, halos, shares, width)

    cuts = (slice(0, width // 32 * 16), slice(width // 32 * 16, width))
    first = parts_of((1,))[0]
    others = parts_of(tuple(range(2, n_z)) + (0,))
    halves = [first[cut].astype(BF16) for cut in cuts]
    for i in range(n_z - 1):
        terms = others[i] + tokens_t.astype(F32) if i == n_z - 2 else others[i]
        sums = []
        for half, cut in zip(halves, cuts):
            arrived = pass_on(half)
            if sums:
                arrived, _ = lax.optimization_barrier((arrived, sums[-1]))
            sums.append((arrived.astype(F32) + terms[cut]).astype(BF16))
        halves = sums
    return jnp.concatenate(halves, axis=0), early


def expert_kernel(tile, hidden, rows_ref, gate_ref, upper_ref, down_ref, out_ref, total_ref, flat_ref):
    step = pl.program_id(0)
    steps = pl.num_programs(0)

    def add(count, initial):
        rows = flat_ref[...]
        gate = dot32(rows, gate_ref[0, :, :count])
        upper = dot32(rows, upper_ref[0, :, :count])
        activation = (gate * jax.nn.sigmoid(1.702 * gate) * (upper + 1.0)).astype(BF16)
        terms = dot32(activation, down_ref[:count, :])
        total_ref[...] = terms if initial else total_ref[...] + terms

    last = hidden - (-(-hidden // tile) - 1) * tile

    @pl.when(step == 0)
    def _():
        flat_ref[...] = rows_ref[...].reshape(flat_ref.shape)
        add(tile, True)

    @pl.when(jnp.logical_and(step > 0, step < steps - 1))
    def _():
        add(tile, False)

    @pl.when(step == steps - 1)
    def _():
        add(last, False)
        out_ref[...] = total_ref[...].astype(BF16).reshape(out_ref.shape)


def run_expert(rows, gate_up, down):
    width = rows.shape[-1]
    count = rows.size // width
    hidden = down.shape[0]
    tile = 512 if hidden > 1024 else 256
    whole = pl.BlockSpec(rows.shape, lambda f: (0,) * rows.ndim)
    return pl.pallas_call(
        functools.partial(expert_kernel, tile, hidden),
        grid=(-(-hidden // tile),),
        in_specs=[
            whole,
            pl.BlockSpec((1, width, tile), lambda f: (0, 0, f)),
            pl.BlockSpec((1, width, tile), lambda f: (1, 0, f)),
            pl.BlockSpec((tile, width), lambda f: (f, 0)),
        ],
        out_specs=whole,
        out_shape=jax.ShapeDtypeStruct(rows.shape, BF16),
        scratch_shapes=[pltpu.VMEM((count, width), F32), pltpu.VMEM((count, width), BF16)],
        compiler_params=pltpu.CompilerParams(vmem_limit_bytes=52 * 2**20),
        cost_estimate=pl.CostEstimate(
            flops=6 * count * width * hidden,
            bytes_accessed=6 * width * hidden + 4 * count * width,
            transcendentals=count * hidden,
        ),
    )(rows, gate_up, gate_up, down)


def slot_chunks(capacity):
    return [capacity - 8, 8] if capacity > 8 else [capacity]


def dispatch_kernel(chosen_ref, normed_ref, out_ref):
    out_ref[...] = dot_nt(chosen_ref[...], normed_ref[...]).astype(BF16).reshape(out_ref.shape)


def dispatch(chosen, normed, size):
    total, rows = chosen.shape
    width = normed.shape[0]
    shape = (total // 4, 4, width) if size % 8 and size % 4 == 0 else (total, width)
    return pl.pallas_call(
        dispatch_kernel,
        out_shape=jax.ShapeDtypeStruct(shape, BF16),
        compiler_params=pltpu.CompilerParams(vmem_limit_bytes=24 * 2**20),
        cost_estimate=pl.CostEstimate(
            flops=2 * total * rows * width, bytes_accessed=2 * width * (total + rows), transcendentals=0
        ),
    )(chosen, normed)


def routing(route_ids, combine, n_ctx, sizes):
    tok_dev = route_ids.shape[0]
    named = route_ids[:, :, None] == jnp.arange(n_ctx, dtype=jnp.int32)[None, None, :]
    member = jnp.any(named, axis=1)
    weight_of = jnp.sum(jnp.where(named, combine[:, :, None], 0.0), axis=1)
    rows = jnp.arange(tok_dev, dtype=jnp.int32)
    earlier = (rows[:, None] > rows[None, :]).astype(BF16)
    slot_of = jnp.where(member, dot32(earlier, member.astype(BF16)), -1.0).T.astype(BF16)
    weight_of = weight_of.T
    high = weight_of.astype(BF16)
    low = (weight_of - high.astype(F32)).astype(BF16)
    table = jnp.concatenate([slot_of, high, low], axis=1)
    chunks = []
    first = 0
    for size in sizes:
        number = jnp.arange(n_ctx * size, dtype=jnp.int32)[:, None]
        device = (number // size == jnp.arange(n_ctx, dtype=jnp.int32)[None, :]).astype(BF16)
        spread = dot32(device, table)
        chosen = spread[:, :tok_dev] == (first + number % size).astype(F32)
        scale = jnp.where(jnp.concatenate([chosen, chosen], axis=1), spread[:, tok_dev:], 0.0).astype(BF16)
        chunks.append((chosen.astype(BF16), scale))
        first += size
    return chunks


def mix_experts(normed, sizes, matrices, gate_up, down):
    width, tok_dev = normed.shape
    n_ctx, n_exp = lax.axis_size("ctx"), lax.axis_size("exp")
    width_local = width // n_exp

    def exchange(parts):
        by_device = parts.reshape((n_ctx, -1) + parts.shape[1:])
        return lax.all_to_all(by_device, "ctx", split_axis=0, concat_axis=0, tiled=True)

    def in_order(parts, earlier):
        return lax.optimization_barrier((parts, earlier))

    outgoing, received = [], []
    for size, (chosen, _) in zip(sizes, matrices):
        if outgoing:
            chosen, outgoing[-1] = in_order(chosen, outgoing[-1])
        outgoing.append(dispatch(chosen, normed, size))
    for parts in outgoing:
        if received:
            parts, received[-1] = in_order(parts, received[-1])
        received.append(exchange(parts))

    results = []
    for i, size in enumerate(sizes):
        if i > 1 and i == len(sizes) - 1:
            received[i], results[0] = in_order(received[i], results[0])
        if results:
            received[i], results[-1] = in_order(received[i], results[-1])
        rows_in = received[i].reshape(outgoing[i].shape)
        results.append(run_expert(rows_in, gate_up, down))

    answers = []
    for parts in results:
        if answers:
            parts, answers[-1] = in_order(parts, answers[-1])
        answers.append(exchange(parts))

    moe_out = jnp.zeros((width_local, tok_dev), F32)
    for size, (_, scale), answer in zip(sizes, matrices, answers):
        if n_exp > 1:
            answer = lax.psum_scatter(answer, "exp", scatter_dimension=answer.ndim - 1, tiled=True)
        terms = lax.dot_general(
            answer.reshape(n_ctx * size, width_local), scale, (((0,), (0,)), ((), ())),
            preferred_element_type=F32,
        )
        moe_out = moe_out + terms[:, :tok_dev] + terms[:, tok_dev:]
    return moe_out


def per_device(
    tokens,
    route_ids,
    combine,
    gain_attn,
    gain_moe,
    query_weight,
    key_weight,
    value_weight,
    attn_sinks,
    out_weight,
    gate_up_weight,
    down_weight,
):
    tok_dev, width_local = tokens.shape
    n_ctx = lax.axis_size("ctx")
    n_exp = lax.axis_size("exp")
    capacity = tok_dev * route_ids.shape[1] * 5 // (4 * n_ctx)
    sizes = slot_chunks(capacity)
    matrices = routing(route_ids, combine, n_ctx, sizes)
    by_planes = n_exp == 1 and n_ctx % PLANE == 0 and n_ctx > PLANE
    project = project_planes if by_planes else project_whole
    residual, matrices = project(
        tokens, gain_attn, query_weight, key_weight, value_weight, attn_sinks, out_weight, matrices
    )
    width = residual.shape[0]
    normed_moe = rms_norm_t(residual, gain_moe)
    exp_index = lax.axis_index("exp")
    residual_local = lax.dynamic_slice_in_dim(residual, exp_index * width_local, width_local, 0)

    moe_out = mix_experts(normed_moe, sizes, matrices, gate_up_weight[0], down_weight[0])
    return (residual_local.astype(F32) + moe_out).astype(BF16).T


def solution(mesh):
    return jax.shard_map(
        per_device,
        mesh=mesh,
        in_specs=(
            P("ctx", "exp"),
            P("ctx", None),
            P("ctx", None),
            P(),
            P(),
            P(None, ("exp", "ctx")),
            P(None, ("exp", "ctx")),
            P(None, ("exp", "ctx")),
            P("exp"),
            P("exp", "ctx"),
            P("ctx", None, None, "exp"),
            P("ctx", "exp", None),
        ),
        out_specs=P("ctx", "exp"),
        check_vma=False,
    )
```
